32 devices in a mesh: section: 2 (over core), dp: 16 (over z, y, x).
Axes of the slice: x: 2, y: 2, z: 4, core: 2. Of those that a mesh axis runs over, the one named last changes fastest.
Arguments:
- tokens: bfloat16 [4, 8192, 768], P(None, 'dp'), may hold values from -9 to 9
- valid: int32 [4, 8192], P(None, 'dp'), may hold values from 0 to 1, as said below
- cotangent: bfloat16 [4, 8192, 768], P(None, 'dp'), may hold values from -11 to 11
- qkv_weight: bfloat16 [2, 768, 2304], P('section'), may hold values from -0.21875 to 0.21875
- out_weight: bfloat16 [2, 768, 768], P('section'), may hold values from -0.875 to 0.875
- ffn_in: bfloat16 [2, 768, 3072], P('section'), may hold values from -0.21875 to 0.21875
- ffn_out: bfloat16 [2, 3072, 768], P('section'), may hold values from -0.15625 to 0.15625
- attn_down: bfloat16 [2, 768, 64], P('section'), may hold values from -0.21875 to 0.21875
- attn_down_bias: float32 [2, 64], P('section'), may hold values from -3 to 3
- attn_up: bfloat16 [2, 64, 768], P('section'), may hold values from -0.75 to 0.75
- attn_up_bias: float32 [2, 768], P('section'), may hold values from -2 to 2
- norm1_gain: float32 [2, 768], P('section'), may hold values from 0.5 to 1.5
- norm1_bias: float32 [2, 768], P('section'), may hold values from -1 to 1
- ffn_down: bfloat16 [2, 768, 64], P('section'), may hold values from -0.21875 to 0.21875
- ffn_down_bias: float32 [2, 64], P('section'), may hold values from -3 to 3
- ffn_up: bfloat16 [2, 64, 768], P('section'), may hold values from -0.75 to 0.75
- ffn_up_bias: float32 [2, 768], P('section'), may hold values from -2 to 2
- norm2_gain: float32 [2, 768], P('section'), may hold values from 0.5 to 1.5
- norm2_bias: float32 [2, 768], P('section'), may hold values from -1 to 1
Outputs:
- result: bfloat16 [4, 8192, 768], P(None, 'dp')
- input_grad: bfloat16 [4, 8192, 768], P('section', 'dp')
- grad_attn_down: float32 [2, 768, 64], P('section')
- grad_attn_down_bias: float32 [2, 64], P('section')
- grad_attn_up: float32 [2, 64, 768], P('section')
- grad_attn_up_bias: float32 [2, 768], P('section')
- grad_norm1_gain: float32 [2, 768], P('section')
- grad_norm1_bias: float32 [2, 768], P('section')
- grad_ffn_down: float32 [2, 768, 64], P('section')
- grad_ffn_down_bias: float32 [2, 64], P('section')
- grad_ffn_up: float32 [2, 64, 768], P('section')
- grad_ffn_up_bias: float32 [2, 768], P('section')
- grad_norm2_gain: float32 [2, 768], P('section')
- grad_norm2_bias: float32 [2, 768], P('section')
- rms_values: float32 [2, 3], P('section')
The draws below stay inside these ranges and needn't reach their ends.
Inputs may be any that keep to these rules, and one draw needn't show every extreme that they name: `valid`: in micro-batch m the slots form sequences of 64 * 2**m consecutive slots; in each sequence the ones are a leading run of at least one slot.
All inputs are finite; a program needn't handle non-finite values.
Results may differ from the reference program's by a relative error of at most 0.034.
Values may be sent and summed in bfloat16 or wider, within the bound.
No kernel may reach another device: no remote copies, remote signals or barrier semaphores. Data moves between devices by JAX's collectives and lax.ppermute only.
A program may use at most 320 MiB of HBM per device.

```python
from functools import partial
import jax
import jax.numpy as jnp
from jax import lax

D = 768
HEADS = 12
HDIM = 64
FF = 3072
ADP = 64
BUCKET = 64
NMB = 4
TOKENS = 8192


def rising_field(key, low_scale):
    shape = (NMB, TOKENS, D)
    places = jnp.arange(TOKENS, dtype=jnp.float32) / max(TOKENS - 1, 1)
    scales = low_scale * 3.0 ** places
    base_values = jnp.clip(jax.random.normal(key, shape, jnp.float32), -6.0, 6.0)
    return base_values * scales[None, :, None]


def draw_tokens(key, part):
    return rising_field(jax.random.fold_in(key, 11), 0.5).astype(jnp.bfloat16)


def draw_cotangent(key, part):
    return rising_field(jax.random.fold_in(key, 23), 0.6).astype(jnp.bfloat16)


def draw_valid(key, part):
    collected = []
    places = jnp.arange(TOKENS, dtype=jnp.int32)
    for level in range(NMB):
        span = BUCKET * 2 ** level
        count = TOKENS // span
        lengths = jax.random.randint(jax.random.fold_in(key, 37 + level), (count,), max(span // 4, 1), span + 1)
        collected.append((places % span < jnp.repeat(lengths, span)).astype(jnp.int32))
    return jnp.stack(collected)


def block_scale(stream_key, dims, pieces, smallest, high):
    factor_of, own = 1.0, jax.random.fold_in(stream_key, 6)
    for axis_at, shards_of in pieces:
        draws = jnp.exp(jax.random.uniform(jax.random.fold_in(own, axis_at), (shards_of,), jnp.float32, smallest / len(pieces), high / len(pieces)))
        factor_of = factor_of * jnp.repeat(draws, dims[axis_at] // shards_of).reshape([-1 if axis == axis_at else 1 for axis in range(len(dims))])
    return factor_of


def scatter_about(key, shape, scale, bound, split=(), kind=jnp.bfloat16):
    drawn = jax.random.normal(key, shape, jnp.float32) * scale
    if len(split) > 0:
        drawn = block_scale(key, shape, split, -0.22, 0.18) * drawn
    return jnp.clip(drawn, min=-bound, max=bound).astype(kind)


def setup_inputs(seed: int = 0) -> dict:
    key_of = jax.random.split(jax.random.key(seed), 20)
    return {
        "tokens": draw_tokens(jax.random.fold_in(key_of[19], 71), 0),
        "valid": draw_valid(jax.random.fold_in(key_of[19], 71), 0),
        "cotangent": draw_cotangent(jax.random.fold_in(key_of[19], 71), 0),
        "qkv_weight": scatter_about(key_of[3], (2, D, 3 * D), D ** -0.5, 0.21875, ((0, 2),)),
        "out_weight": scatter_about(key_of[4], (2, D, D), (D // 16) ** -0.5, 0.875, ((0, 2),)),
        "ffn_in": scatter_about(key_of[5], (2, D, FF), D ** -0.5, 0.21875, ((0, 2),)),
        "ffn_out": scatter_about(key_of[6], (2, FF, D), (FF // 2) ** -0.5, 0.15625, ((0, 2),)),
        "attn_down": scatter_about(key_of[7], (2, D, ADP), D ** -0.5, 0.21875, ((0, 2),)),
        "attn_down_bias": scatter_about(key_of[8], (2, ADP), 0.5, 3.0, ((0, 2),), jnp.float32),
        "attn_up": scatter_about(key_of[9], (2, ADP, D), ADP ** -0.5, 0.75, ((0, 2),)),
        "attn_up_bias": scatter_about(key_of[10], (2, D), 0.3, 2.0, ((0, 2),), jnp.float32),
        "norm1_gain": jnp.clip(1.0 + 0.1 * jax.random.normal(key_of[11], (2, D), jnp.float32), 0.5, 1.5),
        "norm1_bias": scatter_about(key_of[12], (2, D), 0.2, 1.0, ((0, 2),), jnp.float32),
        "ffn_down": scatter_about(key_of[13], (2, D, ADP), D ** -0.5, 0.21875, ((0, 2),)),
        "ffn_down_bias": scatter_about(key_of[14], (2, ADP), 0.5, 3.0, ((0, 2),), jnp.float32),
        "ffn_up": scatter_about(key_of[15], (2, ADP, D), ADP ** -0.5, 0.75, ((0, 2),)),
        "ffn_up_bias": scatter_about(key_of[16], (2, D), 0.3, 2.0, ((0, 2),), jnp.float32),
        "norm2_gain": jnp.clip(1.0 + 0.1 * jax.random.normal(key_of[17], (2, D), jnp.float32), 0.5, 1.5),
        "norm2_bias": scatter_about(key_of[18], (2, D), 0.2, 1.0, ((0, 2),), jnp.float32),
    }


@jax.custom_vjp
def low(v):
    return lax.optimization_barrier(v.astype(jnp.bfloat16)).astype(jnp.float32)

@jax.custom_vjp
def low_back(v):
    return v

def low_keep(v):
    return (low(v), None)

def low_pass(kept, grad):
    return (grad,)

def back_keep(v):
    return (v, None)

def back_low(kept, grad):
    return (low(grad),)
low.defvjp(low_keep, low_pass)
low_back.defvjp(back_keep, back_low)
HIGHEST_MODE = lax.Precision.HIGHEST
NEGATIVE = -1e+30
EPSILON = 1e-12
ROOT_HALF = 0.7071067811865476

def gelu_value(values):
    return 0.5 * values * (1.0 + lax.erf(values * ROOT_HALF))

def matmul(left_side, right_side):
    return jnp.dot(left_side, right_side, precision=HIGHEST_MODE)

def normalize(totals, gains, offsets):
    centered = totals - lax.optimization_barrier(jnp.mean(totals, axis=-1, keepdims=True))
    scaler = lax.rsqrt(lax.optimization_barrier(jnp.mean(centered * centered, axis=-1, keepdims=True)) + EPSILON)
    return centered * scaler * gains + offsets

def one_layer(hidden, kept_mask, length, params):
    qkv_weight, out_weight, ffn_in, ffn_out, attn_down, attn_down_bias, attn_up, attn_up_bias, norm1_gain, norm1_bias, ffn_down, ffn_down_bias, ffn_up, ffn_up_bias, norm2_gain, norm2_bias = params
    row_count = hidden.shape[0]
    sequences = row_count // length
    packed = low(low_back(matmul(hidden, qkv_weight)))
    queries = packed[:, :D].reshape(sequences, length, HEADS, HDIM)
    keys_part = packed[:, D:2 * D].reshape(sequences, length, HEADS, HDIM)
    values_part = packed[:, 2 * D:].reshape(sequences, length, HEADS, HDIM)
    scores = low_back(0.125 * jnp.einsum('bqhd,bkhd->bhqk', queries, keys_part, precision=HIGHEST_MODE))
    allowed = kept_mask.reshape(sequences, 1, 1, length) > 0
    scores = jnp.where(allowed, scores, NEGATIVE)
    highest = lax.optimization_barrier(jnp.max(scores, axis=-1, keepdims=True))
    exponent = jnp.exp(scores - highest)
    portions = low(exponent / lax.optimization_barrier(jnp.sum(exponent, axis=-1, keepdims=True)))
    context = jnp.einsum('bhqk,bkhd->bqhd', portions, values_part, precision=HIGHEST_MODE)
    context = low(low_back(context.reshape(row_count, D)))
    attended = low(low_back(matmul(context, out_weight)))
    first_pre = low_back(matmul(attended, attn_down) + attn_down_bias)
    first_branch = attended + matmul(low(gelu_value(first_pre)), attn_up) + attn_up_bias
    first_total = hidden + low_back(first_branch)
    middle = low(normalize(first_total, norm1_gain, norm1_bias))
    expanded = low_back(matmul(middle, ffn_in))
    returned = low(low_back(matmul(low(gelu_value(expanded)), ffn_out)))
    second_pre = low_back(matmul(returned, ffn_down) + ffn_down_bias)
    second_branch = returned + matmul(low(gelu_value(second_pre)), ffn_up) + ffn_up_bias
    second_total = middle + low_back(second_branch)
    live_rows = (kept_mask > 0).astype(jnp.float32)[:, None]
    partial_sums = jnp.stack([jnp.sum(first_branch * first_branch * live_rows), jnp.sum(second_branch * second_branch * live_rows), jnp.sum(second_total * second_total * live_rows), jnp.sum(live_rows)])
    return (normalize(second_total, norm2_gain, norm2_bias), partial_sums)

def two_layers(trained, frozen, hidden, kept_mask, length):
    collected = []
    for section_number in range(2):
        params = tuple((member[section_number] for member in frozen)) + tuple((member[section_number] for member in trained))
        normed, partial_sums = one_layer(hidden, kept_mask, length, params)
        collected.append(partial_sums)
        if section_number == 0:
            hidden = low_back(low(normed))
        else:
            hidden = low(normed)
    return (hidden, jnp.stack(collected))

def reference(tokens, valid, cotangent, qkv_weight, out_weight, ffn_in, ffn_out, attn_down, attn_down_bias, attn_up, attn_up_bias, norm1_gain, norm1_bias, ffn_down, ffn_down_bias, ffn_up, ffn_up_bias, norm2_gain, norm2_bias):
    frozen = tuple((member.astype(jnp.float32) for member in (qkv_weight, out_weight, ffn_in, ffn_out)))
    trained = tuple((member.astype(jnp.float32) for member in (attn_down, attn_down_bias, attn_up, attn_up_bias, norm1_gain, norm1_bias, ffn_down, ffn_down_bias, ffn_up, ffn_up_bias, norm2_gain, norm2_bias)))
    block_rows = min(4096, TOKENS)

    def advance(carry, item, trained_now, length):
        produced, partial_sums = two_layers(trained_now, frozen, item[0], item[1], length)
        return (carry + partial_sums, produced)

    def forward(trained_now, inputs):
        outputs = []
        statistics = jnp.zeros((2, 4), jnp.float32)
        for level in range(NMB):
            length = BUCKET * 2 ** level
            stepper = jax.checkpoint(partial(advance, trained_now=trained_now, length=length))
            statistics, produced = lax.scan(stepper, statistics, (inputs[level].reshape(-1, block_rows, D), valid[level].reshape(-1, block_rows)))
            outputs.append(produced.reshape(TOKENS, D))
        return (jnp.stack(outputs), statistics)
    result, pullback, statistics = jax.vjp(forward, trained, tokens.astype(jnp.float32), has_aux=True)
    trained_grads, input_grad = pullback(cotangent.astype(jnp.float32))
    rms_values = jnp.sqrt(statistics[:, :3] / (statistics[:, 3:4] * D))
    return (result.astype(jnp.bfloat16), input_grad.astype(jnp.bfloat16), trained_grads[0], trained_grads[1], trained_grads[2], trained_grads[3], trained_grads[4], trained_grads[5], trained_grads[6], trained_grads[7], trained_grads[8], trained_grads[9], trained_grads[10], trained_grads[11], rms_values)
```

```python
import math
from types import SimpleNamespace
from typing import Any, NamedTuple

import jax
import jax.numpy as jnp
from jax import lax
from jax.experimental import pallas as pl
from jax.experimental.pallas import tpu as pltpu
from jax.sharding import PartitionSpec as P

NEGATIVE = -1e30
EPSILON = 1e-12
ROOT_HALF = 0.7071067811865476
INV_ROOT_TAU = 0.3989422804014327
LOG2E = 1.4426950408889634

PLAN = ((3, 0), (1, 2))

BF = jnp.bfloat16
F32 = jnp.float32
ANY = pl.BlockSpec(memory_space=pl.ANY)
VMEM_LIMIT = 60 << 20

ATTN_DOWN, ATTN_UP, FFN_DOWN, FFN_UP = range(4)
MATRIX_ROWS, BLOCK_ROWS = 64, 72
UP_BIAS, GAIN, BIAS, DOWN_BIAS = range(64, 68)
STATS = 64


class Layer(NamedTuple):
    qkv: Any
    out: Any
    win: Any
    wout: Any
    mats: Any
    vecs: Any


class Adapter(NamedTuple):
    down: Any
    down_bias: Any
    up: Any
    up_bias: Any
    gain: Any
    bias: Any


def mm(a, b):
    return jnp.dot(a, b, preferred_element_type=F32)


def mm_nt(a, b):
    return lax.dot_general(a, b, (((1,), (1,)), ((), ())), preferred_element_type=F32)


def mm_tn(a, b):
    return lax.dot_general(a, b, (((0,), (0,)), ((), ())), preferred_element_type=F32)


def span_of(index, size, base=0):
    start = index * size + base
    return pl.ds(start if isinstance(index, int) else pl.multiple_of(start, size), size)


def steps(count, body, unroll=None):
    if unroll is None or unroll >= count:
        for at in range(count):
            body(at)
        return

    def some(group, carry):
        for at in range(unroll):
            body(group * unroll + at)
        return carry

    lax.fori_loop(0, count // unroll, some, 0)


PAIRS_FORWARD, PAIRS_BACKWARD = 6, 6
FFN_FORWARD, FFN_BACKWARD = 12, 12


def gelu_both(z):
    cdf = 0.5 + 0.5 * lax.erf(z * ROOT_HALF)
    bell = jnp.exp2(z * z * (-0.5 * LOG2E))
    return z * cdf, cdf + (z * INV_ROOT_TAU) * bell


def nothing(at):
    pass


def qkv_phase(h, qkv, packed, need=nothing):
    width = h.shape[-1]

    def one(at):
        need(at)
        cols = span_of(at, 256)
        y = mm(h[...], qkv[:, cols])
        if at < width // 256:
            y = y * 0.125
        packed[:, cols] = y.astype(BF)

    steps(qkv.shape[1] // 256, one)


def lane_half(shape):
    return lax.broadcasted_iota(jnp.int32, shape, len(shape) - 1) < 64


def split_pair(pair, first):
    zero = jnp.zeros_like(pair)
    return jnp.concatenate([jnp.where(first, pair, zero), jnp.where(first, zero, pair)], axis=0)


def values_and_ones(v2, first):
    one = jnp.ones_like(v2)
    return jnp.concatenate([split_pair(v2, first), split_pair(one, first)], axis=1)


def by_level(level, run):
    @pl.when(level <= 2)
    def _():
        run(256)

    @pl.when(level == 3)
    def _():
        run(512)


def pair_ignored(pair, length):
    pass


def attention_forward(level, valid, bias, packed, context, portions, linv, done=pair_ignored):
    rows, width = context.shape
    query = 256

    def run(length):
        live = valid_row(valid, level)
        barred = jnp.where(live > 0, 0.0, NEGATIVE)
        if length == 256:
            shift = 6 + level
            a = lax.broadcasted_iota(jnp.int32, (256, 256), 0) >> shift
            b = lax.broadcasted_iota(jnp.int32, (256, 256), 1) >> shift
            apart = jnp.where(a == b, 0.0, NEGATIVE)
            for block in range(rows // 256):
                bias[span_of(block, 256), :] = apart + barred[:, block * 256 : (block + 1) * 256]
        first = lane_half((length, 128))

        def pair(at):
            lanes = span_of(at, 128)
            for block in range(rows // length):
                base = block * length
                k2 = packed[base : base + length, span_of(at, 128, width)]
                v2 = packed[base : base + length, span_of(at, 128, 2 * width)]
                kk = split_pair(k2, first)
                vv = values_and_ones(v2, first)
                for part in range(length // query):
                    at_rows = pl.ds(base + part * query, query)
                    scores = mm_nt(packed[at_rows, lanes], kk)
                    halves = []
                    for head in range(2):
                        s = scores[:, head * length : (head + 1) * length]
                        s = s + (bias[at_rows, :] if length == 256 else barred)
                        top = jnp.max(s, axis=-1, keepdims=True)
                        halves.append(jnp.exp2((s - top) * LOG2E).astype(BF))
                    p = jnp.concatenate(halves, axis=1)
                    portions[at, at_rows, 0 : 2 * length] = p
                    both = mm(p, vv)
                    inverse = 1.0 / both[:, 128:]
                    linv[at_rows, lanes] = inverse.astype(BF)
                    context[at_rows, lanes] = (both[:, :128] * inverse).astype(BF)
            done(at, length)

        steps(width // 128, pair, PAIRS_FORWARD)

    by_level(level, run)


def attention_backward(level, packed, context, portions, linv, dcontext, dpacked, need=pair_ignored):
    rows, width = context.shape
    query = 256

    def run(length):
        first = lane_half((length, 128))

        def pair(at):
            need(at, length)
            lanes = span_of(at, 128)
            for block in range(rows // length):
                base = block * length
                whole = pl.ds(base, length)
                k2 = packed[whole, span_of(at, 128, width)]
                v2 = packed[whole, span_of(at, 128, 2 * width)]
                kk = split_pair(k2, first)
                vv = values_and_ones(v2, first)
                dk = None
                dv = None
                for part in range(length // query):
                    at_rows = pl.ds(base + part * query, query)
                    out = dcontext[at_rows, lanes].astype(F32) * linv[at_rows, lanes].astype(F32)
                    low = out.astype(BF)
                    both = jnp.concatenate(
                        [low, (-out * context[at_rows, lanes].astype(F32)).astype(BF)], axis=1
                    )
                    p = portions[at, at_rows, 0 : 2 * length]
                    ds = p * mm_nt(both, vv).astype(BF)
                    q2 = packed[at_rows, lanes]
                    dpacked[at_rows, lanes] = (mm(ds, kk) * 0.125).astype(BF)
                    more_k = mm_tn(ds, q2)
                    more_v = mm_tn(p, low)
                    dk = more_k if dk is None else dk + more_k
                    dv = more_v if dv is None else dv + more_v
                dk = jnp.where(first, dk[:length], dk[length:])
                dv = jnp.where(first, dv[:length], dv[length:])
                dpacked[whole, span_of(at, 128, width)] = dk.astype(BF)
                dpacked[whole, span_of(at, 128, 2 * width)] = dv.astype(BF)

        steps(width // 128, pair, PAIRS_BACKWARD)

    by_level(level, run)


def project(x, weight, out):
    def one(at):
        cols = span_of(at, 256)
        out[:, cols] = mm(x[...], weight[:, cols]).astype(BF)

    steps(out.shape[1] // 256, one)


def project_back(x, weight, out):
    def one(at):
        cols = span_of(at, 256)
        out[:, cols] = mm_nt(x[...], weight[cols, :]).astype(BF)

    steps(out.shape[1] // 256, one)


def adapter_norm(base, inner, live, w, saved, out, stats):
    act, slope, std, scale = saved
    rows, width = inner.shape
    block = 128

    def one(at):
        r = span_of(at, block)
        x = inner[r, :]
        pre = mm_nt(x, w.down[...]) + w.down_bias
        a, g = gelu_both(pre)
        a = a.astype(BF)
        act[r, :] = a
        slope[r, :] = g
        branch = x.astype(F32) + (mm(a, w.up[...]) + w.up_bias)
        total = base[r, :].astype(F32) + branch
        alive = live[r, :]
        stats[0:1, :] += jnp.sum(branch * branch * alive, axis=0, keepdims=True)
        mean = jnp.mean(total, axis=-1, keepdims=True)
        centered = total - mean
        variance = jnp.mean(centered * centered, axis=-1, keepdims=True)
        square = jnp.sum((variance + mean * mean) * alive, axis=0, keepdims=True)
        stats[1:2, :] += jnp.broadcast_to(square, (1, width))
        s = lax.rsqrt(variance + EPSILON)
        n = centered * s
        std[r, :] = n.astype(BF)
        scale[r, :] = s
        out[r, :] = (n * w.gain + w.bias).astype(BF)

    steps(rows // block, one)


def ffn_forward(middle, win, wout, act, slope, returned, need=nothing):
    need(0)
    expand(middle, win, act, slope)
    need(1)
    project(act, wout, returned)


def expand(middle, win, act, slope):

    def one(at):
        cols = span_of(at, 256)
        z = mm(middle[...], win[:, cols])
        a, g = gelu_both(z)
        act[:, cols] = a.astype(BF)
        slope[:, cols] = g.astype(BF)

    steps(win.shape[1] // 256, one, FFN_FORWARD)


def norm_adapter_back(dtotal, saved, inner, w, low, dpre_all, dinner, grads_down, grads_up):
    act, slope, std, scale = saved
    rows = inner.shape[0]
    block = 128

    def add(row, values):
        grads_down[row : row + 1, 0 : values.shape[1]] += jnp.sum(values, axis=0, keepdims=True)

    def one(at):
        r = span_of(at, block)
        g = dtotal[r, :]
        n = std[r, :].astype(F32)
        add(GAIN, g * n)
        add(BIAS, g)
        gg = g * w.gain
        m1 = jnp.mean(gg, axis=-1, keepdims=True)
        m2 = jnp.mean(gg * n, axis=-1, keepdims=True)
        d = scale[r, :] * (gg - m1 - n * m2)
        dtotal[r, :] = d
        e = d.astype(BF)
        low[r, :] = e
        e32 = e.astype(F32)
        add(UP_BIAS, e32)
        dpre = (mm_nt(e, w.up[...]) * slope[r, :]).astype(BF)
        dpre_all[r, :] = dpre
        add(DOWN_BIAS, dpre.astype(F32))
        dinner[r, :] = (e32 + mm(dpre, w.down[...])).astype(BF)

    steps(rows // block, one)
    grads_up[0:MATRIX_ROWS, :] += mm_tn(act[...], low[...])
    grads_down[0:MATRIX_ROWS, :] += mm_tn(dpre_all[...], inner[...])


def ffn_backward(dreturned, win, wout, slope, dexp, dsecond):
    expand_back(dreturned, wout, slope, dexp)
    project_add(dexp, win, dsecond)


def expand_back(dreturned, wout, slope, dexp):
    def one(at):
        cols = span_of(at, 256)
        d = mm_nt(dreturned[...], wout[cols, :])
        dexp[:, cols] = d.astype(BF) * slope[:, cols]

    steps(wout.shape[0] // 256, one, FFN_BACKWARD)


def project_add(x, weight, out):
    def one(at):
        cols = span_of(at, 256)
        out[:, cols] += mm_nt(x[...], weight[cols, :])

    steps(weight.shape[0] // 256, one)


def input_backward(dpacked, qkv, dfirst, dentry):
    def one(at):
        cols = span_of(at, 256)
        d = mm_nt(dpacked[...], qkv[cols, :])
        dentry[:, cols] = (dfirst[:, cols].astype(F32) + d).astype(BF)

    steps(qkv.shape[0] // 256, one)


class Item(NamedTuple):
    make: Any
    ref: Any

    def start(self):
        self.make().start()

    def wait(self):
        self.make().wait()


class Call:
    def __init__(self, section, slots, base=0):
        self.slots, self.base = slots, base
        self.args, self.in_specs, self.in_names = [], [], []
        self.outs, self.out_specs, self.out_names = [], [], []
        self.scratch, self.scratch_names = [], []
        self.kinds = {}
        self.section = section
        self.flops = 0

    def _add(self, name, array, spec):
        self.args.append(array)
        self.in_specs.append(spec)
        self.in_names.append(name)

    def _temp(self, name, shape):
        self.scratch.append(shape)
        self.scratch_names.append(name)

    def whole(self, **arrays):
        for name, array in arrays.items():
            zeros = (0,) * array.ndim
            self._add(name, array, pl.BlockSpec(array.shape, lambda i, s, zeros=zeros: zeros))

    def raw(self, **arrays):
        for name, array in arrays.items():
            self._add(name, array, ANY)

    def load(self, micro=False, depth=2, **arrays):
        for name, array in arrays.items():
            depth_of = min(depth, self.slots)
            self._add((name, 0), array, ANY)
            self._temp((name, 1), pltpu.VMEM((depth_of,) + array.shape[1:], array.dtype))
            self._temp((name, 2), pltpu.SemaphoreType.DMA((depth_of,)))
            self.kinds[name] = (0, depth_of, micro)

    def save(self, depth=2, **shapes):
        for name, (shape, dtype) in shapes.items():
            depth_of = min(depth, self.slots)
            self.outs.append(jax.ShapeDtypeStruct((self.slots,) + shape, dtype))
            self.out_specs.append(ANY)
            self.out_names.append((name, 0))
            self._temp((name, 1), pltpu.VMEM((depth_of,) + shape, dtype))
            self._temp((name, 2), pltpu.SemaphoreType.DMA((depth_of,)))
            self.kinds[name] = (1, depth_of, False)

    def out(self, **shapes):
        for name, (shape, dtype) in shapes.items():
            self.outs.append(jax.ShapeDtypeStruct(shape, dtype))
            self.out_specs.append(ANY)
            self.out_names.append(name)

    def total(self, **shapes):
        for name, shape in shapes.items():
            zeros = (0,) * len(shape)
            self.outs.append(jax.ShapeDtypeStruct(shape, F32))
            self.out_specs.append(pl.BlockSpec(shape, lambda i, s, zeros=zeros: zeros))
            self.out_names.append(name)

    def temp(self, **shapes):
        for name, (shape, dtype) in shapes.items():
            self._temp(name, pltpu.VMEM(shape, dtype))

    def sems(self, **counts):
        for name, count in counts.items():
            self._temp(name, pltpu.SemaphoreType.DMA(count if isinstance(count, tuple) else (count,)))

    def run(self, body, name):
        names = self.in_names + self.out_names + self.scratch_names
        slots, base = self.slots, self.base

        def kernel(section, *refs):
            step = pl.program_id(0) if slots > 1 else 0
            ref = dict(zip(names, refs))
            r = SimpleNamespace(**{n: v for n, v in ref.items() if isinstance(n, str)})
            r.step, r.section = step, section[0]

            def level_in(which, slot):
                number = PLAN[which][base]
                for other in range(1, slots):
                    number = jnp.where(slot == other, PLAN[which][base + other], number)
                return number

            def level(slot):
                return jnp.where(r.section == 0, level_in(0, slot), level_in(1, slot))

            def copy(name, slot):
                kind, depth, micro = self.kinds[name]
                at = slot if depth > 1 else 0
                near = ref[name, 1].at[at]
                if kind == 0:
                    far = ref[name, 0].at[level(slot) if micro else base + slot]
                    pair = (far, near)
                else:
                    pair = (near, ref[name, 0].at[slot])
                return Item(lambda: pltpu.make_async_copy(*pair, ref[name, 2].at[at]), near)

            def start(*which):
                for n in which:
                    copy(n, step).start()

            def wait(*which):
                for n in which:
                    copy(n, step).wait()

            def at_first(act):
                if slots > 1:
                    pl.when(step == 0)(act)
                else:
                    act()

            def at_last(act):
                if slots > 1:
                    pl.when(step == slots - 1)(act)
                else:
                    act()

            r.level_of, r.level = level, level(step)
            r.copy, r.start, r.wait, r.at_first, r.at_last = copy, start, wait, at_first, at_last
            for n, (kind, depth, micro) in self.kinds.items():
                setattr(r, n, ref[n, 1].at[step if depth > 1 else 0])
                setattr(r, "all_" + n, (ref[n, 0], ref[n, 1]))
            body(r)

        results = pl.pallas_call(
            kernel,
            out_shape=self.outs,
            grid_spec=pltpu.PrefetchScalarGridSpec(
                num_scalar_prefetch=1,
                grid=(slots,),
                in_specs=self.in_specs,
                out_specs=self.out_specs,
                scratch_shapes=self.scratch,
            ),
            compiler_params=pltpu.CompilerParams(vmem_limit_bytes=VMEM_LIMIT),
            cost_estimate=pl.CostEstimate(
                flops=self.flops * slots, bytes_accessed=1 << 20, transcendentals=0
            ),
            name=name,
        )(self.section, *self.args)
        return SimpleNamespace(
            **{n[0] if isinstance(n, tuple) else n: v for n, v in zip(self.out_names, results)}
        )


class Fill:
    def __init__(self, own, got, target, sems, mine, pieces=1, dim=0):
        self.sources, self.target, self.sems, self.mine = (own, got), target, sems, mine
        self.pieces, self.dim = pieces, dim

    def _copy(self, source, piece):
        source = self.sources[source]
        if self.pieces == 1:
            return pltpu.make_async_copy(source, self.target, self.sems.at[0])
        size = self.target.shape[self.dim] // self.pieces
        cut = tuple(
            pl.ds(piece * size, size) if at == self.dim else slice(None)
            for at in range(len(self.target.shape))
        )
        return pltpu.make_async_copy(source.at[cut], self.target.at[cut], self.sems.at[piece])

    def start(self):
        for source, chosen_one in enumerate((self.mine, jnp.logical_not(self.mine))):

            @pl.when(chosen_one)
            def _():
                for piece in range(self.pieces):
                    self._copy(source, piece).start()

    def wait(self, piece=None):
        for at in range(self.pieces) if piece is None else (piece,):
            self._copy(0, at).wait()


def zero(*refs):
    for ref in refs:
        ref[...] = jnp.zeros_like(ref)


def valid_row(valid, level):
    row = valid[0:1, :]
    for other in range(1, valid.shape[0]):
        row = jnp.where(level == other, valid[other : other + 1, :], row)
    return row


def live_column(valid, level, live):
    row = jnp.where(valid_row(valid, level) > 0, 1.0, 0.0)
    row = jnp.broadcast_to(row, (8, row.shape[1])).astype(BF)
    live[...] = mm_tn(row, jnp.full((8, 128), 0.125, BF))[:, 0:1]


def adapter_of(mats, vecs, which):
    vec = vecs.at[which]
    return Adapter(
        mats.at[2 * which], vec[0:1, 0:64], mats.at[2 * which + 1], vec[1:2, :], vec[2:3, :], vec[3:4, :]
    )


def portions_shape(rows, width):
    return ((width // 128, rows, 2 * rows), BF)


def attn_saved(rows, width, hidden):
    return dict(
        packed=((rows, 3 * width), BF), context=((rows, width), BF), linv=((rows, width), BF)
    )


def norm_saved(rows, width):
    return dict(
        attended=((rows, width), BF),
        act1=((rows, 64), BF),
        slope1=((rows, 64), F32),
        std1=((rows, width), BF),
        scale1=((rows, 1), F32),
    )


def ffn_saved(rows, width, hidden):
    return dict(
        slope=((rows, hidden), BF),
        returned=((rows, width), BF),
        act2=((rows, 64), BF),
        slope2=((rows, 64), F32),
        std2=((rows, width), BF),
        scale2=((rows, 1), F32),
    )


STAT_ROWS = 8


def pair_copy(source, target, sems, pair, length):
    lanes = pl.ds(0, 2 * length)
    return pltpu.make_async_copy(
        source.at[pair, :, lanes], target.at[pair, :, lanes], sems.at[pair]
    )


def first_attn_forward(section, tokens, valid, own, got, sizes, slots):
    rows, width, hidden = sizes
    pairs = width // 128
    call = Call(section, slots)
    call.load(micro=True, h=tokens)
    call.whole(valid=valid)
    call.raw(own=own.qkv, got=got.qkv, own_out=own.out, got_out=got.out)
    call.whole(own_mats=own.mats, got_mats=got.mats, own_vecs=own.vecs, got_vecs=got.vecs)
    call.save(**attn_saved(*sizes), **norm_saved(rows, width), middle=((rows, width), BF))
    shape, dtype = portions_shape(rows, width)
    call.out(portions=((slots,) + shape, dtype))
    call.total(stats=(2, width))
    call.temp(
        held=((slots,) + shape, dtype),
        live=((rows, 1), F32),
        bias=((rows, 256), F32),
        qkv=(own.qkv.shape, BF),
        out=(own.out.shape, BF),
        mats=(own.mats.shape, BF),
        vecs=(own.vecs.shape, F32),
    )
    call.sems(qkv_sems=3, out_sems=1, pair_sems=(slots, pairs))
    call.flops = 2 * rows * width * width * 12

    def body(r):
        mine = r.section == 0
        qkv = Fill(r.own, r.got, r.qkv, r.qkv_sems, mine, 3, 2)
        out = Fill(r.own_out, r.got_out, r.out, r.out_sems, mine)

        def begin():
            r.copy("h", 0).start()
            qkv.start()
            out.start()
            for slot in range(1, slots):
                r.copy("h", slot).start()
            zero(r.stats)
            r.mats[...] = jnp.where(mine, r.own_mats[...], r.got_mats[...])
            r.vecs[...] = jnp.where(mine, r.own_vecs[...], r.got_vecs[...])

        r.at_first(begin)
        live_column(r.valid, r.level, r.live)
        r.wait("h")
        qkv_phase(r.h, r.qkv.at[0], r.packed, lambda at: at % 3 or r.at_first(lambda: qkv.wait(at // 3)))
        r.start("packed")

        def pair_copy_of(slot, pair, length):
            return pair_copy(r.held.at[slot], r.portions.at[slot], r.pair_sems.at[slot], pair, length)

        attention_forward(
            r.level, r.valid, r.bias, r.packed, r.context, r.held.at[r.step], r.linv,
            lambda pair, length: pair_copy_of(r.step, pair, length).start(),
        )
        r.start("context", "linv")
        r.at_first(out.wait)
        project(r.context, r.out.at[0], r.attended)
        saved = (r.act1, r.slope1, r.std1, r.scale1)
        adapter_norm(
            r.h, r.attended, r.live, adapter_of(r.mats, r.vecs, 0), saved, r.middle, r.stats
        )
        r.start("middle", *norm_saved(rows, width))

        def finish():
            for slot in range(slots):
                for name in ("middle", *attn_saved(*sizes), *norm_saved(rows, width)):
                    r.copy(name, slot).wait()

                def waits(length):
                    for pair in range(pairs):
                        pair_copy_of(slot, pair, length).wait()

                by_level(r.level_of(slot), waits)

        r.at_last(finish)

    return call.run(body, "first_attn")


STAGE_ATTN0, STAGE_FFN0, STAGE_ATTN1, STAGE_FFN1 = range(4)


def middle_part(section, kept, cotangent, valid, own, got, sizes, slots):
    rows, width, hidden = sizes
    call = Call(section, slots)
    row = ((rows, width), BF)
    call.raw(base=kept.middle, cotangent=cotangent, **{"far_" + n: getattr(kept, n) for n in norm_saved(rows, width)})
    call.whole(valid=valid, stats=kept.stats)
    for name in ("qkv", "out", "win", "wout", "mats", "vecs"):
        call.raw(**{"own_" + name: getattr(own, name), "got_" + name: getattr(got, name)})
    call.temp(
        qkv=(own.qkv.shape, BF),
        win=(own.win.shape, BF),
        wout=(own.wout.shape, BF),
        outs=((2,) + own.out.shape, BF),
        mats=((2,) + own.mats.shape, BF),
        vecs=((2,) + own.vecs.shape, F32),
    )
    call.sems(win_sems=4, wout_sems=1, weight_sems=(8, 1), base_sems=1, up_sems=1, norm_sems=5)
    call.save(depth=1, result=row, dfirst0=row, dcontext0=row)
    call.total(grads=(8, BLOCK_ROWS, width))
    call.temp(**attn_saved(*sizes))
    call.temp(
        attended=((4,) + row[0], BF),
        act1=((4, rows, 64), BF),
        slope1=((4, rows, 64), F32),
        std1=((4,) + row[0], BF),
        scale1=((4, rows, 1), F32),
        slope=((2, rows, hidden), BF),
        chain=((3,) + row[0], BF),
        sums=((4, 2, width), F32),
        up=row,
        held=portions_shape(rows, width),
        live=((rows, 1), F32),
        bias=((rows, 256), F32),
        wide=((rows, hidden), BF),
        dsum=((rows, width), F32),
        low=row,
        dpre=((rows, 64), BF),
        dinner=row,
    )
    call.flops = 12 * rows * width * (4 * width + 2 * hidden)
    norms = tuple(norm_saved(rows, width))

    def body(r):
        first, second = r.section == 0, r.section == 1

        def fill(name, target, at, mine):
            return Fill(
                getattr(r, "own_" + name), getattr(r, "got_" + name), target, r.weight_sems.at[at], mine
            )

        qkv, out1 = fill("qkv", r.qkv, 0, second), fill("out", r.outs.at[1], 1, second)
        mats1, vecs1 = fill("mats", r.mats.at[1], 2, second), fill("vecs", r.vecs.at[1], 3, second)
        out0 = fill("out", r.outs.at[0], 4, first)
        mats0, vecs0 = fill("mats", r.mats.at[0], 5, first), fill("vecs", r.vecs.at[0], 6, first)
        win0, win1 = (Fill(r.own_win, r.got_win, r.win, r.win_sems, m, 4, 2) for m in (first, second))
        wout0, wout1 = (Fill(r.own_wout, r.got_wout, r.wout, r.wout_sems, m) for m in (first, second))

        def base_copy(slot):
            return pltpu.make_async_copy(r.base.at[slot], r.chain.at[0], r.base_sems.at[0])

        def slot_copies():
            copies = [pltpu.make_async_copy(r.cotangent.at[r.level], r.up, r.up_sems.at[0])]
            for at, name in enumerate(norms):
                copies.append(
                    pltpu.make_async_copy(
                        getattr(r, "far_" + name).at[r.step], getattr(r, name).at[0], r.norm_sems.at[at]
                    )
                )
            return copies

        def begin():
            for item in (mats0, vecs0):
                item.start()
            base_copy(0).start()
            for item in (win0, wout0, qkv, out1, mats1, vecs1, out0):
                item.start()
            zero(r.grads, r.sums)
            mats0.wait()
            vecs0.wait()
            win0.wait()
            wout0.wait()

        def later(act):
            pl.when(r.step > 0)(act)

        r.at_first(begin)
        for item in slot_copies():
            item.start()
        live_column(r.valid, r.level, r.live)
        base_copy(r.step).wait()
        later(lambda: r.copy("result", r.step - 1).wait())

        def saved_of(stage):
            return tuple(getattr(r, n).at[stage] for n in ("act1", "slope1", "std1", "scale1"))

        def adapter_at(stage):
            return adapter_of(r.mats.at[stage // 2], r.vecs.at[stage // 2], stage % 2)

        def forward(at, carry):
            stage = at + 1
            inner = r.attended.at[stage]
            here = r.chain.at[at]

            @pl.when(at == 1)
            def _():
                win1.start()
                wout1.start()
                for item in (qkv, out1, mats1, vecs1):
                    r.at_first(item.wait)
                qkv_phase(here, r.qkv.at[0], r.packed)
                attention_forward(r.level, r.valid, r.bias, r.packed, r.context, r.held, r.linv)
                project(r.context, r.outs.at[1, 0], inner)

            @pl.when(at != 1)
            def _():
                @pl.when(at == 2)
                def _():
                    win1.wait()
                    wout1.wait()

                ffn_forward(here, r.win.at[0], r.wout.at[0], r.wide, r.slope.at[stage // 2], inner)

            def norm(target):
                adapter_norm(
                    here, inner, r.live, adapter_at(stage), saved_of(stage), target, r.sums.at[stage]
                )

            norm(r.chain.at[lax.rem(at + 1, 3)])
            return carry

        lax.fori_loop(0, 3, forward, 0)
        r.result[...] = r.chain[0]
        r.start("result")

        @pl.when(r.step + 1 < slots)
        def _():
            base_copy(r.step + 1).start()

        for item in slot_copies():
            item.wait()

        def backward(at, carry):
            stage = 3 - at
            inner = r.attended.at[stage]

            @pl.when(stage % 2 == 1)
            def _():
                r.dsum[...] = r.up[...].astype(F32)

            norm_adapter_back(
                r.dsum, saved_of(stage), inner, adapter_at(stage), r.low, r.dpre, r.dinner,
                r.grads.at[2 * stage], r.grads.at[2 * stage + 1],
            )

            @pl.when(stage % 2 == 1)
            def _():
                @pl.when(at == 2)
                def _():
                    wout0.wait()
                    win0.wait()

                ffn_backward(r.dinner, r.win.at[0], r.wout.at[0], r.slope.at[stage // 2], r.wide, r.dsum)

            @pl.when(stage % 2 == 0)
            def _():
                @pl.when(at == 3)
                def _():
                    r.at_first(out0.wait)
                    later(lambda: r.copy("dfirst0", r.step - 1).wait())

                @pl.when(at == 1)
                def _():
                    wout0.start()
                    win0.start()
                    later(lambda: r.copy("dcontext0", r.step - 1).wait())

                project_back(r.dinner, r.outs.at[stage // 2, 0], r.dcontext0)

                @pl.when(at == 1)
                def _():
                    attention_backward(
                        r.level, r.packed, r.context, r.held, r.linv, r.dcontext0, r.packed
                    )
                    input_backward(r.packed, r.qkv.at[0], r.dsum, r.up)

            return carry

        lax.fori_loop(0, 4, backward, 0)
        r.dfirst0[...] = r.dsum[...].astype(BF)
        r.start("dfirst0", "dcontext0")

        def finish():
            r.wait("result", "dfirst0", "dcontext0")
            for layer in range(2):
                attn, ffn = r.sums.at[2 * layer], r.sums.at[2 * layer + 1]
                target = r.grads.at[4 * layer + ATTN_UP]
                if layer == 0:
                    attn = r.stats
                target[STATS : STATS + 1, :] = attn[0:1, :]
                target[STATS + 1 : STATS + 3, :] = ffn[...]
                count = jnp.zeros((1, 1), F32)
                for slot in range(slots):
                    row = jnp.where(valid_row(r.valid, r.level_of(slot)) > 0, 1.0, 0.0)
                    count += jnp.sum(row, axis=1, keepdims=True)
                target[STATS + 3 : STATS + 4, :] = jnp.broadcast_to(count, (1, width))

        r.at_last(finish)

    return call.run(body, "middle_part")


def first_attn_backward(section, back, kept, own, got, sizes, slot, others=None):
    rows, width, hidden = sizes
    pairs = width // 128
    call = Call(section, 1, slot)
    call.load(packed=kept.packed, dcontext=back.dcontext0, context=kept.context, linv=kept.linv)
    call.load(dfirst=back.dfirst0)
    call.raw(portions=kept.portions, own=own.qkv, got=got.qkv)
    call.temp(held=portions_shape(rows, width), qkv=(own.qkv.shape, BF))
    call.sems(qkv_sems=3, pair_sems=pairs)
    if others is None:
        call.save(dentry=((rows, width), BF))
    else:
        moved, here, there = others
        slots = here.shape[0]
        call.raw(moved=moved, here=here, there=there)
        call.temp(stage=((2 * slots + 1, rows, width), BF))
        call.out(input_grad=((slots, rows, width), BF), result=((2 * slots, rows, width), BF))
        call.temp(dentry=((rows, width), BF))
        call.sems(move_sems=2 * slots + 2, stage_sems=2 * slots + 1)
    call.flops = 2 * rows * width * width * 12

    def body(r):
        fill = Fill(r.own, r.got, r.qkv, r.qkv_sems, r.section == 0, 3, 1)

        def pair_copy_of(pair, length):
            return pair_copy(r.portions.at[slot], r.held, r.pair_sems, pair, length)

        r.start("packed", "dcontext", "context", "linv")
        by_level(
            r.level, lambda length: [pair_copy_of(pair, length).start() for pair in range(pairs)] and None
        )
        fill.start()
        r.start("dfirst")
        moves = []
        if others is not None:
            moves.append((r.moved, r.input_grad.at[1]))
            for at in range(slots):
                mine, other = (
                    jnp.where(r.section == 0, PLAN[a][at], PLAN[1 - a][at]) for a in range(2)
                )
                moves.append((r.here.at[at], r.result.at[mine]))
                moves.append((r.there.at[at], r.result.at[other]))
        ins = [
            pltpu.make_async_copy(source, r.stage.at[at], r.stage_sems.at[at])
            for at, (source, target) in enumerate(moves)
        ]
        moves = [
            pltpu.make_async_copy(r.stage.at[at], target, r.move_sems.at[at])
            for at, (source, target) in enumerate(moves)
        ]
        for item in ins:
            item.start()
        r.wait("packed", "dcontext", "context", "linv")
        attention_backward(
            r.level, r.packed, r.context, r.held, r.linv, r.dcontext, r.packed,
            lambda pair, length: pair_copy_of(pair, length).wait(),
        )
        for item, move in zip(ins, moves):
            item.wait()
            move.start()
        r.wait("dfirst")
        fill.wait()
        input_backward(r.packed, r.qkv.at[0], r.dfirst, r.dentry)
        if others is None:
            r.start("dentry")
            r.wait("dentry")
        else:
            last = pltpu.make_async_copy(r.dentry, r.input_grad.at[0], r.move_sems.at[len(moves)])
            last.start()
            for move in moves + [last]:
                move.wait()

    return call.run(body, "attn_back")


def packed_small(mats, vecs):
    width = mats[0].shape[-1]

    def kernel(*refs):
        sources, (out_mats, out_vecs) = refs[:-2], refs[-2:]
        for at in range(4):
            out_mats[at] = sources[at][0]
        out_vecs[...] = jnp.zeros_like(out_vecs)
        for at, ref in enumerate(sources[4:]):
            out_vecs[at // 4, at % 4 : at % 4 + 1, 0 : ref.shape[1]] = ref[...]

    return pl.pallas_call(
        kernel,
        out_shape=(
            jax.ShapeDtypeStruct((4, 64, width), BF),
            jax.ShapeDtypeStruct((2, 4, width), F32),
        ),
        name="pack",
    )(*mats, *vecs)


def unpacked(part, other, upper):
    width = part.shape[-1]
    matrix = jax.ShapeDtypeStruct((1, MATRIX_ROWS, width), F32)
    vector = jax.ShapeDtypeStruct((1, width), F32)
    small = jax.ShapeDtypeStruct((1, 64), F32)
    group = (matrix, small, matrix, vector, vector, vector)

    def kernel(upper, part, other, *outs):
        def block(at):
            mine = upper[0] == (1 if at >= 2 else 0)
            return jnp.where(mine, part[at % 2], other[at % 2]).astype(F32)

        for down, up, (mat_down, down_bias, mat_up, up_bias, gain, bias) in (
            (ATTN_DOWN, ATTN_UP, outs[:6]),
            (FFN_DOWN, FFN_UP, outs[6:12]),
        ):
            down, up = block(down), block(up)
            mat_down[0] = down[:MATRIX_ROWS]
            mat_up[0] = up[:MATRIX_ROWS]
            for row, target in ((UP_BIAS, up_bias), (GAIN, gain), (BIAS, bias), (DOWN_BIAS, down_bias)):
                target[...] = down[row : row + 1, : target.shape[1]]
        sums = block(ATTN_UP)[STATS : STATS + STAT_ROWS]
        means = jnp.sum(sums, axis=1, keepdims=True) / (sums[3:4, 0:1] * width)
        lane = lax.broadcasted_iota(jnp.int32, (1, 3), 1)
        picked = jnp.where(lane == 0, means[0:1], jnp.where(lane == 1, means[1:2], means[2:3]))
        outs[12][...] = jnp.sqrt(picked)

    vmem = pl.BlockSpec(memory_space=pltpu.VMEM)
    outs = pl.pallas_call(
        kernel,
        in_specs=[pl.BlockSpec(memory_space=pltpu.SMEM), vmem, vmem],
        out_shape=group * 2 + (jax.ShapeDtypeStruct((1, 3), F32),),
        name="unpack",
    )(upper.astype(jnp.int32).reshape(1), part, other)
    outs = list(outs)
    for at in (0, 6):
        outs[at] = jnp.swapaxes(outs[at], 1, 2)
    return tuple(outs)


def swap(value):
    return lax.ppermute(value, "section", [(0, 1), (1, 0)])


def after(value, *others):
    return lax.optimization_barrier((value,) + others)[0]


def exchanged(value, first_bit, second_bit):
    count = lax.axis_size("dp")
    pairs = [
        (section * count + at, section * count + (at ^ bit))
        for section, bit in enumerate((first_bit, second_bit))
        for at in range(count)
    ]
    return lax.ppermute(value, ("section", "dp"), pairs)


def summed_halves(part):
    section, mine = lax.axis_index("section"), lax.axis_index("dp")
    count = lax.axis_size("dp")
    halvings = ((1, 2), (2, 1))

    def is_upper(pair):
        return (mine & jnp.where(section == 0, pair[0], pair[1])) > 0

    for pair in halvings:
        upper = is_upper(pair)
        half = part.shape[0] // 2
        low, high = part[:half], part[half:]
        part = jnp.where(upper, high, low) + exchanged(jnp.where(upper, low, high), *pair)
    bit = 4
    while bit < count:
        part = part + exchanged(part, bit, bit)
        bit *= 2
    other, upper = exchanged(part, *halvings[1]), is_upper(halvings[1])
    part = jnp.concatenate([jnp.where(upper, other, part), jnp.where(upper, part, other)])
    return part, exchanged(part, *halvings[0]), is_upper(halvings[0])


def body(
    tokens, valid, cotangent, qkv, out, win, wout,
    attn_down, attn_down_bias, attn_up, attn_up_bias, gain1, bias1,
    ffn_down, ffn_down_bias, ffn_up, ffn_up_bias, gain2, bias2,
):
    section = lax.axis_index("section")
    micro_count, rows, width = tokens.shape
    sizes = (rows, width, win.shape[-1])
    slots = micro_count // 2
    mats, vecs = packed_small(
        (jnp.swapaxes(attn_down, 1, 2), attn_up, jnp.swapaxes(ffn_down, 1, 2), ffn_up),
        (attn_down_bias, attn_up_bias, gain1, bias1, ffn_down_bias, ffn_up_bias, gain2, bias2),
    )
    own = Layer(qkv, out, win, wout, mats, vecs)
    early = [swap(v) for v in (qkv, out, mats, vecs)]
    got_qkv, got_out, got_mats, got_vecs = early
    got_win, got_wout = (swap(after(v, *early)) for v in (win, wout))
    got = Layer(got_qkv, got_out, got_win, got_wout, got_mats, got_vecs)
    where = section.astype(jnp.int32).reshape(1)

    kept = first_attn_forward(where, tokens, valid, own, got, sizes, slots)
    back = middle_part(where, kept, cotangent, valid, own, got, sizes, slots)
    there = swap(back.result)

    grads = [v.astype(BF) for v in (back.grads[:4], back.grads[4:])]
    part = jnp.where(section == 0, *grads) + swap(jnp.where(section == 0, *grads[::-1]))
    small = unpacked(*summed_halves(part))

    moved = swap(first_attn_backward(where, back, kept, own, got, sizes, 0).dentry[0])
    last = first_attn_backward(where, back, kept, own, got, sizes, 1, (moved, back.result, there))
    return (last.result, last.input_grad) + small


def solution(mesh):
    rows = P(None, "dp", None)
    matrix, vector = P("section", None, None), P("section", None)
    weights = (matrix, vector, matrix, vector, vector, vector)
    return jax.shard_map(
        body,
        mesh=mesh,
        in_specs=(rows, P(None, "dp"), rows) + (matrix,) * 4 + weights * 2,
        out_specs=(rows, P("section", "dp", None)) + weights * 2 + (vector,),
        check_vma=False,
    )
```

```python
import math
from types import SimpleNamespace
from typing import Any, NamedTuple

import jax
import jax.numpy as jnp
from jax import lax
from jax.experimental import pallas as pl
from jax.experimental.pallas import tpu as pltpu
from jax.sharding import PartitionSpec as P

NEGATIVE = -1e30
EPSILON = 1e-12
ROOT_HALF = 0.7071067811865476
INV_ROOT_TAU = 0.3989422804014327
LOG2E = 1.4426950408889634

PLAN = ((0, 1), (3, 2))

BF = jnp.bfloat16
F32 = jnp.float32
ANY = pl.BlockSpec(memory_space=pl.ANY)
VMEM_LIMIT = 60 << 20

ATTN_DOWN, ATTN_UP, FFN_DOWN, FFN_UP = range(4)
MATRIX_ROWS, BLOCK_ROWS = 64, 72
UP_BIAS, GAIN, BIAS, DOWN_BIAS = range(64, 68)
STATS = 64


class Layer(NamedTuple):
    qkv: Any
    out: Any
    win: Any
    wout: Any
    mats: Any
    vecs: Any


class Adapter(NamedTuple):
    down: Any
    down_bias: Any
    up: Any
    up_bias: Any
    gain: Any
    bias: Any


def mm(a, b):
    return jnp.dot(a, b, preferred_element_type=F32)


def mm_nt(a, b):
    return lax.dot_general(a, b, (((1,), (1,)), ((), ())), preferred_element_type=F32)


def mm_tn(a, b):
    return lax.dot_general(a, b, (((0,), (0,)), ((), ())), preferred_element_type=F32)


def span_of(index, size, base=0):
    start = index * size + base
    return pl.ds(start if isinstance(index, int) else pl.multiple_of(start, size), size)


def steps(count, body, unroll=None):
    if unroll is None or unroll >= count:
        for at in range(count):
            body(at)
        return

    def some(group, carry):
        for at in range(unroll):
            body(group * unroll + at)
        return carry

    lax.fori_loop(0, count // unroll, some, 0)


PAIRS_FORWARD, PAIRS_BACKWARD = 2, 1
FFN_FORWARD, FFN_BACKWARD = 12, 12


def gelu_both(z):
    cdf = 0.5 + 0.5 * lax.erf(z * ROOT_HALF)
    bell = jnp.exp2(z * z * (-0.5 * LOG2E))
    return z * cdf, cdf + (z * INV_ROOT_TAU) * bell


def nothing(at):
    pass


def qkv_phase(h, qkv, packed, need=nothing):
    width = h.shape[-1]

    def one(at):
        need(at)
        cols = span_of(at, 256)
        y = mm(h[...], qkv[:, cols])
        if at < width // 256:
            y = y * 0.125
        packed[:, cols] = y.astype(BF)

    steps(qkv.shape[1] // 256, one)


def lane_half(shape):
    return lax.broadcasted_iota(jnp.int32, shape, len(shape) - 1) < 64


def split_pair(pair, first):
    zero = jnp.zeros_like(pair)
    return jnp.concatenate([jnp.where(first, pair, zero), jnp.where(first, zero, pair)], axis=0)


def values_and_ones(v2, first):
    one = jnp.ones_like(v2)
    return jnp.concatenate([split_pair(v2, first), split_pair(one, first)], axis=1)


def by_level(level, run):
    @pl.when(level <= 2)
    def _():
        run(256)

    @pl.when(level == 3)
    def _():
        run(512)


def pair_ignored(pair, length):
    pass


def attention_forward(level, valid, bias, packed, context, portions, linv, done=pair_ignored):
    rows, width = context.shape
    query = 256

    def run(length):
        live = valid_row(valid, level)
        barred = jnp.where(live > 0, 0.0, NEGATIVE)
        if length == 256:
            shift = 6 + level
            a = lax.broadcasted_iota(jnp.int32, (256, 256), 0) >> shift
            b = lax.broadcasted_iota(jnp.int32, (256, 256), 1) >> shift
            apart = jnp.where(a == b, 0.0, NEGATIVE)
            for block in range(rows // 256):
                bias[span_of(block, 256), :] = apart + barred[:, block * 256 : (block + 1) * 256]
        first = lane_half((length, 128))

        def pair(at):
            lanes = span_of(at, 128)
            for block in range(rows // length):
                base = block * length
                k2 = packed[base : base + length, span_of(at, 128, width)]
                v2 = packed[base : base + length, span_of(at, 128, 2 * width)]
                kk = split_pair(k2, first)
                vv = values_and_ones(v2, first)
                for part in range(length // query):
                    at_rows = pl.ds(base + part * query, query)
                    scores = mm_nt(packed[at_rows, lanes], kk)
                    halves = []
                    for head in range(2):
                        s = scores[:, head * length : (head + 1) * length]
                        s = s + (bias[at_rows, :] if length == 256 else barred)
                        top = jnp.max(s, axis=-1, keepdims=True)
                        halves.append(jnp.exp2((s - top) * LOG2E).astype(BF))
                    p = jnp.concatenate(halves, axis=1)
                    portions[at, at_rows, 0 : 2 * length] = p
                    both = mm(p, vv)
                    inverse = 1.0 / both[:, 128:]
                    linv[at_rows, lanes] = inverse.astype(BF)
                    context[at_rows, lanes] = (both[:, :128] * inverse).astype(BF)
            done(at, length)

        steps(width // 128, pair, PAIRS_FORWARD)

    by_level(level, run)


def attention_backward(level, packed, context, portions, linv, dcontext, dpacked, slot=0, copy=None):
    rows, width = context.shape
    query = 256

    def run(length):
        first = lane_half((length, 128))

        def pair(at):
            if copy is not None:
                copy(slot, at, length).wait()
            lanes = span_of(at, 128)
            for block in range(rows // length):
                base = block * length
                whole = pl.ds(base, length)
                k2 = packed[whole, span_of(at, 128, width)]
                v2 = packed[whole, span_of(at, 128, 2 * width)]
                kk = split_pair(k2, first)
                vv = values_and_ones(v2, first)
                dk = None
                dv = None
                for part in range(length // query):
                    at_rows = pl.ds(base + part * query, query)
                    out = dcontext[at_rows, lanes].astype(F32) * linv[at_rows, lanes].astype(F32)
                    low = out.astype(BF)
                    both = jnp.concatenate(
                        [low, (-out * context[at_rows, lanes].astype(F32)).astype(BF)], axis=1
                    )
                    p = portions[at, at_rows, 0 : 2 * length]
                    ds = p * mm_nt(both, vv).astype(BF)
                    q2 = packed[at_rows, lanes]
                    dpacked[at_rows, lanes] = (mm(ds, kk) * 0.125).astype(BF)
                    more_k = mm_tn(ds, q2)
                    more_v = mm_tn(p, low)
                    dk = more_k if dk is None else dk + more_k
                    dv = more_v if dv is None else dv + more_v
                dk = jnp.where(first, dk[:length], dk[length:])
                dv = jnp.where(first, dv[:length], dv[length:])
                dpacked[whole, span_of(at, 128, width)] = dk.astype(BF)
                dpacked[whole, span_of(at, 128, 2 * width)] = dv.astype(BF)

        steps(width // 128, pair, PAIRS_BACKWARD)

    by_level(level, run)


def project(x, weight, out):
    def one(at):
        cols = span_of(at, 256)
        out[:, cols] = mm(x[...], weight[:, cols]).astype(BF)

    steps(out.shape[1] // 256, one)


def project_back(x, weight, out):
    def one(at):
        cols = span_of(at, 256)
        out[:, cols] = mm_nt(x[...], weight[cols, :]).astype(BF)

    steps(out.shape[1] // 256, one)


def adapter_norm(base, inner, live, w, saved, out, stats):
    act, slope, std, scale = saved
    rows, width = inner.shape
    block = 128

    def one(at):
        r = span_of(at, block)
        x = inner[r, :]
        pre = mm_nt(x, w.down[...]) + w.down_bias
        a, g = gelu_both(pre)
        a = a.astype(BF)
        act[r, :] = a
        slope[r, :] = g
        branch = x.astype(F32) + (mm(a, w.up[...]) + w.up_bias)
        total = base[r, :].astype(F32) + branch
        alive = live[r, :]
        stats[0:1, :] += jnp.sum(branch * branch * alive, axis=0, keepdims=True)
        mean = jnp.mean(total, axis=-1, keepdims=True)
        centered = total - mean
        variance = jnp.mean(centered * centered, axis=-1, keepdims=True)
        square = jnp.sum((variance + mean * mean) * alive, axis=0, keepdims=True)
        stats[1:2, :] += jnp.broadcast_to(square, (1, width))
        s = lax.rsqrt(variance + EPSILON)
        n = centered * s
        std[r, :] = n.astype(BF)
        scale[r, :] = s
        out[r, :] = (n * w.gain + w.bias).astype(BF)

    steps(rows // block, one)


def ffn_forward(middle, win, wout, act, slope, returned, need=nothing):
    need(0)
    expand(middle, win, act, slope)
    need(1)
    project(act, wout, returned)


def expand(middle, win, act, slope):

    def one(at):
        cols = span_of(at, 256)
        z = mm(middle[...], win[:, cols])
        a, g = gelu_both(z)
        act[:, cols] = a.astype(BF)
        slope[:, cols] = g.astype(BF)

    steps(win.shape[1] // 256, one, FFN_FORWARD)


def norm_adapter_back(dtotal, saved, inner, w, low, dpre_all, dinner, grads_down, grads_up):
    act, slope, std, scale = saved
    rows = inner.shape[0]
    block = 128

    def add(row, values):
        grads_down[row : row + 1, 0 : values.shape[1]] += jnp.sum(values, axis=0, keepdims=True)

    def one(at):
        r = span_of(at, block)
        g = dtotal[r, :]
        n = std[r, :].astype(F32)
        add(GAIN, g * n)
        add(BIAS, g)
        gg = g * w.gain
        m1 = jnp.mean(gg, axis=-1, keepdims=True)
        m2 = jnp.mean(gg * n, axis=-1, keepdims=True)
        d = scale[r, :] * (gg - m1 - n * m2)
        dtotal[r, :] = d
        e = d.astype(BF)
        low[r, :] = e
        e32 = e.astype(F32)
        add(UP_BIAS, e32)
        dpre = (mm_nt(e, w.up[...]) * slope[r, :]).astype(BF)
        dpre_all[r, :] = dpre
        add(DOWN_BIAS, dpre.astype(F32))
        dinner[r, :] = (e32 + mm(dpre, w.down[...])).astype(BF)

    steps(rows // block, one)
    grads_up[0:MATRIX_ROWS, :] += mm_tn(act[...], low[...])
    grads_down[0:MATRIX_ROWS, :] += mm_tn(dpre_all[...], inner[...])


def ffn_backward(dreturned, win, wout, slope, dexp, dsecond):
    expand_back(dreturned, wout, slope, dexp)
    project_add(dexp, win, dsecond)


def expand_back(dreturned, wout, slope, dexp):
    def one(at):
        cols = span_of(at, 256)
        d = mm_nt(dreturned[...], wout[cols, :])
        dexp[:, cols] = d.astype(BF) * slope[:, cols]

    steps(wout.shape[0] // 256, one, FFN_BACKWARD)


def project_add(x, weight, out):
    def one(at):
        cols = span_of(at, 256)
        out[:, cols] += mm_nt(x[...], weight[cols, :])

    steps(weight.shape[0] // 256, one)


def input_backward(dpacked, qkv, dfirst, dentry):
    def one(at):
        cols = span_of(at, 256)
        d = mm_nt(dpacked[...], qkv[cols, :])
        dentry[:, cols] = (dfirst[:, cols].astype(F32) + d).astype(BF)

    steps(qkv.shape[0] // 256, one)


class Item(NamedTuple):
    make: Any
    ref: Any

    def start(self):
        self.make().start()

    def wait(self):
        self.make().wait()


class Call:
    def __init__(self, section, slots, base=0):
        self.slots, self.base = slots, base
        self.args, self.in_specs, self.in_names = [], [], []
        self.outs, self.out_specs, self.out_names = [], [], []
        self.scratch, self.scratch_names = [], []
        self.kinds = {}
        self.section = section
        self.flops = 0
        self.limit = VMEM_LIMIT

    def _add(self, name, array, spec):
        self.args.append(array)
        self.in_specs.append(spec)
        self.in_names.append(name)

    def _temp(self, name, shape):
        self.scratch.append(shape)
        self.scratch_names.append(name)

    def whole(self, **arrays):
        for name, array in arrays.items():
            zeros = (0,) * array.ndim
            self._add(name, array, pl.BlockSpec(array.shape, lambda i, s, zeros=zeros: zeros))

    def raw(self, **arrays):
        for name, array in arrays.items():
            self._add(name, array, ANY)

    def load(self, micro=False, depth=2, **arrays):
        for name, array in arrays.items():
            depth_of = min(depth, self.slots)
            self._add((name, 0), array, ANY)
            self._temp((name, 1), pltpu.VMEM((depth_of,) + array.shape[1:], array.dtype))
            self._temp((name, 2), pltpu.SemaphoreType.DMA((depth_of,)))
            self.kinds[name] = (0, depth_of, micro)

    def save(self, depth=2, **shapes):
        for name, (shape, dtype) in shapes.items():
            depth_of = min(depth, self.slots)
            self.outs.append(jax.ShapeDtypeStruct((self.slots,) + shape, dtype))
            self.out_specs.append(ANY)
            self.out_names.append((name, 0))
            self._temp((name, 1), pltpu.VMEM((depth_of,) + shape, dtype))
            self._temp((name, 2), pltpu.SemaphoreType.DMA((depth_of,)))
            self.kinds[name] = (1, depth_of, False)

    def out(self, **shapes):
        for name, (shape, dtype) in shapes.items():
            self.outs.append(jax.ShapeDtypeStruct(shape, dtype))
            self.out_specs.append(ANY)
            self.out_names.append(name)

    def blocks(self, **shapes):
        for name, (shape, dtype) in shapes.items():
            zeros = (0,) * len(shape)
            self.outs.append(jax.ShapeDtypeStruct(shape, dtype))
            self.out_specs.append(pl.BlockSpec(shape, lambda i, s, zeros=zeros: zeros))
            self.out_names.append(name)

    def temp(self, **shapes):
        for name, (shape, dtype) in shapes.items():
            self._temp(name, pltpu.VMEM(shape, dtype))

    def sems(self, **counts):
        for name, count in counts.items():
            self._temp(name, pltpu.SemaphoreType.DMA(count if isinstance(count, tuple) else (count,)))

    def run(self, body, name):
        names = self.in_names + self.out_names + self.scratch_names
        slots, base = self.slots, self.base

        def kernel(section, *refs):
            step = pl.program_id(0) if slots > 1 else 0
            ref = dict(zip(names, refs))
            r = SimpleNamespace(**{n: v for n, v in ref.items() if isinstance(n, str)})
            r.step, r.section = step, section[0]

            def level_in(which, slot):
                number = PLAN[which][base]
                for other in range(1, slots):
                    number = jnp.where(slot == other, PLAN[which][base + other], number)
                return number

            def level(slot):
                return jnp.where(r.section == 0, level_in(0, slot), level_in(1, slot))

            def copy(name, slot):
                kind, depth, micro = self.kinds[name]
                at = slot if depth > 1 else 0
                near = ref[name, 1].at[at]
                if kind == 0:
                    far = ref[name, 0].at[level(slot) if micro else base + slot]
                    pair = (far, near)
                else:
                    pair = (near, ref[name, 0].at[slot])
                return Item(lambda: pltpu.make_async_copy(*pair, ref[name, 2].at[at]), near)

            def start(*which):
                for n in which:
                    copy(n, step).start()

            def wait(*which):
                for n in which:
                    copy(n, step).wait()

            def at_first(act):
                if slots > 1:
                    pl.when(step == 0)(act)
                else:
                    act()

            def at_last(act):
                if slots > 1:
                    pl.when(step == slots - 1)(act)
                else:
                    act()

            r.level_of, r.level = level, level(step)
            r.copy, r.start, r.wait, r.at_first, r.at_last = copy, start, wait, at_first, at_last
            for n, (kind, depth, micro) in self.kinds.items():
                setattr(r, n, ref[n, 1].at[step if depth > 1 else 0])
                setattr(r, "all_" + n, (ref[n, 0], ref[n, 1]))
            body(r)

        results = pl.pallas_call(
            kernel,
            out_shape=self.outs,
            grid_spec=pltpu.PrefetchScalarGridSpec(
                num_scalar_prefetch=1,
                grid=(slots,),
                in_specs=self.in_specs,
                out_specs=self.out_specs,
                scratch_shapes=self.scratch,
            ),
            compiler_params=pltpu.CompilerParams(vmem_limit_bytes=self.limit),
            cost_estimate=pl.CostEstimate(
                flops=self.flops * slots, bytes_accessed=1 << 20, transcendentals=0
            ),
            name=name,
        )(self.section, *self.args)
        return SimpleNamespace(
            **{n[0] if isinstance(n, tuple) else n: v for n, v in zip(self.out_names, results)}
        )


class Fill:
    def __init__(self, own, got, target, sems, mine, pieces=1, dim=0):
        self.sources, self.target, self.sems, self.mine = (own, got), target, sems, mine
        self.pieces, self.dim = pieces, dim

    def _copy(self, source, piece):
        source = self.sources[source]
        if self.pieces == 1:
            return pltpu.make_async_copy(source, self.target, self.sems.at[0])
        size = self.target.shape[self.dim] // self.pieces
        cut = tuple(
            pl.ds(piece * size, size) if at == self.dim else slice(None)
            for at in range(len(self.target.shape))
        )
        return pltpu.make_async_copy(source.at[cut], self.target.at[cut], self.sems.at[piece])

    def start(self):
        for source, chosen_one in enumerate((self.mine, jnp.logical_not(self.mine))):

            @pl.when(chosen_one)
            def _():
                for piece in range(self.pieces):
                    self._copy(source, piece).start()

    def wait(self, piece=None):
        for at in range(self.pieces) if piece is None else (piece,):
            self._copy(0, at).wait()


def zero(*refs):
    for ref in refs:
        ref[...] = jnp.zeros_like(ref)


def valid_row(valid, level):
    row = valid[0:1, :]
    for other in range(1, valid.shape[0]):
        row = jnp.where(level == other, valid[other : other + 1, :], row)
    return row


def live_column(valid, level, live):
    row = jnp.where(valid_row(valid, level) > 0, 1.0, 0.0)
    row = jnp.broadcast_to(row, (8, row.shape[1])).astype(BF)
    live[...] = mm_tn(row, jnp.full((8, 128), 0.125, BF))[:, 0:1]


def adapter_of(mats, vecs, which):
    vec = vecs.at[which]
    return Adapter(
        mats.at[2 * which], vec[0:1, 0:64], mats.at[2 * which + 1], vec[1:2, :], vec[2:3, :], vec[3:4, :]
    )


def portions_shape(rows, width):
    return ((width // 128, rows, 2 * rows), BF)


def attn_saved(rows, width, hidden):
    return dict(
        packed=((rows, 3 * width), BF), context=((rows, width), BF), linv=((rows, width), BF)
    )


def norm_saved(rows, width):
    return dict(
        attended=((rows, width), BF),
        act1=((rows, 64), BF),
        slope1=((rows, 64), F32),
        std1=((rows, width), BF),
        scale1=((rows, 1), F32),
    )


def ffn_saved(rows, width, hidden):
    return dict(
        slope=((rows, hidden), BF),
        returned=((rows, width), BF),
        act2=((rows, 64), BF),
        slope2=((rows, 64), F32),
        std2=((rows, width), BF),
        scale2=((rows, 1), F32),
    )


STAT_ROWS = 8


def pair_copy(source, target, sems, pair, length):
    lanes = pl.ds(0, 2 * length)
    return pltpu.make_async_copy(
        source.at[pair, :, lanes], target.at[pair, :, lanes], sems.at[pair]
    )


def first_attn_forward(section, tokens, valid, own, got, sizes, slots):
    rows, width, hidden = sizes
    pairs = width // 128
    call = Call(section, slots)
    call.load(micro=True, h=tokens)
    call.whole(valid=valid)
    call.raw(own=own.qkv, got=got.qkv, own_out=own.out, got_out=got.out)
    call.whole(own_mats=own.mats, got_mats=got.mats, own_vecs=own.vecs, got_vecs=got.vecs)
    call.save(**attn_saved(*sizes), **norm_saved(rows, width), middle=((rows, width), BF))
    shape, dtype = portions_shape(rows, width)
    call.out(portions=((slots,) + shape, dtype))
    call.blocks(stats=((2, width), F32))
    call.temp(
        held=((slots,) + shape, dtype),
        live=((rows, 1), F32),
        bias=((rows, 256), F32),
        qkv=(own.qkv.shape, BF),
        out=(own.out.shape, BF),
        mats=(own.mats.shape, BF),
        vecs=(own.vecs.shape, F32),
    )
    call.sems(qkv_sems=3, out_sems=1, pair_sems=(slots, pairs))
    call.flops = 2 * rows * width * width * 12

    def body(r):
        mine = r.section == 0
        qkv = Fill(r.own, r.got, r.qkv, r.qkv_sems, mine, 3, 2)
        out = Fill(r.own_out, r.got_out, r.out, r.out_sems, mine)

        def begin():
            r.copy("h", 0).start()
            qkv.start()
            out.start()
            for slot in range(1, slots):
                r.copy("h", slot).start()
            zero(r.stats)
            r.mats[...] = jnp.where(mine, r.own_mats[...], r.got_mats[...])
            r.vecs[...] = jnp.where(mine, r.own_vecs[...], r.got_vecs[...])

        r.at_first(begin)
        live_column(r.valid, r.level, r.live)
        r.wait("h")
        qkv_phase(r.h, r.qkv.at[0], r.packed, lambda at: at % 3 or r.at_first(lambda: qkv.wait(at // 3)))
        r.start("packed")

        def pair_copy_of(slot, pair, length):
            return pair_copy(r.held.at[slot], r.portions.at[slot], r.pair_sems.at[slot], pair, length)

        attention_forward(
            r.level, r.valid, r.bias, r.packed, r.context, r.held.at[r.step], r.linv,
            lambda pair, length: pair_copy_of(r.step, pair, length).start(),
        )
        r.start("context", "linv")
        r.at_first(out.wait)
        project(r.context, r.out.at[0], r.attended)
        saved = (r.act1, r.slope1, r.std1, r.scale1)
        adapter_norm(
            r.h, r.attended, r.live, adapter_of(r.mats, r.vecs, 0), saved, r.middle, r.stats
        )
        r.start("middle", *norm_saved(rows, width))

        def finish():
            for slot in range(slots):
                for name in ("middle", *attn_saved(*sizes), *norm_saved(rows, width)):
                    r.copy(name, slot).wait()

                def waits(length):
                    for pair in range(pairs):
                        pair_copy_of(slot, pair, length).wait()

                by_level(r.level_of(slot), waits)

        r.at_last(finish)

    return call.run(body, "first_attn")


STAGE_ATTN0, STAGE_FFN0, STAGE_ATTN1, STAGE_FFN1 = range(4)


def middle_part(section, kept, cotangent, valid, own, got, sizes, slots):
    rows, width, hidden = sizes
    call = Call(section, slots)
    row = ((rows, width), BF)
    call.raw(base=kept.middle, cotangent=cotangent, **{"far_" + n: getattr(kept, n) for n in norm_saved(rows, width)})
    call.whole(valid=valid, stats=kept.stats)
    for name in ("qkv", "out", "win", "wout", "mats", "vecs"):
        call.raw(**{"own_" + name: getattr(own, name), "got_" + name: getattr(got, name)})
    call.temp(
        qkv=(own.qkv.shape, BF),
        win=(own.win.shape, BF),
        wout=(own.wout.shape, BF),
        outs=((2,) + own.out.shape, BF),
        mats=((2,) + own.mats.shape, BF),
        vecs=((2,) + own.vecs.shape, F32),
    )
    call.sems(win_sems=4, wout_sems=1, weight_sems=(8, 1), base_sems=1, up_sems=1, norm_sems=5)
    call.save(depth=1, result=row, dfirst0=row, dcontext0=row)
    grad_shape = (4, BLOCK_ROWS, width)
    call.temp(grads=((8,) + grad_shape[1:], F32))
    call.blocks(keep=(grad_shape, BF), send=(grad_shape, BF))
    call.temp(**attn_saved(*sizes))
    call.temp(
        attended=((4,) + row[0], BF),
        act1=((4, rows, 64), BF),
        slope1=((4, rows, 64), F32),
        std1=((4,) + row[0], BF),
        scale1=((4, rows, 1), F32),
        slope=((2, rows, hidden), BF),
        chain=((3,) + row[0], BF),
        sums=((4, 2, width), F32),
        up=row,
        held=portions_shape(rows, width),
        live=((rows, 1), F32),
        bias=((rows, 256), F32),
        wide=((rows, hidden), BF),
        dsum=((rows, width), F32),
        low=row,
        dpre=((rows, 64), BF),
        dinner=row,
    )
    call.flops = 12 * rows * width * (4 * width + 2 * hidden)
    norms = tuple(norm_saved(rows, width))

    def body(r):
        first, second = r.section == 0, r.section == 1

        def fill(name, target, at, mine):
            return Fill(
                getattr(r, "own_" + name), getattr(r, "got_" + name), target, r.weight_sems.at[at], mine
            )

        qkv, out1 = fill("qkv", r.qkv, 0, second), fill("out", r.outs.at[1], 1, second)
        mats1, vecs1 = fill("mats", r.mats.at[1], 2, second), fill("vecs", r.vecs.at[1], 3, second)
        out0 = fill("out", r.outs.at[0], 4, first)
        mats0, vecs0 = fill("mats", r.mats.at[0], 5, first), fill("vecs", r.vecs.at[0], 6, first)
        win0, win1 = (Fill(r.own_win, r.got_win, r.win, r.win_sems, m, 4, 2) for m in (first, second))
        wout0, wout1 = (Fill(r.own_wout, r.got_wout, r.wout, r.wout_sems, m) for m in (first, second))

        def base_copy(slot):
            return pltpu.make_async_copy(r.base.at[slot], r.chain.at[0], r.base_sems.at[0])

        def slot_copies():
            copies = [pltpu.make_async_copy(r.cotangent.at[r.level], r.up, r.up_sems.at[0])]
            for at, name in enumerate(norms):
                copies.append(
                    pltpu.make_async_copy(
                        getattr(r, "far_" + name).at[r.step], getattr(r, name).at[0], r.norm_sems.at[at]
                    )
                )
            return copies

        def begin():
            for item in (mats0, vecs0):
                item.start()
            base_copy(0).start()
            for item in (win0, wout0, qkv, out1, mats1, vecs1, out0):
                item.start()
            zero(r.grads, r.sums)
            for item in (mats0, vecs0, win0, wout0):
                item.wait()

        def later(act):
            pl.when(r.step > 0)(act)

        r.at_first(begin)
        for item in slot_copies():
            item.start()
        live_column(r.valid, r.level, r.live)
        base_copy(r.step).wait()
        later(lambda: r.copy("result", r.step - 1).wait())

        def saved_of(stage):
            return tuple(getattr(r, n).at[stage] for n in ("act1", "slope1", "std1", "scale1"))

        def adapter_at(stage):
            return adapter_of(r.mats.at[stage // 2], r.vecs.at[stage // 2], stage % 2)

        def forward(at, carry):
            stage = at + 1
            inner = r.attended.at[stage]
            here = r.chain.at[at]

            @pl.when(at == 1)
            def _():
                win1.start()
                wout1.start()
                for item in (qkv, out1, mats1, vecs1):
                    r.at_first(item.wait)
                qkv_phase(here, r.qkv.at[0], r.packed)
                attention_forward(r.level, r.valid, r.bias, r.packed, r.context, r.held, r.linv)
                project(r.context, r.outs.at[1, 0], inner)

            @pl.when(at != 1)
            def _():
                @pl.when(at == 2)
                def _():
                    win1.wait()
                    wout1.wait()

                ffn_forward(here, r.win.at[0], r.wout.at[0], r.wide, r.slope.at[stage // 2], inner)

            def norm(target):
                adapter_norm(
                    here, inner, r.live, adapter_at(stage), saved_of(stage), target, r.sums.at[stage]
                )

            norm(r.chain.at[lax.rem(at + 1, 3)])
            return carry

        lax.fori_loop(0, 3, forward, 0)
        r.result[...] = r.chain[0]
        r.start("result")

        @pl.when(r.step + 1 < slots)
        def _():
            base_copy(r.step + 1).start()

        for item in slot_copies():
            item.wait()

        def backward(at, carry):
            stage = 3 - at
            inner = r.attended.at[stage]

            @pl.when(stage % 2 == 1)
            def _():
                r.dsum[...] = r.up[...].astype(F32)

            norm_adapter_back(
                r.dsum, saved_of(stage), inner, adapter_at(stage), r.low, r.dpre, r.dinner,
                r.grads.at[2 * stage], r.grads.at[2 * stage + 1],
            )

            @pl.when(stage % 2 == 1)
            def _():
                @pl.when(at == 2)
                def _():
                    wout0.wait()
                    win0.wait()

                ffn_backward(r.dinner, r.win.at[0], r.wout.at[0], r.slope.at[stage // 2], r.wide, r.dsum)

            @pl.when(stage % 2 == 0)
            def _():
                @pl.when(at == 3)
                def _():
                    r.at_first(out0.wait)
                    later(lambda: r.copy("dfirst0", r.step - 1).wait())

                @pl.when(at == 1)
                def _():
                    wout0.start()
                    win0.start()
                    later(lambda: r.copy("dcontext0", r.step - 1).wait())

                project_back(r.dinner, r.outs.at[stage // 2, 0], r.dcontext0)

                @pl.when(at == 1)
                def _():
                    attention_backward(
                        r.level, r.packed, r.context, r.held, r.linv, r.dcontext0, r.packed
                    )
                    input_backward(r.packed, r.qkv.at[0], r.dsum, r.up)

            return carry

        lax.fori_loop(0, 4, backward, 0)
        r.dfirst0[...] = r.dsum[...].astype(BF)
        r.start("dfirst0", "dcontext0")

        def finish():
            r.wait("result", "dfirst0", "dcontext0")
            for layer in range(2):
                attn, ffn = r.sums.at[2 * layer], r.sums.at[2 * layer + 1]
                target = r.grads.at[4 * layer + ATTN_UP]
                if layer == 0:
                    attn = r.stats
                target[STATS : STATS + 1, :] = attn[0:1, :]
                target[STATS + 1 : STATS + 3, :] = ffn[...]
                count = jnp.zeros((1, 1), F32)
                for slot in range(slots):
                    row = jnp.where(valid_row(r.valid, r.level_of(slot)) > 0, 1.0, 0.0)
                    count += jnp.sum(row, axis=1, keepdims=True)
                target[STATS + 3 : STATS + 4, :] = jnp.broadcast_to(count, (1, width))
            for block in range(4):
                r.keep[block] = r.grads[4 * r.section + block].astype(BF)
                r.send[block] = r.grads[4 - 4 * r.section + block].astype(BF)

        r.at_last(finish)

    return call.run(body, "middle_part")


def first_attn_backward(section, back, there, kept, own, got, sizes, slots):
    rows, width, hidden = sizes
    pairs = width // 128
    call = Call(section, slots)
    call.load(packed=kept.packed, dcontext=back.dcontext0, context=kept.context, linv=kept.linv)
    call.load(dfirst=back.dfirst0)
    call.raw(portions=kept.portions, own=own.qkv, got=got.qkv, here=back.result, there=there)
    call.out(input_grad=((slots, rows, width), BF), result=((2 * slots, rows, width), BF))
    shape, dtype = portions_shape(rows, width)
    call.temp(
        held=((slots,) + shape, dtype),
        qkv=(own.qkv.shape, BF),
        stage=((2 * slots, rows, width), BF),
        dentry=((slots, rows, width), BF),
    )
    call.sems(
        qkv_sems=3, pair_sems=(slots, pairs), in_sems=2 * slots, out_sems=2 * slots, grad_sems=slots
    )
    call.flops = 2 * rows * width * width * 12

    def body(r):
        fill = Fill(r.own, r.got, r.qkv, r.qkv_sems, r.section == 0, 3, 1)

        def pair_copy_of(slot, pair, length):
            return pair_copy(r.portions.at[slot], r.held.at[slot], r.pair_sems.at[slot], pair, length)

        loads = ("packed", "dcontext", "context", "linv")
        ins, outs = [], []
        for at in range(slots):
            mine, other = (jnp.where(r.section == 0, PLAN[a][at], PLAN[1 - a][at]) for a in range(2))
            for source, target in ((r.here, mine), (r.there, other)):
                n = len(ins)
                ins.append(pltpu.make_async_copy(source.at[at], r.stage.at[n], r.in_sems.at[n]))
                outs.append(
                    pltpu.make_async_copy(r.stage.at[n], r.result.at[target], r.out_sems.at[n])
                )

        def begin():
            for slot in range(slots):
                for name in loads:
                    r.copy(name, slot).start()

                def starts(length):
                    for pair in range(pairs):
                        pair_copy_of(slot, pair, length).start()

                by_level(r.level_of(slot), starts)
                if slot == 0:
                    fill.start()
                r.copy("dfirst", slot).start()
            for item in ins:
                item.start()

        def grad_copy(slot):
            target = jnp.where(r.level_of(slot) % slots == 0, 0, 1)
            return pltpu.make_async_copy(
                r.dentry.at[slot], r.input_grad.at[target], r.grad_sems.at[slot]
            )

        r.at_first(begin)
        r.wait(*loads)
        attention_backward(
            r.level, r.packed, r.context, r.held.at[r.step], r.linv, r.dcontext, r.packed,
            r.step, pair_copy_of,
        )
        r.wait("dfirst")
        r.at_first(fill.wait)
        input_backward(r.packed, r.qkv.at[0], r.dfirst, r.dentry.at[r.step])
        grad_copy(r.step).start()

        def pass_on():
            for come, go in zip(ins, outs):
                come.wait()
                go.start()

        def finish():
            for slot in range(slots):
                grad_copy(slot).wait()
            for item in outs:
                item.wait()

        r.at_first(pass_on)
        r.at_last(finish)

    return call.run(body, "attn_back")


def packed_small(mats, vecs):
    width = mats[0].shape[-1]

    def kernel(*refs):
        sources, (out_mats, out_vecs) = refs[:-2], refs[-2:]
        for at in range(4):
            out_mats[at] = sources[at][0]
        out_vecs[...] = jnp.zeros_like(out_vecs)
        for at, ref in enumerate(sources[4:]):
            out_vecs[at // 4, at % 4 : at % 4 + 1, 0 : ref.shape[1]] = ref[...]

    return pl.pallas_call(
        kernel,
        out_shape=(
            jax.ShapeDtypeStruct((4, 64, width), BF),
            jax.ShapeDtypeStruct((2, 4, width), F32),
        ),
        name="pack",
    )(*mats, *vecs)


def unpacked(part, other, upper):
    width = part.shape[-1]
    matrix = jax.ShapeDtypeStruct((1, MATRIX_ROWS, width), F32)
    vector = jax.ShapeDtypeStruct((1, width), F32)
    small = jax.ShapeDtypeStruct((1, 64), F32)
    group = (matrix, small, matrix, vector, vector, vector)

    def kernel(upper, part, other, *outs):
        def block(at):
            mine = upper[0] == (1 if at >= 2 else 0)
            return jnp.where(mine, part[at % 2], other[at % 2]).astype(F32)

        for down, up, (mat_down, down_bias, mat_up, up_bias, gain, bias) in (
            (ATTN_DOWN, ATTN_UP, outs[:6]),
            (FFN_DOWN, FFN_UP, outs[6:12]),
        ):
            down, up = block(down), block(up)
            mat_down[0] = down[:MATRIX_ROWS]
            mat_up[0] = up[:MATRIX_ROWS]
            for row, target in ((UP_BIAS, up_bias), (GAIN, gain), (BIAS, bias), (DOWN_BIAS, down_bias)):
                target[...] = down[row : row + 1, : target.shape[1]]
        sums = block(ATTN_UP)[STATS : STATS + STAT_ROWS]
        means = jnp.sum(sums, axis=1, keepdims=True) / (sums[3:4, 0:1] * width)
        lane = lax.broadcasted_iota(jnp.int32, (1, 3), 1)
        picked = jnp.where(lane == 0, means[0:1], jnp.where(lane == 1, means[1:2], means[2:3]))
        outs[12][...] = jnp.sqrt(picked)

    vmem = pl.BlockSpec(memory_space=pltpu.VMEM)
    outs = pl.pallas_call(
        kernel,
        in_specs=[pl.BlockSpec(memory_space=pltpu.SMEM), vmem, vmem],
        out_shape=group * 2 + (jax.ShapeDtypeStruct((1, 3), F32),),
        name="unpack",
    )(upper.astype(jnp.int32).reshape(1), part, other)
    outs = list(outs)
    for at in (0, 6):
        outs[at] = jnp.swapaxes(outs[at], 1, 2)
    return tuple(outs)


def swap(value):
    return lax.ppermute(value, "section", [(0, 1), (1, 0)])


def after(value, *others):
    return lax.optimization_barrier((value,) + others)[0]


def exchanged(value, first_bit, second_bit):
    count = lax.axis_size("dp")
    pairs = [
        (section * count + at, section * count + (at ^ bit))
        for section, bit in enumerate((first_bit, second_bit))
        for at in range(count)
    ]
    return lax.ppermute(value, ("section", "dp"), pairs)


def summed_halves(part):
    section, mine = lax.axis_index("section"), lax.axis_index("dp")
    count = lax.axis_size("dp")
    halvings = ((1, 2), (2, 1))

    def is_upper(pair):
        return (mine & jnp.where(section == 0, pair[0], pair[1])) > 0

    for pair in halvings:
        upper = is_upper(pair)
        half = part.shape[0] // 2
        low, high = part[:half], part[half:]
        part = jnp.where(upper, high, low) + exchanged(jnp.where(upper, low, high), *pair)
    bit = 4
    while bit < count:
        part = part + exchanged(part, bit, bit)
        bit *= 2
    other, upper = exchanged(part, *halvings[1]), is_upper(halvings[1])
    part = jnp.concatenate([jnp.where(upper, other, part), jnp.where(upper, part, other)])
    return part, exchanged(part, *halvings[0]), is_upper(halvings[0])


def body(
    tokens, valid, cotangent, qkv, out, win, wout,
    attn_down, attn_down_bias, attn_up, attn_up_bias, gain1, bias1,
    ffn_down, ffn_down_bias, ffn_up, ffn_up_bias, gain2, bias2,
):
    section = lax.axis_index("section")
    micro_count, rows, width = tokens.shape
    sizes = (rows, width, win.shape[-1])
    slots = micro_count // 2
    mats, vecs = packed_small(
        (jnp.swapaxes(attn_down, 1, 2), attn_up, jnp.swapaxes(ffn_down, 1, 2), ffn_up),
        (attn_down_bias, attn_up_bias, gain1, bias1, ffn_down_bias, ffn_up_bias, gain2, bias2),
    )
    own = Layer(qkv, out, win, wout, mats, vecs)
    early = [swap(v) for v in (qkv, out, mats, vecs)]
    got_qkv, got_out, got_mats, got_vecs = early
    got_win, got_wout = (swap(after(v, *early)) for v in (win, wout))
    got = Layer(got_qkv, got_out, got_win, got_wout, got_mats, got_vecs)
    where = section.astype(jnp.int32).reshape(1)

    kept = first_attn_forward(where, tokens, valid, own, got, sizes, slots)
    back = middle_part(where, kept, cotangent, valid, own, got, sizes, slots)
    there = swap(back.result)

    part, other, upper = summed_halves(back.keep + swap(back.send))
    last = first_attn_backward(where, back, there, kept, own, got, sizes, slots)
    small = unpacked(part, after(other, last.input_grad), upper)
    return (last.result, last.input_grad) + small


def solution(mesh):
    rows = P(None, "dp", None)
    matrix, vector = P("section", None, None), P("section", None)
    weights = (matrix, vector, matrix, vector, vector, vector)
    return jax.shard_map(
        body,
        mesh=mesh,
        in_specs=(rows, P(None, "dp"), rows) + (matrix,) * 4 + weights * 2,
        out_specs=(rows, P("section", "dp", None)) + weights * 2 + (vector,),
        check_vma=False,
    )
```

```python
import math
from types import SimpleNamespace
from typing import Any, NamedTuple

import jax
import jax.numpy as jnp
from jax import lax
from jax.experimental import pallas as pl
from jax.experimental.pallas import tpu as pltpu
from jax.sharding import PartitionSpec as P

NEGATIVE = -1e30
EPSILON = 1e-12
ROOT_HALF = 0.7071067811865476
INV_ROOT_TAU = 0.3989422804014327
LOG2E = 1.4426950408889634

PLAN = ((0, 1), (3, 2))

BF = jnp.bfloat16
F32 = jnp.float32
ANY = pl.BlockSpec(memory_space=pl.ANY)
VMEM_LIMIT = 60 << 20
SMALL_LIMIT = 16 << 20

ATTN_DOWN, ATTN_UP, FFN_DOWN, FFN_UP = range(4)
MATRIX_ROWS, BLOCK_ROWS = 64, 72
UP_BIAS, GAIN, BIAS, DOWN_BIAS = range(64, 68)
STATS = 64


class Layer(NamedTuple):
    qkv: Any
    out: Any
    win: Any
    wout: Any
    mats: Any
    vecs: Any


class Adapter(NamedTuple):
    down: Any
    down_bias: Any
    up: Any
    up_bias: Any
    gain: Any
    bias: Any


def mm(a, b):
    return jnp.dot(a, b, preferred_element_type=F32)


def mm_nt(a, b):
    return lax.dot_general(a, b, (((1,), (1,)), ((), ())), preferred_element_type=F32)


def mm_tn(a, b):
    return lax.dot_general(a, b, (((0,), (0,)), ((), ())), preferred_element_type=F32)


def span_of(index, size, base=0):
    start = index * size + base
    return pl.ds(start if isinstance(index, int) else pl.multiple_of(start, size), size)


def steps(count, body, unroll=None):
    if unroll is None or unroll >= count:
        for at in range(count):
            body(at)
        return

    def some(group, carry):
        for at in range(unroll):
            body(group * unroll + at)
        return carry

    lax.fori_loop(0, count // unroll, some, 0)


PAIRS_FORWARD, PAIRS_BACKWARD = 3, 1
FFN_FORWARD, FFN_BACKWARD = 12, 12


def gelu_both(z):
    cdf = 0.5 + 0.5 * lax.erf(z * ROOT_HALF)
    bell = jnp.exp2(z * z * (-0.5 * LOG2E))
    return z * cdf, cdf + (z * INV_ROOT_TAU) * bell


def nothing(at):
    pass


def qkv_phase(h, qkv, packed, need=nothing):
    width = h.shape[-1]

    def one(at):
        need(at)
        cols = span_of(at, 256)
        y = mm(h[...], qkv[:, cols])
        if at < width // 256:
            y = y * 0.125
        packed[:, cols] = y.astype(BF)

    steps(qkv.shape[1] // 256, one)


def lane_half(shape):
    return lax.broadcasted_iota(jnp.int32, shape, len(shape) - 1) < 64


def split_pair(pair, first):
    zero = jnp.zeros_like(pair)
    return jnp.concatenate([jnp.where(first, pair, zero), jnp.where(first, zero, pair)], axis=0)


def values_and_ones(v2, first):
    one = jnp.ones_like(v2)
    return jnp.concatenate([split_pair(v2, first), split_pair(one, first)], axis=1)


def by_level(level, run):
    @pl.when(level <= 2)
    def _():
        run(256)

    @pl.when(level == 3)
    def _():
        run(512)


def pair_ignored(pair, length):
    pass


def attention_forward(level, valid, bias, packed, context, portions, linv, done=pair_ignored):
    rows, width = context.shape
    query = 256

    def run(length):
        live = valid_row(valid, level)
        barred = jnp.where(live > 0, 0.0, NEGATIVE)
        if length == 256:
            shift = 6 + level
            a = lax.broadcasted_iota(jnp.int32, (256, 256), 0) >> shift
            b = lax.broadcasted_iota(jnp.int32, (256, 256), 1) >> shift
            apart = jnp.where(a == b, 0.0, NEGATIVE)
            for block in range(rows // 256):
                bias[span_of(block, 256), :] = apart + barred[:, block * 256 : (block + 1) * 256]
        first = lane_half((length, 128))

        def pair(at):
            lanes = span_of(at, 128)
            for block in range(rows // length):
                base = block * length
                k2 = packed[base : base + length, span_of(at, 128, width)]
                v2 = packed[base : base + length, span_of(at, 128, 2 * width)]
                kk = split_pair(k2, first)
                vv = values_and_ones(v2, first)
                for part in range(length // query):
                    at_rows = pl.ds(base + part * query, query)
                    scores = mm_nt(packed[at_rows, lanes], kk)
                    halves = []
                    for head in range(2):
                        s = scores[:, head * length : (head + 1) * length]
                        s = s + (bias[at_rows, :] if length == 256 else barred)
                        top = jnp.max(s, axis=-1, keepdims=True)
                        halves.append(jnp.exp2((s - top) * LOG2E).astype(BF))
                    p = jnp.concatenate(halves, axis=1)
                    portions[at, at_rows, 0 : 2 * length] = p
                    both = mm(p, vv)
                    inverse = 1.0 / both[:, 128:]
                    linv[at_rows, lanes] = inverse.astype(BF)
                    context[at_rows, lanes] = (both[:, :128] * inverse).astype(BF)
            done(at, length)

        steps(width // 128, pair, PAIRS_FORWARD)

    by_level(level, run)


def attention_backward(level, packed, context, portions, linv, dcontext, dpacked, slot=0, copy=None):
    rows, width = context.shape
    query = 256

    def run(length):
        first = lane_half((length, 128))

        def pair(at):
            if copy is not None:
                copy(slot, at, length).wait()
            lanes = span_of(at, 128)
            for block in range(rows // length):
                base = block * length
                whole = pl.ds(base, length)
                k2 = packed[whole, span_of(at, 128, width)]
                v2 = packed[whole, span_of(at, 128, 2 * width)]
                kk = split_pair(k2, first)
                vv = values_and_ones(v2, first)
                dk = None
                dv = None
                for part in range(length // query):
                    at_rows = pl.ds(base + part * query, query)
                    out = dcontext[at_rows, lanes].astype(F32) * linv[at_rows, lanes].astype(F32)
                    low = out.astype(BF)
                    both = jnp.concatenate(
                        [low, (-out * context[at_rows, lanes].astype(F32)).astype(BF)], axis=1
                    )
                    p = portions[at, at_rows, 0 : 2 * length]
                    ds = p * mm_nt(both, vv).astype(BF)
                    q2 = packed[at_rows, lanes]
                    dpacked[at_rows, lanes] = (mm(ds, kk) * 0.125).astype(BF)
                    more_k = mm_tn(ds, q2)
                    more_v = mm_tn(p, low)
                    dk = more_k if dk is None else dk + more_k
                    dv = more_v if dv is None else dv + more_v
                dk = jnp.where(first, dk[:length], dk[length:])
                dv = jnp.where(first, dv[:length], dv[length:])
                dpacked[whole, span_of(at, 128, width)] = dk.astype(BF)
                dpacked[whole, span_of(at, 128, 2 * width)] = dv.astype(BF)

        steps(width // 128, pair, PAIRS_BACKWARD)

    by_level(level, run)


def project(x, weight, out):
    def one(at):
        cols = span_of(at, 256)
        out[:, cols] = mm(x[...], weight[:, cols]).astype(BF)

    steps(out.shape[1] // 256, one)


def project_back(x, weight, out):
    def one(at):
        cols = span_of(at, 256)
        out[:, cols] = mm_nt(x[...], weight[cols, :]).astype(BF)

    steps(out.shape[1] // 256, one)


def adapter_norm(base, inner, live, w, saved, out, stats):
    act, slope, std, scale = saved
    rows, width = inner.shape
    block = 128

    def one(at):
        r = span_of(at, block)
        x = inner[r, :]
        pre = mm_nt(x, w.down[...]) + w.down_bias
        a, g = gelu_both(pre)
        a = a.astype(BF)
        act[r, :] = a
        slope[r, :] = g
        branch = x.astype(F32) + (mm(a, w.up[...]) + w.up_bias)
        total = base[r, :].astype(F32) + branch
        alive = live[r, :]
        stats[0:1, :] += jnp.sum(branch * branch * alive, axis=0, keepdims=True)
        mean = jnp.mean(total, axis=-1, keepdims=True)
        centered = total - mean
        variance = jnp.mean(centered * centered, axis=-1, keepdims=True)
        square = jnp.sum((variance + mean * mean) * alive, axis=0, keepdims=True)
        stats[1:2, :] += jnp.broadcast_to(square, (1, width))
        s = lax.rsqrt(variance + EPSILON)
        n = centered * s
        std[r, :] = n.astype(BF)
        scale[r, :] = s
        out[r, :] = (n * w.gain + w.bias).astype(BF)

    steps(rows // block, one)


def ffn_forward(middle, win, wout, act, slope, returned, need=nothing):
    need(0)
    expand(middle, win, act, slope)
    need(1)
    project(act, wout, returned)


def expand(middle, win, act, slope):

    def one(at):
        cols = span_of(at, 256)
        z = mm(middle[...], win[:, cols])
        a, g = gelu_both(z)
        act[:, cols] = a.astype(BF)
        slope[:, cols] = g.astype(BF)

    steps(win.shape[1] // 256, one, FFN_FORWARD)


def norm_adapter_back(dtotal, saved, inner, w, low, dpre_all, dinner, grads_down, grads_up):
    act, slope, std, scale = saved
    rows = inner.shape[0]
    block = 128

    def add(row, values):
        grads_down[row : row + 1, 0 : values.shape[1]] += jnp.sum(values, axis=0, keepdims=True)

    def one(at):
        r = span_of(at, block)
        g = dtotal[r, :]
        n = std[r, :].astype(F32)
        add(GAIN, g * n)
        add(BIAS, g)
        gg = g * w.gain
        m1 = jnp.mean(gg, axis=-1, keepdims=True)
        m2 = jnp.mean(gg * n, axis=-1, keepdims=True)
        d = scale[r, :] * (gg - m1 - n * m2)
        dtotal[r, :] = d
        e = d.astype(BF)
        low[r, :] = e
        e32 = e.astype(F32)
        add(UP_BIAS, e32)
        dpre = (mm_nt(e, w.up[...]) * slope[r, :]).astype(BF)
        dpre_all[r, :] = dpre
        add(DOWN_BIAS, dpre.astype(F32))
        dinner[r, :] = (e32 + mm(dpre, w.down[...])).astype(BF)

    steps(rows // block, one)
    grads_up[0:MATRIX_ROWS, :] += mm_tn(act[...], low[...])
    grads_down[0:MATRIX_ROWS, :] += mm_tn(dpre_all[...], inner[...])


def ffn_backward(dreturned, win, wout, slope, dexp, dsecond):
    expand_back(dreturned, wout, slope, dexp)
    project_add(dexp, win, dsecond)


def expand_back(dreturned, wout, slope, dexp):
    def one(at):
        cols = span_of(at, 256)
        d = mm_nt(dreturned[...], wout[cols, :])
        dexp[:, cols] = d.astype(BF) * slope[:, cols]

    steps(wout.shape[0] // 256, one, FFN_BACKWARD)


def project_add(x, weight, out):
    def one(at):
        cols = span_of(at, 256)
        out[:, cols] += mm_nt(x[...], weight[cols, :])

    steps(weight.shape[0] // 256, one)


def input_backward(dpacked, qkv, dfirst, dentry):
    def one(at):
        cols = span_of(at, 256)
        d = mm_nt(dpacked[...], qkv[cols, :])
        dentry[:, cols] = (dfirst[:, cols].astype(F32) + d).astype(BF)

    steps(qkv.shape[0] // 256, one)


class Item(NamedTuple):
    make: Any
    ref: Any

    def start(self):
        self.make().start()

    def wait(self):
        self.make().wait()


class Call:
    def __init__(self, section, slots, base=0):
        self.slots, self.base = slots, base
        self.args, self.in_specs, self.in_names = [], [], []
        self.outs, self.out_specs, self.out_names = [], [], []
        self.scratch, self.scratch_names = [], []
        self.kinds = {}
        self.section = section
        self.flops = 0
        self.limit = VMEM_LIMIT

    def _add(self, name, array, spec):
        self.args.append(array)
        self.in_specs.append(spec)
        self.in_names.append(name)

    def _temp(self, name, shape):
        self.scratch.append(shape)
        self.scratch_names.append(name)

    def whole(self, **arrays):
        for name, array in arrays.items():
            zeros = (0,) * array.ndim
            self._add(name, array, pl.BlockSpec(array.shape, lambda i, s, zeros=zeros: zeros))

    def raw(self, **arrays):
        for name, array in arrays.items():
            self._add(name, array, ANY)

    def load(self, micro=False, depth=2, **arrays):
        for name, array in arrays.items():
            depth_of = min(depth, self.slots)
            self._add((name, 0), array, ANY)
            self._temp((name, 1), pltpu.VMEM((depth_of,) + array.shape[1:], array.dtype))
            self._temp((name, 2), pltpu.SemaphoreType.DMA((depth_of,)))
            self.kinds[name] = (0, depth_of, micro)

    def save(self, depth=2, **shapes):
        for name, (shape, dtype) in shapes.items():
            depth_of = min(depth, self.slots)
            self.outs.append(jax.ShapeDtypeStruct((self.slots,) + shape, dtype))
            self.out_specs.append(ANY)
            self.out_names.append((name, 0))
            self._temp((name, 1), pltpu.VMEM((depth_of,) + shape, dtype))
            self._temp((name, 2), pltpu.SemaphoreType.DMA((depth_of,)))
            self.kinds[name] = (1, depth_of, False)

    def out(self, **shapes):
        for name, (shape, dtype) in shapes.items():
            self.outs.append(jax.ShapeDtypeStruct(shape, dtype))
            self.out_specs.append(ANY)
            self.out_names.append(name)

    def blocks(self, **shapes):
        for name, (shape, dtype) in shapes.items():
            zeros = (0,) * len(shape)
            self.outs.append(jax.ShapeDtypeStruct(shape, dtype))
            self.out_specs.append(pl.BlockSpec(shape, lambda i, s, zeros=zeros: zeros))
            self.out_names.append(name)

    def temp(self, **shapes):
        for name, (shape, dtype) in shapes.items():
            self._temp(name, pltpu.VMEM(shape, dtype))

    def sems(self, **counts):
        for name, count in counts.items():
            self._temp(name, pltpu.SemaphoreType.DMA(count if isinstance(count, tuple) else (count,)))

    def run(self, body, name):
        names = self.in_names + self.out_names + self.scratch_names
        slots, base = self.slots, self.base

        def kernel(section, *refs):
            step = pl.program_id(0) if slots > 1 else 0
            ref = dict(zip(names, refs))
            r = SimpleNamespace(**{n: v for n, v in ref.items() if isinstance(n, str)})
            r.step, r.section = step, section[0]

            def level_in(which, slot):
                number = PLAN[which][base]
                for other in range(1, slots):
                    number = jnp.where(slot == other, PLAN[which][base + other], number)
                return number

            def level(slot):
                return jnp.where(r.section == 0, level_in(0, slot), level_in(1, slot))

            def copy(name, slot):
                kind, depth, micro = self.kinds[name]
                at = slot if depth > 1 else 0
                near = ref[name, 1].at[at]
                if kind == 0:
                    far = ref[name, 0].at[level(slot) if micro else base + slot]
                    pair = (far, near)
                else:
                    pair = (near, ref[name, 0].at[slot])
                return Item(lambda: pltpu.make_async_copy(*pair, ref[name, 2].at[at]), near)

            def start(*which):
                for n in which:
                    copy(n, step).start()

            def wait(*which):
                for n in which:
                    copy(n, step).wait()

            def at_first(act):
                if slots > 1:
                    pl.when(step == 0)(act)
                else:
                    act()

            def at_last(act):
                if slots > 1:
                    pl.when(step == slots - 1)(act)
                else:
                    act()

            r.level_of, r.level = level, level(step)
            r.copy, r.start, r.wait, r.at_first, r.at_last = copy, start, wait, at_first, at_last
            for n, (kind, depth, micro) in self.kinds.items():
                setattr(r, n, ref[n, 1].at[step if depth > 1 else 0])
                setattr(r, "all_" + n, (ref[n, 0], ref[n, 1]))
            body(r)

        results = pl.pallas_call(
            kernel,
            out_shape=self.outs,
            grid_spec=pltpu.PrefetchScalarGridSpec(
                num_scalar_prefetch=1,
                grid=(slots,),
                in_specs=self.in_specs,
                out_specs=self.out_specs,
                scratch_shapes=self.scratch,
            ),
            compiler_params=pltpu.CompilerParams(vmem_limit_bytes=self.limit),
            cost_estimate=pl.CostEstimate(
                flops=self.flops * slots, bytes_accessed=1 << 20, transcendentals=0
            ),
            name=name,
        )(self.section, *self.args)
        return SimpleNamespace(
            **{n[0] if isinstance(n, tuple) else n: v for n, v in zip(self.out_names, results)}
        )


class Fill:
    def __init__(self, own, got, target, sems, mine, pieces=1, dim=0):
        self.sources, self.target, self.sems, self.mine = (own, got), target, sems, mine
        self.pieces, self.dim = pieces, dim

    def _copy(self, source, piece):
        source = self.sources[source]
        if self.pieces == 1:
            return pltpu.make_async_copy(source, self.target, self.sems.at[0])
        size = self.target.shape[self.dim] // self.pieces
        cut = tuple(
            pl.ds(piece * size, size) if at == self.dim else slice(None)
            for at in range(len(self.target.shape))
        )
        return pltpu.make_async_copy(source.at[cut], self.target.at[cut], self.sems.at[piece])

    def start(self):
        for source, chosen_one in enumerate((self.mine, jnp.logical_not(self.mine))):

            @pl.when(chosen_one)
            def _():
                for piece in range(self.pieces):
                    self._copy(source, piece).start()

    def wait(self, piece=None):
        for at in range(self.pieces) if piece is None else (piece,):
            self._copy(0, at).wait()


def zero(*refs):
    for ref in refs:
        ref[...] = jnp.zeros_like(ref)


def valid_row(valid, level):
    row = valid[0:1, :]
    for other in range(1, valid.shape[0]):
        row = jnp.where(level == other, valid[other : other + 1, :], row)
    return row


def live_column(valid, level, live):
    row = jnp.where(valid_row(valid, level) > 0, 1.0, 0.0)
    row = jnp.broadcast_to(row, (8, row.shape[1])).astype(BF)
    live[...] = mm_tn(row, jnp.full((8, 128), 0.125, BF))[:, 0:1]


def adapter_of(mats, vecs, which):
    vec = vecs.at[which]
    return Adapter(
        mats.at[2 * which], vec[0:1, 0:64], mats.at[2 * which + 1], vec[1:2, :], vec[2:3, :], vec[3:4, :]
    )


def portions_shape(rows, width):
    return ((width // 128, rows, 2 * rows), BF)


def attn_saved(rows, width, hidden):
    return dict(
        packed=((rows, 3 * width), BF), context=((rows, width), BF), linv=((rows, width), BF)
    )


def norm_saved(rows, width):
    return dict(
        attended=((rows, width), BF),
        act1=((rows, 64), BF),
        slope1=((rows, 64), F32),
        std1=((rows, width), BF),
        scale1=((rows, 1), F32),
    )


def ffn_saved(rows, width, hidden):
    return dict(
        slope=((rows, hidden), BF),
        returned=((rows, width), BF),
        act2=((rows, 64), BF),
        slope2=((rows, 64), F32),
        std2=((rows, width), BF),
        scale2=((rows, 1), F32),
    )


STAT_ROWS = 8


def pair_copy(source, target, sems, pair, length):
    lanes = pl.ds(0, 2 * length)
    return pltpu.make_async_copy(
        source.at[pair, :, lanes], target.at[pair, :, lanes], sems.at[pair]
    )


def first_attn_forward(section, tokens, valid, own, got, sizes, slots):
    rows, width, hidden = sizes
    pairs = width // 128
    call = Call(section, slots)
    call.load(micro=True, h=tokens)
    call.whole(valid=valid)
    call.raw(own=own.qkv, got=got.qkv, own_out=own.out, got_out=got.out)
    call.raw(own_mats=own.mats, got_mats=got.mats, own_vecs=own.vecs, got_vecs=got.vecs)
    call.save(**attn_saved(*sizes), **norm_saved(rows, width), middle=((rows, width), BF))
    shape, dtype = portions_shape(rows, width)
    call.out(portions=((slots,) + shape, dtype))
    call.blocks(stats=((2, width), F32))
    call.temp(
        held=((slots,) + shape, dtype),
        live=((rows, 1), F32),
        bias=((rows, 256), F32),
        qkv=(own.qkv.shape, BF),
        out=(own.out.shape, BF),
        mats=(own.mats.shape, BF),
        vecs=(own.vecs.shape, F32),
    )
    call.sems(qkv_sems=3, out_sems=1, mats_sems=1, vecs_sems=1, pair_sems=(slots, pairs))
    call.flops = 2 * rows * width * width * 12

    def body(r):
        mine = r.section == 0
        qkv = Fill(r.own, r.got, r.qkv, r.qkv_sems, mine, 3, 2)
        out = Fill(r.own_out, r.got_out, r.out, r.out_sems, mine)
        mats = Fill(r.own_mats, r.got_mats, r.mats, r.mats_sems, mine)
        vecs = Fill(r.own_vecs, r.got_vecs, r.vecs, r.vecs_sems, mine)

        def begin():
            r.copy("h", 0).start()
            for item in (qkv, out, mats, vecs):
                item.start()
            for slot in range(1, slots):
                r.copy("h", slot).start()
            zero(r.stats)

        r.at_first(begin)
        live_column(r.valid, r.level, r.live)
        r.wait("h")
        qkv_phase(r.h, r.qkv.at[0], r.packed, lambda at: at % 3 or r.at_first(lambda: qkv.wait(at // 3)))
        r.start("packed")

        def pair_copy_of(slot, pair, length):
            return pair_copy(r.held.at[slot], r.portions.at[slot], r.pair_sems.at[slot], pair, length)

        attention_forward(
            r.level, r.valid, r.bias, r.packed, r.context, r.held.at[r.step], r.linv,
            lambda pair, length: pair_copy_of(r.step, pair, length).start(),
        )
        r.start("context", "linv")
        r.at_first(lambda: [item.wait() for item in (out, mats, vecs)] and None)
        project(r.context, r.out.at[0], r.attended)
        saved = (r.act1, r.slope1, r.std1, r.scale1)
        adapter_norm(
            r.h, r.attended, r.live, adapter_of(r.mats, r.vecs, 0), saved, r.middle, r.stats
        )
        r.start("middle", *norm_saved(rows, width))

        def finish():
            for slot in range(slots):
                for name in ("middle", *attn_saved(*sizes), *norm_saved(rows, width)):
                    r.copy(name, slot).wait()

                def waits(length):
                    for pair in range(pairs):
                        pair_copy_of(slot, pair, length).wait()

                by_level(r.level_of(slot), waits)

        r.at_last(finish)

    return call.run(body, "first_attn")


STAGE_ATTN0, STAGE_FFN0, STAGE_ATTN1, STAGE_FFN1 = range(4)


def middle_part(section, kept, cotangent, valid, own, got, sizes, slots):
    rows, width, hidden = sizes
    call = Call(section, slots)
    row = ((rows, width), BF)
    call.raw(base=kept.middle, cotangent=cotangent, **{"far_" + n: getattr(kept, n) for n in norm_saved(rows, width)})
    call.whole(valid=valid, stats=kept.stats)
    for name in ("qkv", "out", "win", "wout", "mats", "vecs"):
        call.raw(**{"own_" + name: getattr(own, name), "got_" + name: getattr(got, name)})
    call.temp(
        qkv=(own.qkv.shape, BF),
        win=(own.win.shape, BF),
        wout=(own.wout.shape, BF),
        outs=((2,) + own.out.shape, BF),
        mats=((2,) + own.mats.shape, BF),
        vecs=((2,) + own.vecs.shape, F32),
    )
    call.sems(win_sems=4, wout_sems=1, weight_sems=(8, 1), base_sems=1, up_sems=1, norm_sems=5)
    call.save(depth=1, result=row, dfirst0=row, dcontext0=row)
    grad_shape = (4, BLOCK_ROWS, width)
    call.temp(grads=((8,) + grad_shape[1:], F32))
    call.blocks(keep=(grad_shape, BF), send=(grad_shape, BF))
    call.temp(**attn_saved(*sizes))
    call.temp(
        attended=((4,) + row[0], BF),
        act1=((4, rows, 64), BF),
        slope1=((4, rows, 64), F32),
        std1=((4,) + row[0], BF),
        scale1=((4, rows, 1), F32),
        slope=((2, rows, hidden), BF),
        chain=((3,) + row[0], BF),
        sums=((4, 2, width), F32),
        up=row,
        held=portions_shape(rows, width),
        live=((rows, 1), F32),
        bias=((rows, 256), F32),
        wide=((rows, hidden), BF),
        dsum=((rows, width), F32),
        low=row,
        dpre=((rows, 64), BF),
        dinner=row,
    )
    call.flops = 12 * rows * width * (4 * width + 2 * hidden)
    norms = tuple(norm_saved(rows, width))

    def body(r):
        first, second = r.section == 0, r.section == 1

        def fill(name, target, at, mine):
            return Fill(
                getattr(r, "own_" + name), getattr(r, "got_" + name), target, r.weight_sems.at[at], mine
            )

        qkv, out1 = fill("qkv", r.qkv, 0, second), fill("out", r.outs.at[1], 1, second)
        mats1, vecs1 = fill("mats", r.mats.at[1], 2, second), fill("vecs", r.vecs.at[1], 3, second)
        out0 = fill("out", r.outs.at[0], 4, first)
        mats0, vecs0 = fill("mats", r.mats.at[0], 5, first), fill("vecs", r.vecs.at[0], 6, first)
        win0, win1 = (Fill(r.own_win, r.got_win, r.win, r.win_sems, m, 4, 2) for m in (first, second))
        wout0, wout1 = (Fill(r.own_wout, r.got_wout, r.wout, r.wout_sems, m) for m in (first, second))

        def base_copy(slot):
            return pltpu.make_async_copy(r.base.at[slot], r.chain.at[0], r.base_sems.at[0])

        def slot_copies():
            copies = [pltpu.make_async_copy(r.cotangent.at[r.level], r.up, r.up_sems.at[0])]
            for at, name in enumerate(norms):
                copies.append(
                    pltpu.make_async_copy(
                        getattr(r, "far_" + name).at[r.step], getattr(r, name).at[0], r.norm_sems.at[at]
                    )
                )
            return copies

        def begin():
            for item in (mats0, vecs0):
                item.start()
            base_copy(0).start()
            for item in (win0, wout0, qkv, out1, mats1, vecs1, out0):
                item.start()
            zero(r.grads, r.sums)
            for item in (mats0, vecs0, win0, wout0):
                item.wait()

        def later(act):
            pl.when(r.step > 0)(act)

        r.at_first(begin)
        for item in slot_copies():
            item.start()
        live_column(r.valid, r.level, r.live)
        base_copy(r.step).wait()
        later(lambda: r.copy("result", r.step - 1).wait())

        def saved_of(stage):
            return tuple(getattr(r, n).at[stage] for n in ("act1", "slope1", "std1", "scale1"))

        def adapter_at(stage):
            return adapter_of(r.mats.at[stage // 2], r.vecs.at[stage // 2], stage % 2)

        def forward(at, carry):
            stage = at + 1
            inner = r.attended.at[stage]
            here = r.chain.at[at]

            @pl.when(at == 1)
            def _():
                win1.start()
                wout1.start()
                for item in (qkv, out1, mats1, vecs1):
                    r.at_first(item.wait)
                qkv_phase(here, r.qkv.at[0], r.packed)
                attention_forward(r.level, r.valid, r.bias, r.packed, r.context, r.held, r.linv)
                project(r.context, r.outs.at[1, 0], inner)

            @pl.when(at != 1)
            def _():
                @pl.when(at == 2)
                def _():
                    win1.wait()
                    wout1.wait()

                ffn_forward(here, r.win.at[0], r.wout.at[0], r.wide, r.slope.at[stage // 2], inner)

            def norm(target):
                adapter_norm(
                    here, inner, r.live, adapter_at(stage), saved_of(stage), target, r.sums.at[stage]
                )

            norm(r.chain.at[lax.rem(at + 1, 3)])
            return carry

        lax.fori_loop(0, 3, forward, 0)
        r.result[...] = r.chain[0]
        r.start("result")

        @pl.when(r.step + 1 < slots)
        def _():
            base_copy(r.step + 1).start()

        for item in slot_copies():
            item.wait()

        def backward(at, carry):
            stage = 3 - at
            inner = r.attended.at[stage]

            @pl.when(stage % 2 == 1)
            def _():
                r.dsum[...] = r.up[...].astype(F32)

            norm_adapter_back(
                r.dsum, saved_of(stage), inner, adapter_at(stage), r.low, r.dpre, r.dinner,
                r.grads.at[2 * stage], r.grads.at[2 * stage + 1],
            )

            @pl.when(stage % 2 == 1)
            def _():
                @pl.when(at == 2)
                def _():
                    wout0.wait()
                    win0.wait()

                ffn_backward(r.dinner, r.win.at[0], r.wout.at[0], r.slope.at[stage // 2], r.wide, r.dsum)

            @pl.when(stage % 2 == 0)
            def _():
                @pl.when(at == 3)
                def _():
                    r.at_first(out0.wait)
                    later(lambda: r.copy("dfirst0", r.step - 1).wait())

                @pl.when(at == 1)
                def _():
                    wout0.start()
                    win0.start()
                    later(lambda: r.copy("dcontext0", r.step - 1).wait())

                project_back(r.dinner, r.outs.at[stage // 2, 0], r.dcontext0)

                @pl.when(at == 1)
                def _():
                    attention_backward(
                        r.level, r.packed, r.context, r.held, r.linv, r.dcontext0, r.packed
                    )
                    input_backward(r.packed, r.qkv.at[0], r.dsum, r.up)

            return carry

        lax.fori_loop(0, 4, backward, 0)
        r.dfirst0[...] = r.dsum[...].astype(BF)
        r.start("dfirst0", "dcontext0")

        def finish():
            r.wait("result", "dfirst0", "dcontext0")
            for layer in range(2):
                attn, ffn = r.sums.at[2 * layer], r.sums.at[2 * layer + 1]
                target = r.grads.at[4 * layer + ATTN_UP]
                if layer == 0:
                    attn = r.stats
                target[STATS : STATS + 1, :] = attn[0:1, :]
                target[STATS + 1 : STATS + 3, :] = ffn[...]
                count = jnp.zeros((1, 1), F32)
                for slot in range(slots):
                    row = jnp.where(valid_row(r.valid, r.level_of(slot)) > 0, 1.0, 0.0)
                    count += jnp.sum(row, axis=1, keepdims=True)
                target[STATS + 3 : STATS + 4, :] = jnp.broadcast_to(count, (1, width))
            for block in range(4):
                r.keep[block] = r.grads[4 * r.section + block].astype(BF)
                r.send[block] = r.grads[4 - 4 * r.section + block].astype(BF)

        r.at_last(finish)

    return call.run(body, "middle_part")


def first_attn_backward(section, back, there, kept, own, got, sizes, slots):
    rows, width, hidden = sizes
    pairs = width // 128
    call = Call(section, slots)
    call.load(packed=kept.packed, dcontext=back.dcontext0, context=kept.context, linv=kept.linv)
    call.load(dfirst=back.dfirst0)
    call.raw(portions=kept.portions, own=own.qkv, got=got.qkv, here=back.result, there=there)
    call.out(input_grad=((slots, rows, width), BF), result=((2 * slots, rows, width), BF))
    shape, dtype = portions_shape(rows, width)
    call.temp(
        held=((slots,) + shape, dtype),
        qkv=(own.qkv.shape, BF),
        stage=((2 * slots, rows, width), BF),
        dentry=((slots, rows, width), BF),
    )
    call.sems(
        qkv_sems=3, pair_sems=(slots, pairs), in_sems=2 * slots, out_sems=2 * slots, grad_sems=slots
    )
    call.flops = 2 * rows * width * width * 12

    def body(r):
        fill = Fill(r.own, r.got, r.qkv, r.qkv_sems, r.section == 0, 3, 1)

        def pair_copy_of(slot, pair, length):
            return pair_copy(r.portions.at[slot], r.held.at[slot], r.pair_sems.at[slot], pair, length)

        loads = ("packed", "dcontext", "context", "linv")
        ins, outs = [], []
        for at in range(slots):
            mine, other = (jnp.where(r.section == 0, PLAN[a][at], PLAN[1 - a][at]) for a in range(2))
            for source, target in ((r.here, mine), (r.there, other)):
                n = len(ins)
                ins.append(pltpu.make_async_copy(source.at[at], r.stage.at[n], r.in_sems.at[n]))
                outs.append(
                    pltpu.make_async_copy(r.stage.at[n], r.result.at[target], r.out_sems.at[n])
                )

        def begin():
            for slot in range(slots):
                for name in loads:
                    r.copy(name, slot).start()

                def starts(length):
                    for pair in range(pairs):
                        pair_copy_of(slot, pair, length).start()

                by_level(r.level_of(slot), starts)
                if slot == 0:
                    fill.start()
                r.copy("dfirst", slot).start()
            for item in ins:
                item.start()

        def grad_copy(slot):
            target = jnp.where(r.level_of(slot) % slots == 0, 0, 1)
            return pltpu.make_async_copy(
                r.dentry.at[slot], r.input_grad.at[target], r.grad_sems.at[slot]
            )

        r.at_first(begin)
        r.wait(*loads)
        attention_backward(
            r.level, r.packed, r.context, r.held.at[r.step], r.linv, r.dcontext, r.packed,
            r.step, pair_copy_of,
        )
        r.wait("dfirst")
        r.at_first(fill.wait)
        input_backward(r.packed, r.qkv.at[0], r.dfirst, r.dentry.at[r.step])
        grad_copy(r.step).start()

        def pass_on():
            for come, go in zip(ins, outs):
                come.wait()
                go.start()

        def finish():
            for slot in range(slots):
                grad_copy(slot).wait()
            for item in outs:
                item.wait()

        r.at_first(pass_on)
        r.at_last(finish)

    return call.run(body, "attn_back")


def packed_small(mats, vecs):
    width = mats[0].shape[-1]

    def kernel(*refs):
        sources, (out_mats, out_vecs) = refs[:-2], refs[-2:]
        for at in range(4):
            out_mats[at] = sources[at][0]
        out_vecs[...] = jnp.zeros_like(out_vecs)
        for at, ref in enumerate(sources[4:]):
            out_vecs[at // 4, at % 4 : at % 4 + 1, 0 : ref.shape[1]] = ref[...]

    return pl.pallas_call(
        kernel,
        out_shape=(
            jax.ShapeDtypeStruct((4, 64, width), BF),
            jax.ShapeDtypeStruct((2, 4, width), F32),
        ),
        name="pack",
    )(*mats, *vecs)


def unpacked(quarters, member):
    width = quarters[0].shape[-1]
    matrix = jax.ShapeDtypeStruct((1, MATRIX_ROWS, width), F32)
    vector = jax.ShapeDtypeStruct((1, width), F32)
    small = jax.ShapeDtypeStruct((1, 64), F32)
    group = (matrix, small, matrix, vector, vector, vector)

    def kernel(member, *refs):
        sources, outs = refs[:4], refs[4:]

        def block(at):
            picked = sources[0][...]
            for d in (1, 2, 3):
                picked = jnp.where((member[0] ^ at) == d, sources[d][...], picked)
            return picked.astype(F32)

        for down, up, (mat_down, down_bias, mat_up, up_bias, gain, bias) in (
            (ATTN_DOWN, ATTN_UP, outs[:6]),
            (FFN_DOWN, FFN_UP, outs[6:12]),
        ):
            down, up = block(down), block(up)
            mat_down[0] = down[:MATRIX_ROWS]
            mat_up[0] = up[:MATRIX_ROWS]
            for row, target in ((UP_BIAS, up_bias), (GAIN, gain), (BIAS, bias), (DOWN_BIAS, down_bias)):
                target[...] = down[row : row + 1, : target.shape[1]]
        sums = block(ATTN_UP)[STATS : STATS + STAT_ROWS]
        means = jnp.sum(sums, axis=1, keepdims=True) / (sums[3:4, 0:1] * width)
        lane = lax.broadcasted_iota(jnp.int32, (1, 3), 1)
        picked = jnp.where(lane == 0, means[0:1], jnp.where(lane == 1, means[1:2], means[2:3]))
        outs[12][...] = jnp.sqrt(picked)

    vmem = pl.BlockSpec(memory_space=pltpu.VMEM)
    outs = pl.pallas_call(
        kernel,
        in_specs=[pl.BlockSpec(memory_space=pltpu.SMEM)] + [vmem] * 4,
        out_shape=group * 2 + (jax.ShapeDtypeStruct((1, 3), F32),),
        compiler_params=pltpu.CompilerParams(vmem_limit_bytes=SMALL_LIMIT),
        name="unpack",
    )(member.astype(jnp.int32).reshape(1), *quarters)
    outs = list(outs)
    for at in (0, 6):
        outs[at] = jnp.swapaxes(outs[at], 1, 2)
    return tuple(outs)


def swap(value):
    return lax.ppermute(value, "section", [(0, 1), (1, 0)])


def after(value, *others):
    return lax.optimization_barrier((value,) + others)[0]


def exchanged(value, bits):
    count = lax.axis_size("dp")
    return lax.ppermute(value, "dp", [(at, at ^ bits) for at in range(count)])


def summed_quarters(part):
    mine, count = lax.axis_index("dp"), lax.axis_size("dp")
    member = mine & 3

    def quarter(d):
        return lax.dynamic_index_in_dim(part, member ^ d, 0, keepdims=False)

    def together(own, a, b, c):
        own, a, b, c = (v.astype(F32) for v in (own, a, b, c))
        return ((own + a) + (b + c)).astype(BF)

    total = together(quarter(0), *(exchanged(quarter(d), d) for d in (1, 2, 3)))
    bit = 4
    while bit < count:
        total = total + exchanged(total, bit)
        bit *= 2
    return [total] + [exchanged(total, d) for d in (1, 2, 3)], member


def body(
    tokens, valid, cotangent, qkv, out, win, wout,
    attn_down, attn_down_bias, attn_up, attn_up_bias, gain1, bias1,
    ffn_down, ffn_down_bias, ffn_up, ffn_up_bias, gain2, bias2,
):
    section = lax.axis_index("section")
    micro_count, rows, width = tokens.shape
    sizes = (rows, width, win.shape[-1])
    slots = micro_count // 2
    mats, vecs = packed_small(
        (jnp.swapaxes(attn_down, 1, 2), attn_up, jnp.swapaxes(ffn_down, 1, 2), ffn_up),
        (attn_down_bias, attn_up_bias, gain1, bias1, ffn_down_bias, ffn_up_bias, gain2, bias2),
    )
    own = Layer(qkv, out, win, wout, mats, vecs)
    early = [swap(v) for v in (qkv, out, mats, vecs)]
    got_qkv, got_out, got_mats, got_vecs = early
    got_win, got_wout = (swap(after(v, *early)) for v in (win, wout))
    got = Layer(got_qkv, got_out, got_win, got_wout, got_mats, got_vecs)
    where = section.astype(jnp.int32).reshape(1)

    kept = first_attn_forward(where, tokens, valid, own, got, sizes, slots)
    back = middle_part(where, kept, cotangent, valid, own, got, sizes, slots)
    there = swap(back.result)

    quarters, member = summed_quarters(back.keep + swap(back.send))
    last = first_attn_backward(where, back, there, kept, own, got, sizes, slots)
    small = unpacked([quarters[0]] + [after(v, last.input_grad) for v in quarters[1:]], member)
    return (last.result, last.input_grad) + small


def solution(mesh):
    rows = P(None, "dp", None)
    matrix, vector = P("section", None, None), P("section", None)
    weights = (matrix, vector, matrix, vector, vector, vector)
    return jax.shard_map(
        body,
        mesh=mesh,
        in_specs=(rows, P(None, "dp"), rows) + (matrix,) * 4 + weights * 2,
        out_specs=(rows, P("section", "dp", None)) + weights * 2 + (vector,),
        check_vma=False,
    )
```

```python
import math
from types import SimpleNamespace
from typing import Any, NamedTuple

import jax
import jax.numpy as jnp
from jax import lax
from jax.experimental import pallas as pl
from jax.experimental.pallas import tpu as pltpu
from jax.sharding import PartitionSpec as P

NEGATIVE = -1e30
EPSILON = 1e-12
ROOT_HALF = 0.7071067811865476
INV_ROOT_TAU = 0.3989422804014327
LOG2E = 1.4426950408889634

PLAN = ((0, 1), (3, 2))

BF = jnp.bfloat16
F32 = jnp.float32
ANY = pl.BlockSpec(memory_space=pl.ANY)
VMEM_LIMIT = 60 << 20
SMALL_LIMIT = 16 << 20

ATTN_DOWN, ATTN_UP, FFN_DOWN, FFN_UP = range(4)
MATRIX_ROWS, BLOCK_ROWS = 64, 72
UP_BIAS, GAIN, BIAS, DOWN_BIAS = range(64, 68)
STATS = 64


class Layer(NamedTuple):
    qkv: Any
    out: Any
    win: Any
    wout: Any
    mats: Any
    vecs: Any


class Adapter(NamedTuple):
    down: Any
    down_bias: Any
    up: Any
    up_bias: Any
    gain: Any
    bias: Any


def mm(a, b):
    return jnp.dot(a, b, preferred_element_type=F32)


def mm_nt(a, b):
    return lax.dot_general(a, b, (((1,), (1,)), ((), ())), preferred_element_type=F32)


def mm_tn(a, b):
    return lax.dot_general(a, b, (((0,), (0,)), ((), ())), preferred_element_type=F32)


def span_of(index, size, base=0):
    start = index * size + base
    return pl.ds(start if isinstance(index, int) else pl.multiple_of(start, size), size)


def steps(count, body, unroll=None):
    if unroll is None or unroll >= count:
        for at in range(count):
            body(at)
        return

    def some(group, carry):
        for at in range(unroll):
            body(group * unroll + at)
        return carry

    lax.fori_loop(0, count // unroll, some, 0)


PAIRS_FORWARD, PAIRS_BACKWARD = 3, 1
FFN_FORWARD, FFN_BACKWARD = 12, 12


def gelu_both(z):
    cdf = 0.5 + 0.5 * lax.erf(z * ROOT_HALF)
    bell = jnp.exp2(z * z * (-0.5 * LOG2E))
    return z * cdf, cdf + (z * INV_ROOT_TAU) * bell


def nothing(at):
    pass


def qkv_phase(h, qkv, packed, need=nothing):
    width = h.shape[-1]

    def one(at):
        need(at)
        cols = span_of(at, 256)
        y = mm(h[...], qkv[:, cols])
        if at < width // 256:
            y = y * 0.125
        packed[:, cols] = y.astype(BF)

    steps(qkv.shape[1] // 256, one)


def lane_half(shape):
    return lax.broadcasted_iota(jnp.int32, shape, len(shape) - 1) < 64


def split_pair(pair, first):
    zero = jnp.zeros_like(pair)
    return jnp.concatenate([jnp.where(first, pair, zero), jnp.where(first, zero, pair)], axis=0)


def values_and_ones(v2, first):
    one = jnp.ones_like(v2)
    return jnp.concatenate([split_pair(v2, first), split_pair(one, first)], axis=1)


def by_level(level, run):
    @pl.when(level <= 2)
    def _():
        run(256)

    @pl.when(level == 3)
    def _():
        run(512)


def pair_ignored(pair, length):
    pass


def attention_forward(level, valid, bias, packed, context, portions, linv, done=pair_ignored):
    rows, width = context.shape
    query = 256

    def run(length):
        live = valid_row(valid, level)
        barred = jnp.where(live > 0, 0.0, NEGATIVE)
        if length == 256:
            shift = 6 + level
            a = lax.broadcasted_iota(jnp.int32, (256, 256), 0) >> shift
            b = lax.broadcasted_iota(jnp.int32, (256, 256), 1) >> shift
            apart = jnp.where(a == b, 0.0, NEGATIVE)
            for block in range(rows // 256):
                bias[span_of(block, 256), :] = apart + barred[:, block * 256 : (block + 1) * 256]
        first = lane_half((length, 128))

        def pair(at):
            lanes = span_of(at, 128)
            for block in range(rows // length):
                base = block * length
                k2 = packed[base : base + length, span_of(at, 128, width)]
                v2 = packed[base : base + length, span_of(at, 128, 2 * width)]
                kk = split_pair(k2, first)
                vv = values_and_ones(v2, first)
                for part in range(length // query):
                    at_rows = pl.ds(base + part * query, query)
                    scores = mm_nt(packed[at_rows, lanes], kk)
                    halves = []
                    for head in range(2):
                        s = scores[:, head * length : (head + 1) * length]
                        s = s + (bias[at_rows, :] if length == 256 else barred)
                        top = jnp.max(s, axis=-1, keepdims=True)
                        halves.append(jnp.exp2((s - top) * LOG2E).astype(BF))
                    p = jnp.concatenate(halves, axis=1)
                    portions[at, at_rows, 0 : 2 * length] = p
                    both = mm(p, vv)
                    inverse = 1.0 / both[:, 128:]
                    linv[at_rows, lanes] = inverse.astype(BF)
                    context[at_rows, lanes] = (both[:, :128] * inverse).astype(BF)
            done(at, length)

        steps(width // 128, pair, PAIRS_FORWARD)

    by_level(level, run)


def attention_backward(level, packed, context, portions, linv, dcontext, dpacked, slot=0, copy=None):
    rows, width = context.shape
    query = 256

    def run(length):
        first = lane_half((length, 128))

        def pair(at):
            if copy is not None:
                copy(slot, at, length).wait()
            lanes = span_of(at, 128)
            for block in range(rows // length):
                base = block * length
                whole = pl.ds(base, length)
                k2 = packed[whole, span_of(at, 128, width)]
                v2 = packed[whole, span_of(at, 128, 2 * width)]
                kk = split_pair(k2, first)
                vv = values_and_ones(v2, first)
                dk = None
                dv = None
                for part in range(length // query):
                    at_rows = pl.ds(base + part * query, query)
                    out = dcontext[at_rows, lanes].astype(F32) * linv[at_rows, lanes].astype(F32)
                    low = out.astype(BF)
                    both = jnp.concatenate(
                        [low, (-out * context[at_rows, lanes].astype(F32)).astype(BF)], axis=1
                    )
                    p = portions[at, at_rows, 0 : 2 * length]
                    ds = p * mm_nt(both, vv).astype(BF)
                    q2 = packed[at_rows, lanes]
                    dpacked[at_rows, lanes] = (mm(ds, kk) * 0.125).astype(BF)
                    more_k = mm_tn(ds, q2)
                    more_v = mm_tn(p, low)
                    dk = more_k if dk is None else dk + more_k
                    dv = more_v if dv is None else dv + more_v
                dk = jnp.where(first, dk[:length], dk[length:])
                dv = jnp.where(first, dv[:length], dv[length:])
                dpacked[whole, span_of(at, 128, width)] = dk.astype(BF)
                dpacked[whole, span_of(at, 128, 2 * width)] = dv.astype(BF)

        steps(width // 128, pair, PAIRS_BACKWARD)

    by_level(level, run)


def project(x, weight, out):
    def one(at):
        cols = span_of(at, 256)
        out[:, cols] = mm(x[...], weight[:, cols]).astype(BF)

    steps(out.shape[1] // 256, one)


def project_back(x, weight, out):
    def one(at):
        cols = span_of(at, 256)
        out[:, cols] = mm_nt(x[...], weight[cols, :]).astype(BF)

    steps(out.shape[1] // 256, one)


def adapter_norm(base, inner, live, w, saved, out, stats):
    act, slope, std, scale = saved
    rows, width = inner.shape
    block = 128

    def one(at):
        r = span_of(at, block)
        x = inner[r, :]
        pre = mm_nt(x, w.down[...]) + w.down_bias
        a, g = gelu_both(pre)
        a = a.astype(BF)
        act[r, :] = a
        slope[r, :] = g
        branch = x.astype(F32) + (mm(a, w.up[...]) + w.up_bias)
        total = base[r, :].astype(F32) + branch
        alive = live[r, :]
        stats[0:1, :] += jnp.sum(branch * branch * alive, axis=0, keepdims=True)
        mean = jnp.mean(total, axis=-1, keepdims=True)
        centered = total - mean
        variance = jnp.mean(centered * centered, axis=-1, keepdims=True)
        square = jnp.sum((variance + mean * mean) * alive, axis=0, keepdims=True)
        stats[1:2, :] += jnp.broadcast_to(square, (1, width))
        s = lax.rsqrt(variance + EPSILON)
        n = centered * s
        std[r, :] = n.astype(BF)
        scale[r, :] = s
        out[r, :] = (n * w.gain + w.bias).astype(BF)

    steps(rows // block, one)


def ffn_forward(middle, win, wout, act, slope, returned, need=nothing):
    need(0)
    expand(middle, win, act, slope)
    need(1)
    project(act, wout, returned)


def expand(middle, win, act, slope):

    def one(at):
        cols = span_of(at, 256)
        z = mm(middle[...], win[:, cols])
        a, g = gelu_both(z)
        act[:, cols] = a.astype(BF)
        slope[:, cols] = g.astype(BF)

    steps(win.shape[1] // 256, one, FFN_FORWARD)


def norm_adapter_back(dtotal, saved, inner, w, low, dpre_all, dinner, grads_down, grads_up):
    act, slope, std, scale = saved
    rows = inner.shape[0]
    block = 128

    def add(row, values):
        grads_down[row : row + 1, 0 : values.shape[1]] += jnp.sum(values, axis=0, keepdims=True)

    def one(at):
        r = span_of(at, block)
        g = dtotal[r, :]
        n = std[r, :].astype(F32)
        add(GAIN, g * n)
        add(BIAS, g)
        gg = g * w.gain
        m1 = jnp.mean(gg, axis=-1, keepdims=True)
        m2 = jnp.mean(gg * n, axis=-1, keepdims=True)
        d = scale[r, :] * (gg - m1 - n * m2)
        dtotal[r, :] = d
        e = d.astype(BF)
        low[r, :] = e
        e32 = e.astype(F32)
        add(UP_BIAS, e32)
        dpre = (mm_nt(e, w.up[...]) * slope[r, :]).astype(BF)
        dpre_all[r, :] = dpre
        add(DOWN_BIAS, dpre.astype(F32))
        dinner[r, :] = (e32 + mm(dpre, w.down[...])).astype(BF)

    steps(rows // block, one)
    grads_up[0:MATRIX_ROWS, :] += mm_tn(act[...], low[...])
    grads_down[0:MATRIX_ROWS, :] += mm_tn(dpre_all[...], inner[...])


def ffn_backward(dreturned, win, wout, slope, dexp, dsecond):
    expand_back(dreturned, wout, slope, dexp)
    project_add(dexp, win, dsecond)


def expand_back(dreturned, wout, slope, dexp):
    def one(at):
        cols = span_of(at, 256)
        d = mm_nt(dreturned[...], wout[cols, :])
        dexp[:, cols] = d.astype(BF) * slope[:, cols]

    steps(wout.shape[0] // 256, one, FFN_BACKWARD)


def project_add(x, weight, out):
    def one(at):
        cols = span_of(at, 256)
        out[:, cols] += mm_nt(x[...], weight[cols, :])

    steps(weight.shape[0] // 256, one)


def input_backward(dpacked, qkv, dfirst, dentry):
    def one(at):
        cols = span_of(at, 256)
        d = mm_nt(dpacked[...], qkv[cols, :])
        dentry[:, cols] = (dfirst[:, cols].astype(F32) + d).astype(BF)

    steps(qkv.shape[0] // 256, one)


class Item(NamedTuple):
    make: Any
    ref: Any

    def start(self):
        self.make().start()

    def wait(self):
        self.make().wait()


class Call:
    def __init__(self, section, slots, base=0):
        self.slots, self.base = slots, base
        self.args, self.in_specs, self.in_names = [], [], []
        self.outs, self.out_specs, self.out_names = [], [], []
        self.scratch, self.scratch_names = [], []
        self.kinds = {}
        self.section = section
        self.flops = 0
        self.limit = VMEM_LIMIT

    def _add(self, name, array, spec):
        self.args.append(array)
        self.in_specs.append(spec)
        self.in_names.append(name)

    def _temp(self, name, shape):
        self.scratch.append(shape)
        self.scratch_names.append(name)

    def whole(self, **arrays):
        for name, array in arrays.items():
            zeros = (0,) * array.ndim
            self._add(name, array, pl.BlockSpec(array.shape, lambda i, s, zeros=zeros: zeros))

    def raw(self, **arrays):
        for name, array in arrays.items():
            self._add(name, array, ANY)

    def load(self, micro=False, depth=2, **arrays):
        for name, array in arrays.items():
            depth_of = min(depth, self.slots)
            self._add((name, 0), array, ANY)
            self._temp((name, 1), pltpu.VMEM((depth_of,) + array.shape[1:], array.dtype))
            self._temp((name, 2), pltpu.SemaphoreType.DMA((depth_of,)))
            self.kinds[name] = (0, depth_of, micro)

    def save(self, depth=2, **shapes):
        for name, (shape, dtype) in shapes.items():
            depth_of = min(depth, self.slots)
            self.outs.append(jax.ShapeDtypeStruct((self.slots,) + shape, dtype))
            self.out_specs.append(ANY)
            self.out_names.append((name, 0))
            self._temp((name, 1), pltpu.VMEM((depth_of,) + shape, dtype))
            self._temp((name, 2), pltpu.SemaphoreType.DMA((depth_of,)))
            self.kinds[name] = (1, depth_of, False)

    def out(self, **shapes):
        for name, (shape, dtype) in shapes.items():
            self.outs.append(jax.ShapeDtypeStruct(shape, dtype))
            self.out_specs.append(ANY)
            self.out_names.append(name)

    def blocks(self, **shapes):
        for name, (shape, dtype) in shapes.items():
            zeros = (0,) * len(shape)
            self.outs.append(jax.ShapeDtypeStruct(shape, dtype))
            self.out_specs.append(pl.BlockSpec(shape, lambda i, s, zeros=zeros: zeros))
            self.out_names.append(name)

    def temp(self, **shapes):
        for name, (shape, dtype) in shapes.items():
            self._temp(name, pltpu.VMEM(shape, dtype))

    def sems(self, **counts):
        for name, count in counts.items():
            self._temp(name, pltpu.SemaphoreType.DMA(count if isinstance(count, tuple) else (count,)))

    def run(self, body, name):
        names = self.in_names + self.out_names + self.scratch_names
        slots, base = self.slots, self.base

        def kernel(section, *refs):
            step = pl.program_id(0) if slots > 1 else 0
            ref = dict(zip(names, refs))
            r = SimpleNamespace(**{n: v for n, v in ref.items() if isinstance(n, str)})
            r.step, r.section = step, section[0]

            def level_in(which, slot):
                number = PLAN[which][base]
                for other in range(1, slots):
                    number = jnp.where(slot == other, PLAN[which][base + other], number)
                return number

            def level(slot):
                return jnp.where(r.section == 0, level_in(0, slot), level_in(1, slot))

            def copy(name, slot):
                kind, depth, micro = self.kinds[name]
                at = slot if depth > 1 else 0
                near = ref[name, 1].at[at]
                if kind == 0:
                    far = ref[name, 0].at[level(slot) if micro else base + slot]
                    pair = (far, near)
                else:
                    pair = (near, ref[name, 0].at[slot])
                return Item(lambda: pltpu.make_async_copy(*pair, ref[name, 2].at[at]), near)

            def start(*which):
                for n in which:
                    copy(n, step).start()

            def wait(*which):
                for n in which:
                    copy(n, step).wait()

            def at_first(act):
                if slots > 1:
                    pl.when(step == 0)(act)
                else:
                    act()

            def at_last(act):
                if slots > 1:
                    pl.when(step == slots - 1)(act)
                else:
                    act()

            r.level_of, r.level = level, level(step)
            r.copy, r.start, r.wait, r.at_first, r.at_last = copy, start, wait, at_first, at_last
            for n, (kind, depth, micro) in self.kinds.items():
                setattr(r, n, ref[n, 1].at[step if depth > 1 else 0])
                setattr(r, "all_" + n, (ref[n, 0], ref[n, 1]))
            body(r)

        results = pl.pallas_call(
            kernel,
            out_shape=self.outs,
            grid_spec=pltpu.PrefetchScalarGridSpec(
                num_scalar_prefetch=1,
                grid=(slots,),
                in_specs=self.in_specs,
                out_specs=self.out_specs,
                scratch_shapes=self.scratch,
            ),
            compiler_params=pltpu.CompilerParams(vmem_limit_bytes=self.limit),
            cost_estimate=pl.CostEstimate(
                flops=self.flops * slots, bytes_accessed=1 << 20, transcendentals=0
            ),
            name=name,
        )(self.section, *self.args)
        return SimpleNamespace(
            **{n[0] if isinstance(n, tuple) else n: v for n, v in zip(self.out_names, results)}
        )


class Fill:
    def __init__(self, own, got, target, sems, mine, pieces=1, dim=0):
        self.sources, self.target, self.sems, self.mine = (own, got), target, sems, mine
        self.pieces, self.dim = pieces, dim

    def _copy(self, source, piece):
        source = self.sources[source]
        if self.pieces == 1:
            return pltpu.make_async_copy(source, self.target, self.sems.at[0])
        size = self.target.shape[self.dim] // self.pieces
        cut = tuple(
            pl.ds(piece * size, size) if at == self.dim else slice(None)
            for at in range(len(self.target.shape))
        )
        return pltpu.make_async_copy(source.at[cut], self.target.at[cut], self.sems.at[piece])

    def start(self):
        for source, chosen_one in enumerate((self.mine, jnp.logical_not(self.mine))):

            @pl.when(chosen_one)
            def _():
                for piece in range(self.pieces):
                    self._copy(source, piece).start()

    def wait(self, piece=None):
        for at in range(self.pieces) if piece is None else (piece,):
            self._copy(0, at).wait()


def zero(*refs):
    for ref in refs:
        ref[...] = jnp.zeros_like(ref)


def valid_row(valid, level):
    row = valid[0:1, :]
    for other in range(1, valid.shape[0]):
        row = jnp.where(level == other, valid[other : other + 1, :], row)
    return row


def live_column(valid, level, live):
    row = jnp.where(valid_row(valid, level) > 0, 1.0, 0.0)
    row = jnp.broadcast_to(row, (8, row.shape[1])).astype(BF)
    live[...] = mm_tn(row, jnp.full((8, 128), 0.125, BF))[:, 0:1]


def adapter_of(mats, vecs, which):
    vec = vecs.at[which]
    return Adapter(
        mats.at[2 * which], vec[0:1, 0:64], mats.at[2 * which + 1], vec[1:2, :], vec[2:3, :], vec[3:4, :]
    )


def portions_shape(rows, width):
    return ((width // 128, rows, 2 * rows), BF)


def attn_saved(rows, width, hidden):
    return dict(
        packed=((rows, 3 * width), BF), context=((rows, width), BF), linv=((rows, width), BF)
    )


def norm_saved(rows, width):
    return dict(
        attended=((rows, width), BF),
        act1=((rows, 64), BF),
        slope1=((rows, 64), F32),
        std1=((rows, width), BF),
        scale1=((rows, 1), F32),
    )


def ffn_saved(rows, width, hidden):
    return dict(
        slope=((rows, hidden), BF),
        returned=((rows, width), BF),
        act2=((rows, 64), BF),
        slope2=((rows, 64), F32),
        std2=((rows, width), BF),
        scale2=((rows, 1), F32),
    )


STAT_ROWS = 8


def pair_copy(source, target, sems, pair, length):
    lanes = pl.ds(0, 2 * length)
    return pltpu.make_async_copy(
        source.at[pair, :, lanes], target.at[pair, :, lanes], sems.at[pair]
    )


def first_attn_forward(section, tokens, valid, own, got, sizes, slots):
    rows, width, hidden = sizes
    pairs = width // 128
    call = Call(section, slots)
    call.load(micro=True, h=tokens)
    call.whole(valid=valid)
    call.raw(own=own.qkv, got=got.qkv, own_out=own.out, got_out=got.out)
    call.raw(own_mats=own.mats, got_mats=got.mats, own_vecs=own.vecs, got_vecs=got.vecs)
    call.save(**attn_saved(*sizes), **norm_saved(rows, width), middle=((rows, width), BF))
    shape, dtype = portions_shape(rows, width)
    call.out(portions=((slots,) + shape, dtype))
    call.blocks(stats=((2, width), F32))
    call.temp(
        held=((slots,) + shape, dtype),
        live=((rows, 1), F32),
        bias=((rows, 256), F32),
        qkv=(own.qkv.shape, BF),
        out=(own.out.shape, BF),
        mats=(own.mats.shape, BF),
        vecs=(own.vecs.shape, F32),
    )
    call.sems(qkv_sems=3, out_sems=1, mats_sems=1, vecs_sems=1, pair_sems=(slots, pairs))
    call.flops = 2 * rows * width * width * 12

    def body(r):
        mine = r.section == 0
        qkv = Fill(r.own, r.got, r.qkv, r.qkv_sems, mine, 3, 2)
        out = Fill(r.own_out, r.got_out, r.out, r.out_sems, mine)
        mats = Fill(r.own_mats, r.got_mats, r.mats, r.mats_sems, mine)
        vecs = Fill(r.own_vecs, r.got_vecs, r.vecs, r.vecs_sems, mine)

        def begin():
            r.copy("h", 0).start()
            for item in (qkv, out, mats, vecs):
                item.start()
            for slot in range(1, slots):
                r.copy("h", slot).start()
            zero(r.stats)

        r.at_first(begin)
        live_column(r.valid, r.level, r.live)
        r.wait("h")
        qkv_phase(r.h, r.qkv.at[0], r.packed, lambda at: at % 3 or r.at_first(lambda: qkv.wait(at // 3)))
        r.start("packed")

        def pair_copy_of(slot, pair, length):
            return pair_copy(r.held.at[slot], r.portions.at[slot], r.pair_sems.at[slot], pair, length)

        attention_forward(
            r.level, r.valid, r.bias, r.packed, r.context, r.held.at[r.step], r.linv,
            lambda pair, length: pair_copy_of(r.step, pair, length).start(),
        )
        r.start("context", "linv")
        r.at_first(lambda: [item.wait() for item in (out, mats, vecs)] and None)
        project(r.context, r.out.at[0], r.attended)
        saved = (r.act1, r.slope1, r.std1, r.scale1)
        adapter_norm(
            r.h, r.attended, r.live, adapter_of(r.mats, r.vecs, 0), saved, r.middle, r.stats
        )
        r.start("middle", *norm_saved(rows, width))

        def finish():
            for slot in range(slots):
                for name in ("middle", *attn_saved(*sizes), *norm_saved(rows, width)):
                    r.copy(name, slot).wait()

                def waits(length):
                    for pair in range(pairs):
                        pair_copy_of(slot, pair, length).wait()

                by_level(r.level_of(slot), waits)

        r.at_last(finish)

    return call.run(body, "first_attn")


STAGE_ATTN0, STAGE_FFN0, STAGE_ATTN1, STAGE_FFN1 = range(4)


def middle_part(section, kept, cotangent, valid, own, got, sizes, slots):
    rows, width, hidden = sizes
    call = Call(section, slots)
    row = ((rows, width), BF)
    call.raw(base=kept.middle, cotangent=cotangent, **{"far_" + n: getattr(kept, n) for n in norm_saved(rows, width)})
    call.whole(valid=valid, stats=kept.stats)
    for name in ("qkv", "out", "win", "wout", "mats", "vecs"):
        call.raw(**{"own_" + name: getattr(own, name), "got_" + name: getattr(got, name)})
    call.temp(
        qkv=(own.qkv.shape, BF),
        win=(own.win.shape, BF),
        wout=(own.wout.shape, BF),
        outs=((2,) + own.out.shape, BF),
        mats=((2,) + own.mats.shape, BF),
        vecs=((2,) + own.vecs.shape, F32),
    )
    call.sems(win_sems=4, wout_sems=1, weight_sems=(8, 1), base_sems=1, up_sems=1, norm_sems=5)
    call.save(depth=1, result=row, dfirst0=row, dcontext0=row)
    grad_shape = (4, BLOCK_ROWS, width)
    call.temp(grads=((8,) + grad_shape[1:], F32))
    call.blocks(keep=(grad_shape, BF), send=(grad_shape, BF))
    call.temp(**attn_saved(*sizes))
    call.temp(
        attended=((4,) + row[0], BF),
        act1=((4, rows, 64), BF),
        slope1=((4, rows, 64), F32),
        std1=((4,) + row[0], BF),
        scale1=((4, rows, 1), F32),
        slope=((2, rows, hidden), BF),
        chain=((3,) + row[0], BF),
        sums=((4, 2, width), F32),
        up=row,
        held=portions_shape(rows, width),
        live=((rows, 1), F32),
        bias=((rows, 256), F32),
        wide=((rows, hidden), BF),
        dsum=((rows, width), F32),
        low=row,
        dpre=((rows, 64), BF),
        dinner=row,
    )
    call.flops = 12 * rows * width * (4 * width + 2 * hidden)
    norms = tuple(norm_saved(rows, width))

    def body(r):
        first, second = r.section == 0, r.section == 1

        def fill(name, target, at, mine):
            return Fill(
                getattr(r, "own_" + name), getattr(r, "got_" + name), target, r.weight_sems.at[at], mine
            )

        qkv, out1 = fill("qkv", r.qkv, 0, second), fill("out", r.outs.at[1], 1, second)
        mats1, vecs1 = fill("mats", r.mats.at[1], 2, second), fill("vecs", r.vecs.at[1], 3, second)
        out0 = fill("out", r.outs.at[0], 4, first)
        mats0, vecs0 = fill("mats", r.mats.at[0], 5, first), fill("vecs", r.vecs.at[0], 6, first)
        win0, win1 = (Fill(r.own_win, r.got_win, r.win, r.win_sems, m, 4, 2) for m in (first, second))
        wout0, wout1 = (Fill(r.own_wout, r.got_wout, r.wout, r.wout_sems, m) for m in (first, second))

        def base_copy(slot):
            return pltpu.make_async_copy(r.base.at[slot], r.chain.at[0], r.base_sems.at[0])

        def slot_copies():
            copies = [pltpu.make_async_copy(r.cotangent.at[r.level], r.up, r.up_sems.at[0])]
            for at, name in enumerate(norms):
                copies.append(
                    pltpu.make_async_copy(
                        getattr(r, "far_" + name).at[r.step], getattr(r, name).at[0], r.norm_sems.at[at]
                    )
                )
            return copies

        def begin():
            for item in (mats0, vecs0):
                item.start()
            base_copy(0).start()
            for item in (win0, wout0, qkv, out1, mats1, vecs1, out0):
                item.start()
            zero(r.grads, r.sums)
            for item in (mats0, vecs0, win0, wout0):
                item.wait()

        def later(act):
            pl.when(r.step > 0)(act)

        r.at_first(begin)
        for item in slot_copies():
            item.start()
        live_column(r.valid, r.level, r.live)
        base_copy(r.step).wait()
        later(lambda: r.copy("result", r.step - 1).wait())

        def saved_of(stage):
            return tuple(getattr(r, n).at[stage] for n in ("act1", "slope1", "std1", "scale1"))

        def adapter_at(stage):
            return adapter_of(r.mats.at[stage // 2], r.vecs.at[stage // 2], stage % 2)

        def forward(at, carry):
            stage = at + 1
            inner = r.attended.at[stage]
            here = r.chain.at[at]

            @pl.when(at == 1)
            def _():
                win1.start()
                wout1.start()
                for item in (qkv, out1, mats1, vecs1):
                    r.at_first(item.wait)
                qkv_phase(here, r.qkv.at[0], r.packed)
                attention_forward(r.level, r.valid, r.bias, r.packed, r.context, r.held, r.linv)
                project(r.context, r.outs.at[1, 0], inner)

            @pl.when(at != 1)
            def _():
                @pl.when(at == 2)
                def _():
                    win1.wait()
                    wout1.wait()

                ffn_forward(here, r.win.at[0], r.wout.at[0], r.wide, r.slope.at[stage // 2], inner)

            def norm(target):
                adapter_norm(
                    here, inner, r.live, adapter_at(stage), saved_of(stage), target, r.sums.at[stage]
                )

            norm(r.chain.at[lax.rem(at + 1, 3)])
            return carry

        lax.fori_loop(0, 3, forward, 0)
        r.result[...] = r.chain[0]
        r.start("result")

        @pl.when(r.step + 1 < slots)
        def _():
            base_copy(r.step + 1).start()

        for item in slot_copies():
            item.wait()

        def backward(at, carry):
            stage = 3 - at
            inner = r.attended.at[stage]

            @pl.when(stage % 2 == 1)
            def _():
                r.dsum[...] = r.up[...].astype(F32)

            norm_adapter_back(
                r.dsum, saved_of(stage), inner, adapter_at(stage), r.low, r.dpre, r.dinner,
                r.grads.at[2 * stage], r.grads.at[2 * stage + 1],
            )

            @pl.when(stage % 2 == 1)
            def _():
                @pl.when(at == 2)
                def _():
                    wout0.wait()
                    win0.wait()

                ffn_backward(r.dinner, r.win.at[0], r.wout.at[0], r.slope.at[stage // 2], r.wide, r.dsum)

            @pl.when(stage % 2 == 0)
            def _():
                @pl.when(at == 3)
                def _():
                    r.at_first(out0.wait)
                    later(lambda: r.copy("dfirst0", r.step - 1).wait())

                @pl.when(at == 1)
                def _():
                    wout0.start()
                    win0.start()
                    later(lambda: r.copy("dcontext0", r.step - 1).wait())

                project_back(r.dinner, r.outs.at[stage // 2, 0], r.dcontext0)

                @pl.when(at == 1)
                def _():
                    attention_backward(
                        r.level, r.packed, r.context, r.held, r.linv, r.dcontext0, r.packed
                    )
                    input_backward(r.packed, r.qkv.at[0], r.dsum, r.up)

            return carry

        lax.fori_loop(0, 4, backward, 0)
        r.dfirst0[...] = r.dsum[...].astype(BF)
        r.start("dfirst0", "dcontext0")

        def finish():
            r.wait("result", "dfirst0", "dcontext0")
            for layer in range(2):
                attn, ffn = r.sums.at[2 * layer], r.sums.at[2 * layer + 1]
                target = r.grads.at[4 * layer + ATTN_UP]
                if layer == 0:
                    attn = r.stats
                target[STATS : STATS + 1, :] = attn[0:1, :]
                target[STATS + 1 : STATS + 3, :] = ffn[...]
                count = jnp.zeros((1, 1), F32)
                for slot in range(slots):
                    row = jnp.where(valid_row(r.valid, r.level_of(slot)) > 0, 1.0, 0.0)
                    count += jnp.sum(row, axis=1, keepdims=True)
                target[STATS + 3 : STATS + 4, :] = jnp.broadcast_to(count, (1, width))
            for block in range(4):
                r.keep[block] = r.grads[4 * r.section + block].astype(BF)
                r.send[block] = r.grads[4 - 4 * r.section + block].astype(BF)

        r.at_last(finish)

    return call.run(body, "middle_part")


def first_attn_backward(section, back, there, kept, own, got, sizes, slots):
    rows, width, hidden = sizes
    pairs = width // 128
    call = Call(section, slots)
    call.load(packed=kept.packed, dcontext=back.dcontext0, context=kept.context, linv=kept.linv)
    call.load(dfirst=back.dfirst0)
    call.raw(portions=kept.portions, own=own.qkv, got=got.qkv, here=back.result, there=there)
    call.out(input_grad=((slots, rows, width), BF), result=((2 * slots, rows, width), BF))
    shape, dtype = portions_shape(rows, width)
    call.temp(
        held=((slots,) + shape, dtype),
        qkv=(own.qkv.shape, BF),
        stage=((2 * slots, rows, width), BF),
        dentry=((slots, rows, width), BF),
    )
    call.sems(
        qkv_sems=3, pair_sems=(slots, pairs), in_sems=2 * slots, out_sems=2 * slots, grad_sems=slots
    )
    call.flops = 2 * rows * width * width * 12

    def body(r):
        fill = Fill(r.own, r.got, r.qkv, r.qkv_sems, r.section == 0, 3, 1)

        def pair_copy_of(slot, pair, length):
            return pair_copy(r.portions.at[slot], r.held.at[slot], r.pair_sems.at[slot], pair, length)

        loads = ("packed", "dcontext", "context", "linv")
        ins, outs = [], []
        for at in range(slots):
            mine, other = (jnp.where(r.section == 0, PLAN[a][at], PLAN[1 - a][at]) for a in range(2))
            for source, target in ((r.here, mine), (r.there, other)):
                n = len(ins)
                ins.append(pltpu.make_async_copy(source.at[at], r.stage.at[n], r.in_sems.at[n]))
                outs.append(
                    pltpu.make_async_copy(r.stage.at[n], r.result.at[target], r.out_sems.at[n])
                )

        def begin():
            for slot in range(slots):
                for name in loads:
                    r.copy(name, slot).start()

                def starts(length):
                    for pair in range(pairs):
                        pair_copy_of(slot, pair, length).start()

                by_level(r.level_of(slot), starts)
                if slot == 0:
                    fill.start()
                r.copy("dfirst", slot).start()
            for item in ins:
                item.start()

        def grad_copy(slot):
            target = jnp.where(r.level_of(slot) % slots == 0, 0, 1)
            return pltpu.make_async_copy(
                r.dentry.at[slot], r.input_grad.at[target], r.grad_sems.at[slot]
            )

        r.at_first(begin)
        r.wait(*loads)
        attention_backward(
            r.level, r.packed, r.context, r.held.at[r.step], r.linv, r.dcontext, r.packed,
            r.step, pair_copy_of,
        )
        r.wait("dfirst")
        r.at_first(fill.wait)
        input_backward(r.packed, r.qkv.at[0], r.dfirst, r.dentry.at[r.step])
        grad_copy(r.step).start()

        def pass_on():
            for come, go in zip(ins, outs):
                come.wait()
                go.start()

        def finish():
            for slot in range(slots):
                grad_copy(slot).wait()
            for item in outs:
                item.wait()

        r.at_first(pass_on)
        r.at_last(finish)

    return call.run(body, "attn_back")


def packed_small(mats, vecs):
    width = mats[0].shape[-1]

    def kernel(*refs):
        sources, (out_mats, out_vecs) = refs[:-2], refs[-2:]
        for at in range(4):
            out_mats[at] = sources[at][0]
        out_vecs[...] = jnp.zeros_like(out_vecs)
        for at, ref in enumerate(sources[4:]):
            out_vecs[at // 4, at % 4 : at % 4 + 1, 0 : ref.shape[1]] = ref[...]

    return pl.pallas_call(
        kernel,
        out_shape=(
            jax.ShapeDtypeStruct((4, 64, width), BF),
            jax.ShapeDtypeStruct((2, 4, width), F32),
        ),
        compiler_params=pltpu.CompilerParams(vmem_limit_bytes=62 << 20),
        name="pack",
    )(*mats, *vecs)


def unpacked(quarters, member):
    width = quarters[0].shape[-1]
    matrix = jax.ShapeDtypeStruct((1, MATRIX_ROWS, width), F32)
    vector = jax.ShapeDtypeStruct((1, width), F32)
    small = jax.ShapeDtypeStruct((1, 64), F32)
    group = (matrix, small, matrix, vector, vector, vector)

    def kernel(member, *refs):
        sources, outs = refs[:4], refs[4:]

        def block(at):
            picked = sources[0][...]
            for d in (1, 2, 3):
                picked = jnp.where((member[0] ^ at) == d, sources[d][...], picked)
            return picked.astype(F32)

        for down, up, (mat_down, down_bias, mat_up, up_bias, gain, bias) in (
            (ATTN_DOWN, ATTN_UP, outs[:6]),
            (FFN_DOWN, FFN_UP, outs[6:12]),
        ):
            down, up = block(down), block(up)
            mat_down[0] = down[:MATRIX_ROWS]
            mat_up[0] = up[:MATRIX_ROWS]
            for row, target in ((UP_BIAS, up_bias), (GAIN, gain), (BIAS, bias), (DOWN_BIAS, down_bias)):
                target[...] = down[row : row + 1, : target.shape[1]]
        sums = block(ATTN_UP)[STATS : STATS + STAT_ROWS]
        means = jnp.sum(sums, axis=1, keepdims=True) / (sums[3:4, 0:1] * width)
        lane = lax.broadcasted_iota(jnp.int32, (1, 3), 1)
        picked = jnp.where(lane == 0, means[0:1], jnp.where(lane == 1, means[1:2], means[2:3]))
        outs[12][...] = jnp.sqrt(picked)

    vmem = pl.BlockSpec(memory_space=pltpu.VMEM)
    outs = pl.pallas_call(
        kernel,
        in_specs=[pl.BlockSpec(memory_space=pltpu.SMEM)] + [vmem] * 4,
        out_shape=group * 2 + (jax.ShapeDtypeStruct((1, 3), F32),),
        compiler_params=pltpu.CompilerParams(vmem_limit_bytes=SMALL_LIMIT),
        name="unpack",
    )(member.astype(jnp.int32).reshape(1), *quarters)
    outs = list(outs)
    for at in (0, 6):
        outs[at] = jnp.swapaxes(outs[at], 1, 2)
    return tuple(outs)


def swap(value):
    return lax.ppermute(value, "section", [(0, 1), (1, 0)])


def after(value, *others):
    return lax.optimization_barrier((value,) + others)[0]


def exchanged(value, bits):
    count = lax.axis_size("dp")
    return lax.ppermute(value, "dp", [(at, at ^ bits) for at in range(count)])


def summed_quarters(parts, before_last):
    mine, count = lax.axis_index("dp"), lax.axis_size("dp")
    member = mine & 3

    def quarter(d):
        first, second = (lax.dynamic_index_in_dim(v, member ^ d, 0, keepdims=False) for v in parts)
        return first + second

    def together(own, a, b, c):
        own, a, b, c = (v.astype(F32) for v in (own, a, b, c))
        return ((own + a) + (b + c)).astype(BF)

    total = together(quarter(0), *(exchanged(quarter(d), d) for d in (1, 2, 3)))
    bit = 4
    while bit < count:
        total = total + exchanged(total, bit)
        bit *= 2
    total = after(total, before_last)
    return [total] + [exchanged(total, d) for d in (1, 2, 3)], member


def body(
    tokens, valid, cotangent, qkv, out, win, wout,
    attn_down, attn_down_bias, attn_up, attn_up_bias, gain1, bias1,
    ffn_down, ffn_down_bias, ffn_up, ffn_up_bias, gain2, bias2,
):
    section = lax.axis_index("section")
    micro_count, rows, width = tokens.shape
    sizes = (rows, width, win.shape[-1])
    slots = micro_count // 2
    mats, vecs = packed_small(
        (jnp.swapaxes(attn_down, 1, 2), attn_up, jnp.swapaxes(ffn_down, 1, 2), ffn_up),
        (attn_down_bias, attn_up_bias, gain1, bias1, ffn_down_bias, ffn_up_bias, gain2, bias2),
    )
    own = Layer(qkv, out, win, wout, mats, vecs)
    early = [swap(v) for v in (qkv, out, mats, vecs)]
    got_qkv, got_out, got_mats, got_vecs = early
    got_win, got_wout = (swap(after(v, *early)) for v in (win, wout))
    got = Layer(got_qkv, got_out, got_win, got_wout, got_mats, got_vecs)
    where = section.astype(jnp.int32).reshape(1)

    kept = first_attn_forward(where, tokens, valid, own, got, sizes, slots)
    back = middle_part(where, kept, cotangent, valid, own, got, sizes, slots)

    got_grads = swap(back.send)
    there = swap(after(back.result, got_grads))
    quarters, member = summed_quarters((back.keep, got_grads), there)
    last = first_attn_backward(where, back, there, kept, own, got, sizes, slots)
    small = unpacked([quarters[0]] + [after(v, last.input_grad) for v in quarters[1:]], member)
    return (last.result, last.input_grad) + small


def solution(mesh):
    rows = P(None, "dp", None)
    matrix, vector = P("section", None, None), P("section", None)
    weights = (matrix, vector, matrix, vector, vector, vector)
    return jax.shard_map(
        body,
        mesh=mesh,
        in_specs=(rows, P(None, "dp"), rows) + (matrix,) * 4 + weights * 2,
        out_specs=(rows, P("section", "dp", None)) + weights * 2 + (vector,),
        check_vma=False,
    )
```

```python
import math
from types import SimpleNamespace
from typing import Any, NamedTuple

import jax
import jax.numpy as jnp
from jax import lax
from jax.experimental import pallas as pl
from jax.experimental.pallas import tpu as pltpu
from jax.sharding import PartitionSpec as P

NEGATIVE = -1e30
EPSILON = 1e-12
ROOT_HALF = 0.7071067811865476
INV_ROOT_TAU = 0.3989422804014327
LOG2E = 1.4426950408889634

PLAN = ((0, 1), (3, 2))

BF = jnp.bfloat16
F32 = jnp.float32
ANY = pl.BlockSpec(memory_space=pl.ANY)
VMEM_LIMIT = 60 << 20
SMALL_LIMIT = 16 << 20

ATTN_DOWN, ATTN_UP, FFN_DOWN, FFN_UP = range(4)
MATRIX_ROWS, BLOCK_ROWS = 64, 72
UP_BIAS, GAIN, BIAS, DOWN_BIAS = range(64, 68)
STATS = 64


class Layer(NamedTuple):
    qkv: Any
    out: Any
    win: Any
    wout: Any
    mats: Any
    vecs: Any


class Adapter(NamedTuple):
    down: Any
    down_bias: Any
    up: Any
    up_bias: Any
    gain: Any
    bias: Any


def mm(a, b):
    return jnp.dot(a, b, preferred_element_type=F32)


def mm_nt(a, b):
    return lax.dot_general(a, b, (((1,), (1,)), ((), ())), preferred_element_type=F32)


def mm_tn(a, b):
    return lax.dot_general(a, b, (((0,), (0,)), ((), ())), preferred_element_type=F32)


def span_of(index, size, base=0):
    start = index * size + base
    return pl.ds(start if isinstance(index, int) else pl.multiple_of(start, size), size)


def steps(count, body, unroll=None):
    if unroll is None or unroll >= count:
        for at in range(count):
            body(at)
        return

    def some(group, carry):
        for at in range(unroll):
            body(group * unroll + at)
        return carry

    lax.fori_loop(0, count // unroll, some, 0)


PAIRS_FORWARD, PAIRS_BACKWARD = 3, 1
FFN_FORWARD, FFN_BACKWARD = 12, 12


def gelu_both(z):
    cdf = 0.5 + 0.5 * lax.erf(z * ROOT_HALF)
    bell = jnp.exp2(z * z * (-0.5 * LOG2E))
    return z * cdf, cdf + (z * INV_ROOT_TAU) * bell


def nothing(at):
    pass


def qkv_phase(h, qkv, packed, need=nothing):
    width = h.shape[-1]

    def one(at):
        need(at)
        cols = span_of(at, 256)
        y = mm(h[...], qkv[:, cols])
        if at < width // 256:
            y = y * 0.125
        packed[:, cols] = y.astype(BF)

    steps(qkv.shape[1] // 256, one)


def lane_half(shape):
    return lax.broadcasted_iota(jnp.int32, shape, len(shape) - 1) < 64


def split_pair(pair, first):
    zero = jnp.zeros_like(pair)
    return jnp.concatenate([jnp.where(first, pair, zero), jnp.where(first, zero, pair)], axis=0)


def values_and_ones(v2, first):
    one = jnp.ones_like(v2)
    return jnp.concatenate([split_pair(v2, first), split_pair(one, first)], axis=1)


def by_level(level, run):
    @pl.when(level <= 2)
    def _():
        run(256)

    @pl.when(level == 3)
    def _():
        run(512)


def pair_ignored(pair, length):
    pass


def attention_forward(level, valid, bias, packed, context, portions, linv, done=pair_ignored):
    rows, width = context.shape
    query = 256

    def run(length):
        live = valid_row(valid, level)
        barred = jnp.where(live > 0, 0.0, NEGATIVE)
        if length == 256:
            shift = 6 + level
            a = lax.broadcasted_iota(jnp.int32, (256, 256), 0) >> shift
            b = lax.broadcasted_iota(jnp.int32, (256, 256), 1) >> shift
            apart = jnp.where(a == b, 0.0, NEGATIVE)
            for block in range(rows // 256):
                bias[span_of(block, 256), :] = apart + barred[:, block * 256 : (block + 1) * 256]
        first = lane_half((length, 128))

        def pair(at):
            lanes = span_of(at, 128)
            for block in range(rows // length):
                base = block * length
                k2 = packed[base : base + length, span_of(at, 128, width)]
                v2 = packed[base : base + length, span_of(at, 128, 2 * width)]
                kk = split_pair(k2, first)
                vv = values_and_ones(v2, first)
                for part in range(length // query):
                    at_rows = pl.ds(base + part * query, query)
                    scores = mm_nt(packed[at_rows, lanes], kk)
                    halves = []
                    for head in range(2):
                        s = scores[:, head * length : (head + 1) * length]
                        s = s + (bias[at_rows, :] if length == 256 else barred)
                        top = jnp.max(s, axis=-1, keepdims=True)
                        halves.append(jnp.exp2((s - top) * LOG2E).astype(BF))
                    p = jnp.concatenate(halves, axis=1)
                    portions[at, at_rows, 0 : 2 * length] = p
                    both = mm(p, vv)
                    inverse = 1.0 / both[:, 128:]
                    linv[at_rows, lanes] = inverse.astype(BF)
                    context[at_rows, lanes] = (both[:, :128] * inverse).astype(BF)
            done(at, length)

        steps(width // 128, pair, PAIRS_FORWARD)

    by_level(level, run)


def attention_backward(level, packed, context, portions, linv, dcontext, dpacked, slot=0, copy=None):
    rows, width = context.shape
    query = 256

    def run(length):
        first = lane_half((length, 128))

        def pair(at):
            if copy is not None:
                copy(slot, at, length).wait()
            lanes = span_of(at, 128)
            for block in range(rows // length):
                base = block * length
                whole = pl.ds(base, length)
                k2 = packed[whole, span_of(at, 128, width)]
                v2 = packed[whole, span_of(at, 128, 2 * width)]
                kk = split_pair(k2, first)
                vv = values_and_ones(v2, first)
                dk = None
                dv = None
                for part in range(length // query):
                    at_rows = pl.ds(base + part * query, query)
                    out = dcontext[at_rows, lanes].astype(F32) * linv[at_rows, lanes].astype(F32)
                    low = out.astype(BF)
                    both = jnp.concatenate(
                        [low, (-out * context[at_rows, lanes].astype(F32)).astype(BF)], axis=1
                    )
                    p = portions[at, at_rows, 0 : 2 * length]
                    ds = p * mm_nt(both, vv).astype(BF)
                    q2 = packed[at_rows, lanes]
                    dpacked[at_rows, lanes] = (mm(ds, kk) * 0.125).astype(BF)
                    more_k = mm_tn(ds, q2)
                    more_v = mm_tn(p, low)
                    dk = more_k if dk is None else dk + more_k
                    dv = more_v if dv is None else dv + more_v
                dk = jnp.where(first, dk[:length], dk[length:])
                dv = jnp.where(first, dv[:length], dv[length:])
                dpacked[whole, span_of(at, 128, width)] = dk.astype(BF)
                dpacked[whole, span_of(at, 128, 2 * width)] = dv.astype(BF)

        steps(width // 128, pair, PAIRS_BACKWARD)

    by_level(level, run)


def project(x, weight, out):
    def one(at):
        cols = span_of(at, 256)
        out[:, cols] = mm(x[...], weight[:, cols]).astype(BF)

    steps(out.shape[1] // 256, one)


def project_back(x, weight, out):
    def one(at):
        cols = span_of(at, 256)
        out[:, cols] = mm_nt(x[...], weight[cols, :]).astype(BF)

    steps(out.shape[1] // 256, one)


def adapter_norm(base, inner, live, w, saved, out, stats):
    act, slope, std, scale = saved
    rows, width = inner.shape
    block = 128

    def one(at):
        r = span_of(at, block)
        x = inner[r, :]
        pre = mm_nt(x, w.down[...]) + w.down_bias
        a, g = gelu_both(pre)
        a = a.astype(BF)
        act[r, :] = a
        slope[r, :] = g
        branch = x.astype(F32) + (mm(a, w.up[...]) + w.up_bias)
        total = base[r, :].astype(F32) + branch
        alive = live[r, :]
        stats[0:1, :] += jnp.sum(branch * branch * alive, axis=0, keepdims=True)
        mean = jnp.mean(total, axis=-1, keepdims=True)
        centered = total - mean
        variance = jnp.mean(centered * centered, axis=-1, keepdims=True)
        square = jnp.sum((variance + mean * mean) * alive, axis=0, keepdims=True)
        stats[1:2, :] += jnp.broadcast_to(square, (1, width))
        s = lax.rsqrt(variance + EPSILON)
        n = centered * s
        std[r, :] = n.astype(BF)
        scale[r, :] = s
        out[r, :] = (n * w.gain + w.bias).astype(BF)

    steps(rows // block, one)


def ffn_forward(middle, win, wout, act, slope, returned, need=nothing):
    need(0)
    expand(middle, win, act, slope)
    need(1)
    project(act, wout, returned)


def expand(middle, win, act, slope):

    def one(at):
        cols = span_of(at, 256)
        z = mm(middle[...], win[:, cols])
        a, g = gelu_both(z)
        act[:, cols] = a.astype(BF)
        slope[:, cols] = g.astype(BF)

    steps(win.shape[1] // 256, one, FFN_FORWARD)


def norm_adapter_back(dtotal, saved, inner, w, low, dpre_all, dinner, grads_down, grads_up):
    act, slope, std, scale = saved
    rows = inner.shape[0]
    block = 128

    def add(row, values):
        grads_down[row : row + 1, 0 : values.shape[1]] += jnp.sum(values, axis=0, keepdims=True)

    def one(at):
        r = span_of(at, block)
        g = dtotal[r, :]
        n = std[r, :].astype(F32)
        add(GAIN, g * n)
        add(BIAS, g)
        gg = g * w.gain
        m1 = jnp.mean(gg, axis=-1, keepdims=True)
        m2 = jnp.mean(gg * n, axis=-1, keepdims=True)
        d = scale[r, :] * (gg - m1 - n * m2)
        dtotal[r, :] = d
        e = d.astype(BF)
        low[r, :] = e
        e32 = e.astype(F32)
        add(UP_BIAS, e32)
        dpre = (mm_nt(e, w.up[...]) * slope[r, :]).astype(BF)
        dpre_all[r, :] = dpre
        add(DOWN_BIAS, dpre.astype(F32))
        dinner[r, :] = (e32 + mm(dpre, w.down[...])).astype(BF)

    steps(rows // block, one)
    grads_up[0:MATRIX_ROWS, :] += mm_tn(act[...], low[...])
    grads_down[0:MATRIX_ROWS, :] += mm_tn(dpre_all[...], inner[...])


def ffn_backward(dreturned, win, wout, slope, dexp, dsecond):
    expand_back(dreturned, wout, slope, dexp)
    project_add(dexp, win, dsecond)


def expand_back(dreturned, wout, slope, dexp):
    def one(at):
        cols = span_of(at, 256)
        d = mm_nt(dreturned[...], wout[cols, :])
        dexp[:, cols] = d.astype(BF) * slope[:, cols]

    steps(wout.shape[0] // 256, one, FFN_BACKWARD)


def project_add(x, weight, out):
    def one(at):
        cols = span_of(at, 256)
        out[:, cols] += mm_nt(x[...], weight[cols, :])

    steps(weight.shape[0] // 256, one)


def input_backward(dpacked, qkv, dfirst, dentry):
    def one(at):
        cols = span_of(at, 256)
        d = mm_nt(dpacked[...], qkv[cols, :])
        dentry[:, cols] = (dfirst[:, cols].astype(F32) + d).astype(BF)

    steps(qkv.shape[0] // 256, one)


class Item(NamedTuple):
    make: Any
    ref: Any

    def start(self):
        self.make().start()

    def wait(self):
        self.make().wait()


class Call:
    def __init__(self, section, slots, base=0):
        self.slots, self.base = slots, base
        self.args, self.in_specs, self.in_names = [], [], []
        self.outs, self.out_specs, self.out_names = [], [], []
        self.scratch, self.scratch_names = [], []
        self.kinds = {}
        self.section = section
        self.flops = 0
        self.limit = VMEM_LIMIT

    def _add(self, name, array, spec):
        self.args.append(array)
        self.in_specs.append(spec)
        self.in_names.append(name)

    def _temp(self, name, shape):
        self.scratch.append(shape)
        self.scratch_names.append(name)

    def whole(self, **arrays):
        for name, array in arrays.items():
            zeros = (0,) * array.ndim
            self._add(name, array, pl.BlockSpec(array.shape, lambda i, s, zeros=zeros: zeros))

    def raw(self, **arrays):
        for name, array in arrays.items():
            self._add(name, array, ANY)

    def load(self, micro=False, depth=2, **arrays):
        for name, array in arrays.items():
            depth_of = min(depth, self.slots)
            self._add((name, 0), array, ANY)
            self._temp((name, 1), pltpu.VMEM((depth_of,) + array.shape[1:], array.dtype))
            self._temp((name, 2), pltpu.SemaphoreType.DMA((depth_of,)))
            self.kinds[name] = (0, depth_of, micro)

    def save(self, depth=2, **shapes):
        for name, (shape, dtype) in shapes.items():
            depth_of = min(depth, self.slots)
            self.outs.append(jax.ShapeDtypeStruct((self.slots,) + shape, dtype))
            self.out_specs.append(ANY)
            self.out_names.append((name, 0))
            self._temp((name, 1), pltpu.VMEM((depth_of,) + shape, dtype))
            self._temp((name, 2), pltpu.SemaphoreType.DMA((depth_of,)))
            self.kinds[name] = (1, depth_of, False)

    def out(self, **shapes):
        for name, (shape, dtype) in shapes.items():
            self.outs.append(jax.ShapeDtypeStruct(shape, dtype))
            self.out_specs.append(ANY)
            self.out_names.append(name)

    def blocks(self, **shapes):
        for name, (shape, dtype) in shapes.items():
            zeros = (0,) * len(shape)
            self.outs.append(jax.ShapeDtypeStruct(shape, dtype))
            self.out_specs.append(pl.BlockSpec(shape, lambda i, s, zeros=zeros: zeros))
            self.out_names.append(name)

    def temp(self, **shapes):
        for name, (shape, dtype) in shapes.items():
            self._temp(name, pltpu.VMEM(shape, dtype))

    def sems(self, **counts):
        for name, count in counts.items():
            self._temp(name, pltpu.SemaphoreType.DMA(count if isinstance(count, tuple) else (count,)))

    def run(self, body, name):
        names = self.in_names + self.out_names + self.scratch_names
        slots, base = self.slots, self.base

        def kernel(section, *refs):
            step = pl.program_id(0) if slots > 1 else 0
            ref = dict(zip(names, refs))
            r = SimpleNamespace(**{n: v for n, v in ref.items() if isinstance(n, str)})
            r.step, r.section = step, section[0]

            def level_in(which, slot):
                number = PLAN[which][base]
                for other in range(1, slots):
                    number = jnp.where(slot == other, PLAN[which][base + other], number)
                return number

            def level(slot):
                return jnp.where(r.section == 0, level_in(0, slot), level_in(1, slot))

            def copy(name, slot):
                kind, depth, micro = self.kinds[name]
                at = slot if depth > 1 else 0
                near = ref[name, 1].at[at]
                if kind == 0:
                    far = ref[name, 0].at[level(slot) if micro else base + slot]
                    pair = (far, near)
                else:
                    pair = (near, ref[name, 0].at[slot])
                return Item(lambda: pltpu.make_async_copy(*pair, ref[name, 2].at[at]), near)

            def start(*which):
                for n in which:
                    copy(n, step).start()

            def wait(*which):
                for n in which:
                    copy(n, step).wait()

            def at_first(act):
                if slots > 1:
                    pl.when(step == 0)(act)
                else:
                    act()

            def at_last(act):
                if slots > 1:
                    pl.when(step == slots - 1)(act)
                else:
                    act()

            r.level_of, r.level = level, level(step)
            r.copy, r.start, r.wait, r.at_first, r.at_last = copy, start, wait, at_first, at_last
            for n, (kind, depth, micro) in self.kinds.items():
                setattr(r, n, ref[n, 1].at[step if depth > 1 else 0])
                setattr(r, "all_" + n, (ref[n, 0], ref[n, 1]))
            body(r)

        results = pl.pallas_call(
            kernel,
            out_shape=self.outs,
            grid_spec=pltpu.PrefetchScalarGridSpec(
                num_scalar_prefetch=1,
                grid=(slots,),
                in_specs=self.in_specs,
                out_specs=self.out_specs,
                scratch_shapes=self.scratch,
            ),
            compiler_params=pltpu.CompilerParams(vmem_limit_bytes=self.limit),
            cost_estimate=pl.CostEstimate(
                flops=self.flops * slots, bytes_accessed=1 << 20, transcendentals=0
            ),
            name=name,
        )(self.section, *self.args)
        return SimpleNamespace(
            **{n[0] if isinstance(n, tuple) else n: v for n, v in zip(self.out_names, results)}
        )


class Fill:
    def __init__(self, own, got, target, sems, mine, pieces=1, dim=0):
        self.sources, self.target, self.sems, self.mine = (own, got), target, sems, mine
        self.pieces, self.dim = pieces, dim

    def _copy(self, source, piece):
        source = self.sources[source]
        if self.pieces == 1:
            return pltpu.make_async_copy(source, self.target, self.sems.at[0])
        size = self.target.shape[self.dim] // self.pieces
        cut = tuple(
            pl.ds(piece * size, size) if at == self.dim else slice(None)
            for at in range(len(self.target.shape))
        )
        return pltpu.make_async_copy(source.at[cut], self.target.at[cut], self.sems.at[piece])

    def start(self):
        for source, chosen_one in enumerate((self.mine, jnp.logical_not(self.mine))):

            @pl.when(chosen_one)
            def _():
                for piece in range(self.pieces):
                    self._copy(source, piece).start()

    def wait(self, piece=None):
        for at in range(self.pieces) if piece is None else (piece,):
            self._copy(0, at).wait()


def zero(*refs):
    for ref in refs:
        ref[...] = jnp.zeros_like(ref)


def valid_row(valid, level):
    row = valid[0:1, :]
    for other in range(1, valid.shape[0]):
        row = jnp.where(level == other, valid[other : other + 1, :], row)
    return row


def live_column(valid, level, live):
    row = jnp.where(valid_row(valid, level) > 0, 1.0, 0.0)
    row = jnp.broadcast_to(row, (8, row.shape[1])).astype(BF)
    live[...] = mm_tn(row, jnp.full((8, 128), 0.125, BF))[:, 0:1]


def adapter_of(mats, vecs, which):
    vec = vecs.at[which]
    return Adapter(
        mats.at[2 * which], vec[0:1, 0:64], mats.at[2 * which + 1], vec[1:2, :], vec[2:3, :], vec[3:4, :]
    )


def portions_shape(rows, width):
    return ((width // 128, rows, 2 * rows), BF)


def attn_saved(rows, width, hidden):
    return dict(
        packed=((rows, 3 * width), BF), context=((rows, width), BF), linv=((rows, width), BF)
    )


def norm_saved(rows, width):
    return dict(
        attended=((rows, width), BF),
        act1=((rows, 64), BF),
        slope1=((rows, 64), F32),
        std1=((rows, width), BF),
        scale1=((rows, 1), F32),
    )


def ffn_saved(rows, width, hidden):
    return dict(
        slope=((rows, hidden), BF),
        returned=((rows, width), BF),
        act2=((rows, 64), BF),
        slope2=((rows, 64), F32),
        std2=((rows, width), BF),
        scale2=((rows, 1), F32),
    )


STAT_ROWS = 8


def pair_copy(source, target, sems, pair, length):
    lanes = pl.ds(0, 2 * length)
    return pltpu.make_async_copy(
        source.at[pair, :, lanes], target.at[pair, :, lanes], sems.at[pair]
    )


def first_attn_forward(section, tokens, valid, own, got, sizes, slots):
    rows, width, hidden = sizes
    pairs = width // 128
    call = Call(section, slots)
    call.load(micro=True, h=tokens)
    call.whole(valid=valid)
    call.raw(own=own.qkv, got=got.qkv, own_out=own.out, got_out=got.out)
    call.raw(own_mats=own.mats, got_mats=got.mats, own_vecs=own.vecs, got_vecs=got.vecs)
    call.save(**attn_saved(*sizes), **norm_saved(rows, width), middle=((rows, width), BF))
    shape, dtype = portions_shape(rows, width)
    call.out(portions=((slots,) + shape, dtype))
    call.blocks(stats=((2, width), F32))
    call.temp(
        held=((slots,) + shape, dtype),
        live=((rows, 1), F32),
        bias=((rows, 256), F32),
        qkv=(own.qkv.shape, BF),
        out=(own.out.shape, BF),
        mats=(own.mats.shape, BF),
        vecs=(own.vecs.shape, F32),
    )
    call.sems(qkv_sems=3, out_sems=1, mats_sems=1, vecs_sems=1, pair_sems=(slots, pairs))
    call.flops = 2 * rows * width * width * 12

    def body(r):
        mine = r.section == 0
        qkv = Fill(r.own, r.got, r.qkv, r.qkv_sems, mine, 3, 2)
        out = Fill(r.own_out, r.got_out, r.out, r.out_sems, mine)
        mats = Fill(r.own_mats, r.got_mats, r.mats, r.mats_sems, mine)
        vecs = Fill(r.own_vecs, r.got_vecs, r.vecs, r.vecs_sems, mine)

        def begin():
            r.copy("h", 0).start()
            qkv.start()
            zero(r.stats)

        def go_on():
            for item in (out, mats, vecs):
                item.start()
            for slot in range(1, slots):
                r.copy("h", slot).start()

        r.at_first(begin)
        live_column(r.valid, r.level, r.live)
        r.wait("h")
        qkv_phase(r.h, r.qkv.at[0], r.packed, lambda at: at % 3 or r.at_first(lambda: qkv.wait(at // 3)))
        r.at_first(go_on)
        r.start("packed")

        def pair_copy_of(slot, pair, length):
            return pair_copy(r.held.at[slot], r.portions.at[slot], r.pair_sems.at[slot], pair, length)

        attention_forward(
            r.level, r.valid, r.bias, r.packed, r.context, r.held.at[r.step], r.linv,
            lambda pair, length: pair_copy_of(r.step, pair, length).start(),
        )
        r.start("context", "linv")
        r.at_first(lambda: [item.wait() for item in (out, mats, vecs)] and None)
        project(r.context, r.out.at[0], r.attended)
        r.start("attended")
        saved = (r.act1, r.slope1, r.std1, r.scale1)
        adapter_norm(
            r.h, r.attended, r.live, adapter_of(r.mats, r.vecs, 0), saved, r.middle, r.stats
        )
        r.start("middle", *(n for n in norm_saved(rows, width) if n != "attended"))

        def finish():
            for slot in range(slots):
                for name in ("middle", *attn_saved(*sizes), *norm_saved(rows, width)):
                    r.copy(name, slot).wait()

                def waits(length):
                    for pair in range(pairs):
                        pair_copy_of(slot, pair, length).wait()

                by_level(r.level_of(slot), waits)

        r.at_last(finish)

    return call.run(body, "first_attn")


STAGE_ATTN0, STAGE_FFN0, STAGE_ATTN1, STAGE_FFN1 = range(4)


def middle_part(section, kept, cotangent, valid, own, got, sizes, slots):
    rows, width, hidden = sizes
    call = Call(section, slots)
    row = ((rows, width), BF)
    call.raw(base=kept.middle, cotangent=cotangent, **{"far_" + n: getattr(kept, n) for n in norm_saved(rows, width)})
    call.whole(valid=valid, stats=kept.stats)
    for name in ("qkv", "out", "win", "wout", "mats", "vecs"):
        call.raw(**{"own_" + name: getattr(own, name), "got_" + name: getattr(got, name)})
    call.temp(
        qkv=(own.qkv.shape, BF),
        win=(own.win.shape, BF),
        wout=(own.wout.shape, BF),
        outs=((2,) + own.out.shape, BF),
        mats=((2,) + own.mats.shape, BF),
        vecs=((2,) + own.vecs.shape, F32),
    )
    call.sems(win_sems=4, wout_sems=1, weight_sems=(8, 1), base_sems=1, up_sems=1, norm_sems=5)
    call.save(depth=1, result=row, dfirst0=row, dcontext0=row)
    grad_shape = (4, BLOCK_ROWS, width)
    call.temp(grads=((8,) + grad_shape[1:], F32))
    call.blocks(keep=(grad_shape, BF), send=(grad_shape, BF))
    call.temp(**attn_saved(*sizes))
    call.temp(
        attended=((4,) + row[0], BF),
        act1=((4, rows, 64), BF),
        slope1=((4, rows, 64), F32),
        std1=((4,) + row[0], BF),
        scale1=((4, rows, 1), F32),
        slope=((2, rows, hidden), BF),
        chain=((3,) + row[0], BF),
        sums=((4, 2, width), F32),
        up=row,
        held=portions_shape(rows, width),
        live=((rows, 1), F32),
        bias=((rows, 256), F32),
        wide=((rows, hidden), BF),
        dsum=((rows, width), F32),
        low=row,
        dpre=((rows, 64), BF),
        dinner=row,
    )
    call.flops = 12 * rows * width * (4 * width + 2 * hidden)
    norms = tuple(norm_saved(rows, width))

    def body(r):
        first, second = r.section == 0, r.section == 1

        def fill(name, target, at, mine):
            return Fill(
                getattr(r, "own_" + name), getattr(r, "got_" + name), target, r.weight_sems.at[at], mine
            )

        qkv, out1 = fill("qkv", r.qkv, 0, second), fill("out", r.outs.at[1], 1, second)
        mats1, vecs1 = fill("mats", r.mats.at[1], 2, second), fill("vecs", r.vecs.at[1], 3, second)
        out0 = fill("out", r.outs.at[0], 4, first)
        mats0, vecs0 = fill("mats", r.mats.at[0], 5, first), fill("vecs", r.vecs.at[0], 6, first)
        win0, win1 = (Fill(r.own_win, r.got_win, r.win, r.win_sems, m, 4, 2) for m in (first, second))
        wout0, wout1 = (Fill(r.own_wout, r.got_wout, r.wout, r.wout_sems, m) for m in (first, second))

        def base_copy(slot):
            return pltpu.make_async_copy(r.base.at[slot], r.chain.at[0], r.base_sems.at[0])

        def slot_copies():
            copies = [pltpu.make_async_copy(r.cotangent.at[r.level], r.up, r.up_sems.at[0])]
            for at, name in enumerate(norms):
                copies.append(
                    pltpu.make_async_copy(
                        getattr(r, "far_" + name).at[r.step], getattr(r, name).at[0], r.norm_sems.at[at]
                    )
                )
            return copies

        def begin():
            for item in (mats0, vecs0):
                item.start()
            base_copy(0).start()
            for item in (win0, wout0):
                item.start()
            zero(r.grads, r.sums)
            for item in (mats0, vecs0, win0, wout0):
                item.wait()
            for item in (qkv, out1, mats1, vecs1, out0):
                item.start()

        def later(act):
            pl.when(r.step > 0)(act)

        r.at_first(begin)
        for item in slot_copies():
            item.start()
        live_column(r.valid, r.level, r.live)
        base_copy(r.step).wait()
        later(lambda: r.copy("result", r.step - 1).wait())

        def saved_of(stage):
            return tuple(getattr(r, n).at[stage] for n in ("act1", "slope1", "std1", "scale1"))

        def adapter_at(stage):
            return adapter_of(r.mats.at[stage // 2], r.vecs.at[stage // 2], stage % 2)

        def forward(at, carry):
            stage = at + 1
            inner = r.attended.at[stage]
            here = r.chain.at[at]

            @pl.when(at == 1)
            def _():
                win1.start()
                wout1.start()
                for item in (qkv, out1, mats1, vecs1):
                    r.at_first(item.wait)
                qkv_phase(here, r.qkv.at[0], r.packed)
                attention_forward(r.level, r.valid, r.bias, r.packed, r.context, r.held, r.linv)
                project(r.context, r.outs.at[1, 0], inner)

            @pl.when(at != 1)
            def _():
                @pl.when(at == 2)
                def _():
                    win1.wait()
                    wout1.wait()

                ffn_forward(here, r.win.at[0], r.wout.at[0], r.wide, r.slope.at[stage // 2], inner)

            def norm(target):
                adapter_norm(
                    here, inner, r.live, adapter_at(stage), saved_of(stage), target, r.sums.at[stage]
                )

            norm(r.chain.at[lax.rem(at + 1, 3)])
            return carry

        lax.fori_loop(0, 3, forward, 0)
        r.result[...] = r.chain[0]
        r.start("result")

        @pl.when(r.step + 1 < slots)
        def _():
            base_copy(r.step + 1).start()

        for item in slot_copies():
            item.wait()

        def backward(at, carry):
            stage = 3 - at
            inner = r.attended.at[stage]

            @pl.when(stage % 2 == 1)
            def _():
                r.dsum[...] = r.up[...].astype(F32)

            norm_adapter_back(
                r.dsum, saved_of(stage), inner, adapter_at(stage), r.low, r.dpre, r.dinner,
                r.grads.at[2 * stage], r.grads.at[2 * stage + 1],
            )

            @pl.when(stage % 2 == 1)
            def _():
                @pl.when(at == 2)
                def _():
                    wout0.wait()
                    win0.wait()

                ffn_backward(r.dinner, r.win.at[0], r.wout.at[0], r.slope.at[stage // 2], r.wide, r.dsum)

            @pl.when(stage % 2 == 0)
            def _():
                @pl.when(at == 3)
                def _():
                    r.at_first(out0.wait)
                    later(lambda: r.copy("dfirst0", r.step - 1).wait())

                @pl.when(at == 1)
                def _():
                    wout0.start()
                    win0.start()
                    later(lambda: r.copy("dcontext0", r.step - 1).wait())

                project_back(r.dinner, r.outs.at[stage // 2, 0], r.dcontext0)

                @pl.when(at == 1)
                def _():
                    attention_backward(
                        r.level, r.packed, r.context, r.held, r.linv, r.dcontext0, r.packed
                    )
                    input_backward(r.packed, r.qkv.at[0], r.dsum, r.up)

            return carry

        lax.fori_loop(0, 4, backward, 0)
        r.dfirst0[...] = r.dsum[...].astype(BF)
        r.start("dfirst0", "dcontext0")

        def finish():
            r.wait("result", "dfirst0", "dcontext0")
            for layer in range(2):
                attn, ffn = r.sums.at[2 * layer], r.sums.at[2 * layer + 1]
                target = r.grads.at[4 * layer + ATTN_UP]
                if layer == 0:
                    attn = r.stats
                target[STATS : STATS + 1, :] = attn[0:1, :]
                target[STATS + 1 : STATS + 3, :] = ffn[...]
                count = jnp.zeros((1, 1), F32)
                for slot in range(slots):
                    row = jnp.where(valid_row(r.valid, r.level_of(slot)) > 0, 1.0, 0.0)
                    count += jnp.sum(row, axis=1, keepdims=True)
                target[STATS + 3 : STATS + 4, :] = jnp.broadcast_to(count, (1, width))
            for block in range(4):
                r.keep[block] = r.grads[4 * r.section + block].astype(BF)
                r.send[block] = r.grads[4 - 4 * r.section + block].astype(BF)

        r.at_last(finish)

    return call.run(body, "middle_part")


def first_attn_backward(section, back, there, kept, own, got, sizes, slots):
    rows, width, hidden = sizes
    pairs = width // 128
    call = Call(section, slots)
    call.load(packed=kept.packed, dcontext=back.dcontext0, context=kept.context, linv=kept.linv)
    call.load(dfirst=back.dfirst0)
    call.raw(portions=kept.portions, own=own.qkv, got=got.qkv, here=back.result, there=there)
    call.out(input_grad=((slots, rows, width), BF), result=((2 * slots, rows, width), BF))
    shape, dtype = portions_shape(rows, width)
    call.temp(
        held=((slots,) + shape, dtype),
        qkv=(own.qkv.shape, BF),
        stage=((2 * slots, rows, width), BF),
        dentry=((slots, rows, width), BF),
    )
    call.sems(
        qkv_sems=3, pair_sems=(slots, pairs), in_sems=2 * slots, out_sems=2 * slots, grad_sems=slots
    )
    call.flops = 2 * rows * width * width * 12

    def body(r):
        fill = Fill(r.own, r.got, r.qkv, r.qkv_sems, r.section == 0, 3, 1)

        def pair_copy_of(slot, pair, length):
            return pair_copy(r.portions.at[slot], r.held.at[slot], r.pair_sems.at[slot], pair, length)

        loads = ("packed", "dcontext", "context", "linv")
        ins, outs = [], []
        for at in range(slots):
            mine, other = (jnp.where(r.section == 0, PLAN[a][at], PLAN[1 - a][at]) for a in range(2))
            for source, target in ((r.here, mine), (r.there, other)):
                n = len(ins)
                ins.append(pltpu.make_async_copy(source.at[at], r.stage.at[n], r.in_sems.at[n]))
                outs.append(
                    pltpu.make_async_copy(r.stage.at[n], r.result.at[target], r.out_sems.at[n])
                )

        def start_pairs(slot, some):
            def starts(length):
                for pair in some:
                    pair_copy_of(slot, pair, length).start()

            by_level(r.level_of(slot), starts)

        def begin():
            for name in loads:
                r.copy(name, 0).start()
            start_pairs(0, range(2))

        def go_on():
            start_pairs(0, range(2, pairs))
            fill.start()
            r.copy("dfirst", 0).start()
            for slot in range(1, slots):
                for name in loads:
                    r.copy(name, slot).start()
                start_pairs(slot, range(pairs))
                r.copy("dfirst", slot).start()
            for item in ins:
                item.start()

        def grad_copy(slot):
            target = jnp.where(r.level_of(slot) % slots == 0, 0, 1)
            return pltpu.make_async_copy(
                r.dentry.at[slot], r.input_grad.at[target], r.grad_sems.at[slot]
            )

        r.at_first(begin)
        r.wait(*loads)
        r.at_first(go_on)
        attention_backward(
            r.level, r.packed, r.context, r.held.at[r.step], r.linv, r.dcontext, r.packed,
            r.step, pair_copy_of,
        )
        r.wait("dfirst")
        r.at_first(fill.wait)
        input_backward(r.packed, r.qkv.at[0], r.dfirst, r.dentry.at[r.step])
        grad_copy(r.step).start()

        def pass_on():
            for come, go in zip(ins, outs):
                come.wait()
                go.start()

        def finish():
            for slot in range(slots):
                grad_copy(slot).wait()
            for item in outs:
                item.wait()

        r.at_first(pass_on)
        r.at_last(finish)

    return call.run(body, "attn_back")


def packed_small(mats, vecs):
    width = mats[0].shape[-1]

    def kernel(*refs):
        sources, (out_mats, out_vecs) = refs[:-2], refs[-2:]
        for at in range(4):
            out_mats[at] = sources[at][0]
        out_vecs[...] = jnp.zeros_like(out_vecs)
        for at, ref in enumerate(sources[4:]):
            out_vecs[at // 4, at % 4 : at % 4 + 1, 0 : ref.shape[1]] = ref[...]

    return pl.pallas_call(
        kernel,
        out_shape=(
            jax.ShapeDtypeStruct((4, 64, width), BF),
            jax.ShapeDtypeStruct((2, 4, width), F32),
        ),
        compiler_params=pltpu.CompilerParams(vmem_limit_bytes=62 << 20),
        name="pack",
    )(*mats, *vecs)


def unpacked(quarters, member):
    width = quarters[0].shape[-1]
    matrix = jax.ShapeDtypeStruct((1, MATRIX_ROWS, width), F32)
    vector = jax.ShapeDtypeStruct((1, width), F32)
    small = jax.ShapeDtypeStruct((1, 64), F32)
    group = (matrix, small, matrix, vector, vector, vector)

    def kernel(member, *refs):
        sources, outs = refs[:4], refs[4:]

        def block(at):
            picked = sources[0][...]
            for d in (1, 2, 3):
                picked = jnp.where((member[0] ^ at) == d, sources[d][...], picked)
            return picked.astype(F32)

        for down, up, (mat_down, down_bias, mat_up, up_bias, gain, bias) in (
            (ATTN_DOWN, ATTN_UP, outs[:6]),
            (FFN_DOWN, FFN_UP, outs[6:12]),
        ):
            down, up = block(down), block(up)
            mat_down[0] = down[:MATRIX_ROWS]
            mat_up[0] = up[:MATRIX_ROWS]
            for row, target in ((UP_BIAS, up_bias), (GAIN, gain), (BIAS, bias), (DOWN_BIAS, down_bias)):
                target[...] = down[row : row + 1, : target.shape[1]]
        sums = block(ATTN_UP)[STATS : STATS + STAT_ROWS]
        means = jnp.sum(sums, axis=1, keepdims=True) / (sums[3:4, 0:1] * width)
        lane = lax.broadcasted_iota(jnp.int32, (1, 3), 1)
        picked = jnp.where(lane == 0, means[0:1], jnp.where(lane == 1, means[1:2], means[2:3]))
        outs[12][...] = jnp.sqrt(picked)

    vmem = pl.BlockSpec(memory_space=pltpu.VMEM)
    outs = pl.pallas_call(
        kernel,
        in_specs=[pl.BlockSpec(memory_space=pltpu.SMEM)] + [vmem] * 4,
        out_shape=group * 2 + (jax.ShapeDtypeStruct((1, 3), F32),),
        compiler_params=pltpu.CompilerParams(vmem_limit_bytes=SMALL_LIMIT),
        name="unpack",
    )(member.astype(jnp.int32).reshape(1), *quarters)
    outs = list(outs)
    for at in (0, 6):
        outs[at] = jnp.swapaxes(outs[at], 1, 2)
    return tuple(outs)


def swap(value):
    return lax.ppermute(value, "section", [(0, 1), (1, 0)])


def after(value, *others):
    return lax.optimization_barrier((value,) + others)[0]


def exchanged(value, bits):
    count = lax.axis_size("dp")
    return lax.ppermute(value, "dp", [(at, at ^ bits) for at in range(count)])


def summed_quarters(parts, before_last):
    mine, count = lax.axis_index("dp"), lax.axis_size("dp")
    member = mine & 3

    def quarter(d):
        first, second = (lax.dynamic_index_in_dim(v, member ^ d, 0, keepdims=False) for v in parts)
        return first + second

    def together(own, a, b, c):
        own, a, b, c = (v.astype(F32) for v in (own, a, b, c))
        return ((own + a) + (b + c)).astype(BF)

    total = together(quarter(0), *(exchanged(quarter(d), d) for d in (1, 2, 3)))
    bit = 4
    while bit < count:
        total = total + exchanged(total, bit)
        bit *= 2
    total = after(total, before_last)
    return [total] + [exchanged(total, d) for d in (1, 2, 3)], member


def body(
    tokens, valid, cotangent, qkv, out, win, wout,
    attn_down, attn_down_bias, attn_up, attn_up_bias, gain1, bias1,
    ffn_down, ffn_down_bias, ffn_up, ffn_up_bias, gain2, bias2,
):
    section = lax.axis_index("section")
    micro_count, rows, width = tokens.shape
    sizes = (rows, width, win.shape[-1])
    slots = micro_count // 2
    mats, vecs = packed_small(
        (jnp.swapaxes(attn_down, 1, 2), attn_up, jnp.swapaxes(ffn_down, 1, 2), ffn_up),
        (attn_down_bias, attn_up_bias, gain1, bias1, ffn_down_bias, ffn_up_bias, gain2, bias2),
    )
    own = Layer(qkv, out, win, wout, mats, vecs)
    early = [swap(v) for v in (qkv, out, mats, vecs)]
    got_qkv, got_out, got_mats, got_vecs = early
    got_win, got_wout = (swap(after(v, *early)) for v in (win, wout))
    got = Layer(got_qkv, got_out, got_win, got_wout, got_mats, got_vecs)
    where = section.astype(jnp.int32).reshape(1)

    kept = first_attn_forward(where, tokens, valid, own, got, sizes, slots)
    back = middle_part(where, kept, cotangent, valid, own, got, sizes, slots)

    got_grads = swap(back.send)
    there = swap(after(back.result, got_grads))
    quarters, member = summed_quarters((back.keep, got_grads), there)
    last = first_attn_backward(where, back, there, kept, own, got, sizes, slots)
    small = unpacked([quarters[0]] + [after(v, last.input_grad) for v in quarters[1:]], member)
    return (last.result, last.input_grad) + small


def solution(mesh):
    rows = P(None, "dp", None)
    matrix, vector = P("section", None, None), P("section", None)
    weights = (matrix, vector, matrix, vector, vector, vector)
    return jax.shard_map(
        body,
        mesh=mesh,
        in_specs=(rows, P(None, "dp"), rows) + (matrix,) * 4 + weights * 2,
        out_specs=(rows, P("section", "dp", None)) + weights * 2 + (vector,),
        check_vma=False,
    )
```

```python
import math
from types import SimpleNamespace
from typing import Any, NamedTuple

import jax
import jax.numpy as jnp
from jax import lax
from jax.experimental import pallas as pl
from jax.experimental.pallas import tpu as pltpu
from jax.sharding import PartitionSpec as P

NEGATIVE = -1e30
EPSILON = 1e-12
ROOT_HALF = 0.7071067811865476
INV_ROOT_TAU = 0.3989422804014327
LOG2E = 1.4426950408889634

PLAN = ((0, 1), (3, 2))

BF = jnp.bfloat16
F32 = jnp.float32
ANY = pl.BlockSpec(memory_space=pl.ANY)
VMEM_LIMIT = 60 << 20
SMALL_LIMIT = 16 << 20

ATTN_DOWN, ATTN_UP, FFN_DOWN, FFN_UP = range(4)
MATRIX_ROWS, BLOCK_ROWS = 64, 72
UP_BIAS, GAIN, BIAS, DOWN_BIAS = range(64, 68)
STATS = 64


class Layer(NamedTuple):
    qkv: Any
    out: Any
    win: Any
    wout: Any
    mats: Any
    vecs: Any


class Adapter(NamedTuple):
    down: Any
    down_bias: Any
    up: Any
    up_bias: Any
    gain: Any
    bias: Any


def mm(a, b):
    return jnp.dot(a, b, preferred_element_type=F32)


def mm_nt(a, b):
    return lax.dot_general(a, b, (((1,), (1,)), ((), ())), preferred_element_type=F32)


def mm_tn(a, b):
    return lax.dot_general(a, b, (((0,), (0,)), ((), ())), preferred_element_type=F32)


def span_of(index, size, base=0):
    start = index * size + base
    return pl.ds(start if isinstance(index, int) else pl.multiple_of(start, size), size)


def steps(count, body, unroll=None):
    if unroll is None or unroll >= count:
        for at in range(count):
            body(at)
        return

    def some(group, carry):
        for at in range(unroll):
            body(group * unroll + at)
        return carry

    lax.fori_loop(0, count // unroll, some, 0)


PAIRS_FORWARD, PAIRS_BACKWARD = 3, 1
FFN_FORWARD, FFN_BACKWARD = 12, 12


def gelu_both(z):
    cdf = 0.5 + 0.5 * lax.erf(z * ROOT_HALF)
    bell = jnp.exp2(z * z * (-0.5 * LOG2E))
    return z * cdf, cdf + (z * INV_ROOT_TAU) * bell


def nothing(at):
    pass


def qkv_phase(h, qkv, packed, need=nothing):
    width = h.shape[-1]

    def one(at):
        need(at)
        cols = span_of(at, 256)
        y = mm(h[...], qkv[:, cols])
        if at < width // 256:
            y = y * 0.125
        packed[:, cols] = y.astype(BF)

    steps(qkv.shape[1] // 256, one)


def lane_half(shape):
    return lax.broadcasted_iota(jnp.int32, shape, len(shape) - 1) < 64


def split_pair(pair, first):
    zero = jnp.zeros_like(pair)
    return jnp.concatenate([jnp.where(first, pair, zero), jnp.where(first, zero, pair)], axis=0)


def values_and_ones(v2, first):
    one = jnp.ones_like(v2)
    return jnp.concatenate([split_pair(v2, first), split_pair(one, first)], axis=1)


def by_level(level, run):
    @pl.when(level <= 2)
    def _():
        run(256)

    @pl.when(level == 3)
    def _():
        run(512)


def pair_ignored(pair, length):
    pass


def attention_forward(level, valid, bias, packed, context, portions, linv, done=pair_ignored):
    rows, width = context.shape
    query = 256

    def run(length):
        live = valid_row(valid, level)
        barred = jnp.where(live > 0, 0.0, NEGATIVE)
        if length == 256:
            shift = 6 + level
            a = lax.broadcasted_iota(jnp.int32, (256, 256), 0) >> shift
            b = lax.broadcasted_iota(jnp.int32, (256, 256), 1) >> shift
            apart = jnp.where(a == b, 0.0, NEGATIVE)
            for block in range(rows // 256):
                bias[span_of(block, 256), :] = apart + barred[:, block * 256 : (block + 1) * 256]
        first = lane_half((length, 128))

        def pair(at):
            lanes = span_of(at, 128)
            for block in range(rows // length):
                base = block * length
                k2 = packed[base : base + length, span_of(at, 128, width)]
                v2 = packed[base : base + length, span_of(at, 128, 2 * width)]
                kk = split_pair(k2, first)
                vv = values_and_ones(v2, first)
                for part in range(length // query):
                    at_rows = pl.ds(base + part * query, query)
                    scores = mm_nt(packed[at_rows, lanes], kk)
                    halves = []
                    for head in range(2):
                        s = scores[:, head * length : (head + 1) * length]
                        s = s + (bias[at_rows, :] if length == 256 else barred)
                        top = jnp.max(s, axis=-1, keepdims=True)
                        halves.append(jnp.exp2((s - top) * LOG2E).astype(BF))
                    p = jnp.concatenate(halves, axis=1)
                    portions[at, at_rows, 0 : 2 * length] = p
                    both = mm(p, vv)
                    inverse = 1.0 / both[:, 128:]
                    linv[at_rows, lanes] = inverse.astype(BF)
                    context[at_rows, lanes] = (both[:, :128] * inverse).astype(BF)
            done(at, length)

        steps(width // 128, pair, PAIRS_FORWARD)

    by_level(level, run)


def attention_backward(level, packed, context, portions, linv, dcontext, dpacked, slot=0, copy=None, short_pairs=1):
    rows, width = context.shape
    query = 256

    def run(length):
        first = lane_half((length, 128))

        def pair(at):
            if copy is not None:
                copy(slot, at, length).wait()
            lanes = span_of(at, 128)
            for block in range(rows // length):
                base = block * length
                whole = pl.ds(base, length)
                k2 = packed[whole, span_of(at, 128, width)]
                v2 = packed[whole, span_of(at, 128, 2 * width)]
                kk = split_pair(k2, first)
                vv = values_and_ones(v2, first)
                dk = None
                dv = None
                for part in range(length // query):
                    at_rows = pl.ds(base + part * query, query)
                    out = dcontext[at_rows, lanes].astype(F32) * linv[at_rows, lanes].astype(F32)
                    low = out.astype(BF)
                    both = jnp.concatenate(
                        [low, (-out * context[at_rows, lanes].astype(F32)).astype(BF)], axis=1
                    )
                    p = portions[at, at_rows, 0 : 2 * length]
                    ds = p * mm_nt(both, vv).astype(BF)
                    q2 = packed[at_rows, lanes]
                    dpacked[at_rows, lanes] = (mm(ds, kk) * 0.125).astype(BF)
                    more_k = mm_tn(ds, q2)
                    more_v = mm_tn(p, low)
                    dk = more_k if dk is None else dk + more_k
                    dv = more_v if dv is None else dv + more_v
                dk = jnp.where(first, dk[:length], dk[length:])
                dv = jnp.where(first, dv[:length], dv[length:])
                dpacked[whole, span_of(at, 128, width)] = dk.astype(BF)
                dpacked[whole, span_of(at, 128, 2 * width)] = dv.astype(BF)

        steps(width // 128, pair, short_pairs if length == 256 else PAIRS_BACKWARD)

    by_level(level, run)


def project(x, weight, out):
    def one(at):
        cols = span_of(at, 256)
        out[:, cols] = mm(x[...], weight[:, cols]).astype(BF)

    steps(out.shape[1] // 256, one)


def project_back(x, weight, out):
    def one(at):
        cols = span_of(at, 256)
        out[:, cols] = mm_nt(x[...], weight[cols, :]).astype(BF)

    steps(out.shape[1] // 256, one)


def adapter_norm(base, inner, live, w, saved, out, stats):
    act, slope, std, scale = saved
    rows, width = inner.shape
    block = 128

    def one(at):
        r = span_of(at, block)
        x = inner[r, :]
        pre = mm_nt(x, w.down[...]) + w.down_bias
        a, g = gelu_both(pre)
        a = a.astype(BF)
        act[r, :] = a
        slope[r, :] = g
        branch = x.astype(F32) + (mm(a, w.up[...]) + w.up_bias)
        total = base[r, :].astype(F32) + branch
        alive = live[r, :]
        stats[0:1, :] += jnp.sum(branch * branch * alive, axis=0, keepdims=True)
        mean = jnp.mean(total, axis=-1, keepdims=True)
        centered = total - mean
        variance = jnp.mean(centered * centered, axis=-1, keepdims=True)
        square = jnp.sum((variance + mean * mean) * alive, axis=0, keepdims=True)
        stats[1:2, :] += jnp.broadcast_to(square, (1, width))
        s = lax.rsqrt(variance + EPSILON)
        n = centered * s
        std[r, :] = n.astype(BF)
        scale[r, :] = s
        out[r, :] = (n * w.gain + w.bias).astype(BF)

    steps(rows // block, one)


def ffn_forward(middle, win, wout, act, slope, returned, need=nothing):
    need(0)
    expand(middle, win, act, slope)
    need(1)
    project(act, wout, returned)


def expand(middle, win, act, slope):

    def one(at):
        cols = span_of(at, 256)
        z = mm(middle[...], win[:, cols])
        a, g = gelu_both(z)
        act[:, cols] = a.astype(BF)
        slope[:, cols] = g.astype(BF)

    steps(win.shape[1] // 256, one, FFN_FORWARD)


def norm_adapter_back(dtotal, saved, inner, w, low, dpre_all, dinner, grads_down, grads_up):
    act, slope, std, scale = saved
    rows = inner.shape[0]
    block = 128

    def add(row, values):
        grads_down[row : row + 1, 0 : values.shape[1]] += jnp.sum(values, axis=0, keepdims=True)

    def one(at):
        r = span_of(at, block)
        g = dtotal[r, :]
        n = std[r, :].astype(F32)
        add(GAIN, g * n)
        add(BIAS, g)
        gg = g * w.gain
        m1 = jnp.mean(gg, axis=-1, keepdims=True)
        m2 = jnp.mean(gg * n, axis=-1, keepdims=True)
        d = scale[r, :] * (gg - m1 - n * m2)
        dtotal[r, :] = d
        e = d.astype(BF)
        low[r, :] = e
        e32 = e.astype(F32)
        add(UP_BIAS, e32)
        dpre = (mm_nt(e, w.up[...]) * slope[r, :]).astype(BF)
        dpre_all[r, :] = dpre
        add(DOWN_BIAS, dpre.astype(F32))
        dinner[r, :] = (e32 + mm(dpre, w.down[...])).astype(BF)

    steps(rows // block, one)
    grads_up[0:MATRIX_ROWS, :] += mm_tn(act[...], low[...])
    grads_down[0:MATRIX_ROWS, :] += mm_tn(dpre_all[...], inner[...])


def ffn_backward(dreturned, win, wout, slope, dexp, dsecond):
    expand_back(dreturned, wout, slope, dexp)
    project_add(dexp, win, dsecond)


def expand_back(dreturned, wout, slope, dexp):
    def one(at):
        cols = span_of(at, 256)
        d = mm_nt(dreturned[...], wout[cols, :])
        dexp[:, cols] = d.astype(BF) * slope[:, cols]

    steps(wout.shape[0] // 256, one, FFN_BACKWARD)


def project_add(x, weight, out):
    def one(at):
        cols = span_of(at, 256)
        out[:, cols] += mm_nt(x[...], weight[cols, :])

    steps(weight.shape[0] // 256, one)


def input_backward(dpacked, qkv, dfirst, dentry):
    def one(at):
        cols = span_of(at, 256)
        d = mm_nt(dpacked[...], qkv[cols, :])
        dentry[:, cols] = (dfirst[:, cols].astype(F32) + d).astype(BF)

    steps(qkv.shape[0] // 256, one)


class Item(NamedTuple):
    make: Any
    ref: Any

    def start(self):
        self.make().start()

    def wait(self):
        self.make().wait()


class Call:
    def __init__(self, section, slots, base=0):
        self.slots, self.base = slots, base
        self.args, self.in_specs, self.in_names = [], [], []
        self.outs, self.out_specs, self.out_names = [], [], []
        self.scratch, self.scratch_names = [], []
        self.kinds = {}
        self.section = section
        self.flops = 0
        self.limit = VMEM_LIMIT

    def _add(self, name, array, spec):
        self.args.append(array)
        self.in_specs.append(spec)
        self.in_names.append(name)

    def _temp(self, name, shape):
        self.scratch.append(shape)
        self.scratch_names.append(name)

    def whole(self, **arrays):
        for name, array in arrays.items():
            zeros = (0,) * array.ndim
            self._add(name, array, pl.BlockSpec(array.shape, lambda i, s, zeros=zeros: zeros))

    def raw(self, **arrays):
        for name, array in arrays.items():
            self._add(name, array, ANY)

    def load(self, micro=False, depth=2, **arrays):
        for name, array in arrays.items():
            depth_of = min(depth, self.slots)
            self._add((name, 0), array, ANY)
            self._temp((name, 1), pltpu.VMEM((depth_of,) + array.shape[1:], array.dtype))
            self._temp((name, 2), pltpu.SemaphoreType.DMA((depth_of,)))
            self.kinds[name] = (0, depth_of, micro)

    def save(self, depth=2, **shapes):
        for name, (shape, dtype) in shapes.items():
            depth_of = min(depth, self.slots)
            self.outs.append(jax.ShapeDtypeStruct((self.slots,) + shape, dtype))
            self.out_specs.append(ANY)
            self.out_names.append((name, 0))
            self._temp((name, 1), pltpu.VMEM((depth_of,) + shape, dtype))
            self._temp((name, 2), pltpu.SemaphoreType.DMA((depth_of,)))
            self.kinds[name] = (1, depth_of, False)

    def out(self, **shapes):
        for name, (shape, dtype) in shapes.items():
            self.outs.append(jax.ShapeDtypeStruct(shape, dtype))
            self.out_specs.append(ANY)
            self.out_names.append(name)

    def blocks(self, **shapes):
        for name, (shape, dtype) in shapes.items():
            zeros = (0,) * len(shape)
            self.outs.append(jax.ShapeDtypeStruct(shape, dtype))
            self.out_specs.append(pl.BlockSpec(shape, lambda i, s, zeros=zeros: zeros))
            self.out_names.append(name)

    def temp(self, **shapes):
        for name, (shape, dtype) in shapes.items():
            self._temp(name, pltpu.VMEM(shape, dtype))

    def sems(self, **counts):
        for name, count in counts.items():
            self._temp(name, pltpu.SemaphoreType.DMA(count if isinstance(count, tuple) else (count,)))

    def run(self, body, name):
        names = self.in_names + self.out_names + self.scratch_names
        slots, base = self.slots, self.base

        def kernel(section, *refs):
            step = pl.program_id(0) if slots > 1 else 0
            ref = dict(zip(names, refs))
            r = SimpleNamespace(**{n: v for n, v in ref.items() if isinstance(n, str)})
            r.step, r.section = step, section[0]

            def level_in(which, slot):
                number = PLAN[which][base]
                for other in range(1, slots):
                    number = jnp.where(slot == other, PLAN[which][base + other], number)
                return number

            def level(slot):
                return jnp.where(r.section == 0, level_in(0, slot), level_in(1, slot))

            def copy(name, slot):
                kind, depth, micro = self.kinds[name]
                at = slot if depth > 1 else 0
                near = ref[name, 1].at[at]
                if kind == 0:
                    far = ref[name, 0].at[level(slot) if micro else base + slot]
                    pair = (far, near)
                else:
                    pair = (near, ref[name, 0].at[slot])
                return Item(lambda: pltpu.make_async_copy(*pair, ref[name, 2].at[at]), near)

            def start(*which):
                for n in which:
                    copy(n, step).start()

            def wait(*which):
                for n in which:
                    copy(n, step).wait()

            def at_first(act):
                if slots > 1:
                    pl.when(step == 0)(act)
                else:
                    act()

            def at_last(act):
                if slots > 1:
                    pl.when(step == slots - 1)(act)
                else:
                    act()

            r.level_of, r.level = level, level(step)
            r.copy, r.start, r.wait, r.at_first, r.at_last = copy, start, wait, at_first, at_last
            for n, (kind, depth, micro) in self.kinds.items():
                setattr(r, n, ref[n, 1].at[step if depth > 1 else 0])
                setattr(r, "all_" + n, (ref[n, 0], ref[n, 1]))
            body(r)

        results = pl.pallas_call(
            kernel,
            out_shape=self.outs,
            grid_spec=pltpu.PrefetchScalarGridSpec(
                num_scalar_prefetch=1,
                grid=(slots,),
                in_specs=self.in_specs,
                out_specs=self.out_specs,
                scratch_shapes=self.scratch,
            ),
            compiler_params=pltpu.CompilerParams(vmem_limit_bytes=self.limit),
            cost_estimate=pl.CostEstimate(
                flops=self.flops * slots, bytes_accessed=1 << 20, transcendentals=0
            ),
            name=name,
        )(self.section, *self.args)
        return SimpleNamespace(
            **{n[0] if isinstance(n, tuple) else n: v for n, v in zip(self.out_names, results)}
        )


class Fill:
    def __init__(self, own, got, target, sems, mine, pieces=1, dim=0):
        self.sources, self.target, self.sems, self.mine = (own, got), target, sems, mine
        self.pieces, self.dim = pieces, dim

    def _copy(self, source, piece):
        source = self.sources[source]
        if self.pieces == 1:
            return pltpu.make_async_copy(source, self.target, self.sems.at[0])
        size = self.target.shape[self.dim] // self.pieces
        cut = tuple(
            pl.ds(piece * size, size) if at == self.dim else slice(None)
            for at in range(len(self.target.shape))
        )
        return pltpu.make_async_copy(source.at[cut], self.target.at[cut], self.sems.at[piece])

    def start(self):
        for source, chosen_one in enumerate((self.mine, jnp.logical_not(self.mine))):

            @pl.when(chosen_one)
            def _():
                for piece in range(self.pieces):
                    self._copy(source, piece).start()

    def wait(self, piece=None):
        for at in range(self.pieces) if piece is None else (piece,):
            self._copy(0, at).wait()


def zero(*refs):
    for ref in refs:
        ref[...] = jnp.zeros_like(ref)


def valid_row(valid, level):
    row = valid[0:1, :]
    for other in range(1, valid.shape[0]):
        row = jnp.where(level == other, valid[other : other + 1, :], row)
    return row


def live_column(valid, level, live):
    row = jnp.where(valid_row(valid, level) > 0, 1.0, 0.0)
    row = jnp.broadcast_to(row, (8, row.shape[1])).astype(BF)
    live[...] = mm_tn(row, jnp.full((8, 128), 0.125, BF))[:, 0:1]


def adapter_of(mats, vecs, which):
    vec = vecs.at[which]
    return Adapter(
        mats.at[2 * which], vec[0:1, 0:64], mats.at[2 * which + 1], vec[1:2, :], vec[2:3, :], vec[3:4, :]
    )


def portions_shape(rows, width):
    return ((width // 128, rows, 2 * rows), BF)


def attn_saved(rows, width, hidden):
    return dict(
        packed=((rows, 3 * width), BF), context=((rows, width), BF), linv=((rows, width), BF)
    )


def norm_saved(rows, width):
    return dict(
        attended=((rows, width), BF),
        act1=((rows, 64), BF),
        slope1=((rows, 64), F32),
        std1=((rows, width), BF),
        scale1=((rows, 1), F32),
    )


def ffn_saved(rows, width, hidden):
    return dict(
        slope=((rows, hidden), BF),
        returned=((rows, width), BF),
        act2=((rows, 64), BF),
        slope2=((rows, 64), F32),
        std2=((rows, width), BF),
        scale2=((rows, 1), F32),
    )


STAT_ROWS = 8


def pair_copy(source, target, sems, pair, length):
    lanes = pl.ds(0, 2 * length)
    return pltpu.make_async_copy(
        source.at[pair, :, lanes], target.at[pair, :, lanes], sems.at[pair]
    )


def first_attn_forward(section, tokens, valid, own, got, sizes, slots):
    rows, width, hidden = sizes
    pairs = width // 128
    call = Call(section, slots)
    call.load(micro=True, h=tokens)
    call.whole(valid=valid)
    call.raw(own=own.qkv, got=got.qkv, own_out=own.out, got_out=got.out)
    call.raw(own_mats=own.mats, got_mats=got.mats, own_vecs=own.vecs, got_vecs=got.vecs)
    call.save(**attn_saved(*sizes), **norm_saved(rows, width), middle=((rows, width), BF))
    shape, dtype = portions_shape(rows, width)
    call.out(portions=((slots,) + shape, dtype))
    call.blocks(stats=((2, width), F32))
    call.temp(
        held=((slots,) + shape, dtype),
        live=((rows, 1), F32),
        bias=((rows, 256), F32),
        qkv=(own.qkv.shape, BF),
        out=(own.out.shape, BF),
        mats=(own.mats.shape, BF),
        vecs=(own.vecs.shape, F32),
    )
    call.sems(qkv_sems=3, out_sems=1, mats_sems=1, vecs_sems=1, pair_sems=(slots, pairs))
    call.flops = 2 * rows * width * width * 12

    def body(r):
        mine = r.section == 0
        qkv = Fill(r.own, r.got, r.qkv, r.qkv_sems, mine, 3, 2)
        out = Fill(r.own_out, r.got_out, r.out, r.out_sems, mine)
        mats = Fill(r.own_mats, r.got_mats, r.mats, r.mats_sems, mine)
        vecs = Fill(r.own_vecs, r.got_vecs, r.vecs, r.vecs_sems, mine)

        def begin():
            r.copy("h", 0).start()
            qkv.start()
            zero(r.stats)

        def go_on():
            for item in (out, mats, vecs):
                item.start()
            for slot in range(1, slots):
                r.copy("h", slot).start()

        r.at_first(begin)
        live_column(r.valid, r.level, r.live)
        r.wait("h")
        qkv_phase(r.h, r.qkv.at[0], r.packed, lambda at: at % 3 or r.at_first(lambda: qkv.wait(at // 3)))
        r.at_first(go_on)
        r.start("packed")

        def pair_copy_of(slot, pair, length):
            return pair_copy(r.held.at[slot], r.portions.at[slot], r.pair_sems.at[slot], pair, length)

        attention_forward(
            r.level, r.valid, r.bias, r.packed, r.context, r.held.at[r.step], r.linv,
            lambda pair, length: pair_copy_of(r.step, pair, length).start(),
        )
        r.start("context", "linv")
        r.at_first(lambda: [item.wait() for item in (out, mats, vecs)] and None)
        project(r.context, r.out.at[0], r.attended)
        r.start("attended")
        saved = (r.act1, r.slope1, r.std1, r.scale1)
        adapter_norm(
            r.h, r.attended, r.live, adapter_of(r.mats, r.vecs, 0), saved, r.middle, r.stats
        )
        r.start("middle", *(n for n in norm_saved(rows, width) if n != "attended"))

        def finish():
            for slot in range(slots):
                for name in ("middle", *attn_saved(*sizes), *norm_saved(rows, width)):
                    r.copy(name, slot).wait()

                def waits(length):
                    for pair in range(pairs):
                        pair_copy_of(slot, pair, length).wait()

                by_level(r.level_of(slot), waits)

        r.at_last(finish)

    return call.run(body, "first_attn")


STAGE_ATTN0, STAGE_FFN0, STAGE_ATTN1, STAGE_FFN1 = range(4)


def middle_part(section, kept, cotangent, valid, own, got, sizes, slots):
    rows, width, hidden = sizes
    call = Call(section, slots)
    row = ((rows, width), BF)
    call.raw(base=kept.middle, cotangent=cotangent, **{"far_" + n: getattr(kept, n) for n in norm_saved(rows, width)})
    call.whole(valid=valid, stats=kept.stats)
    for name in ("qkv", "out", "win", "wout", "mats", "vecs"):
        call.raw(**{"own_" + name: getattr(own, name), "got_" + name: getattr(got, name)})
    call.temp(
        qkv=(own.qkv.shape, BF),
        win=(own.win.shape, BF),
        wout=(own.wout.shape, BF),
        outs=((2,) + own.out.shape, BF),
        mats=((2,) + own.mats.shape, BF),
        vecs=((2,) + own.vecs.shape, F32),
    )
    call.sems(win_sems=4, wout_sems=1, weight_sems=(8, 1), base_sems=1, up_sems=1, norm_sems=5)
    call.save(depth=1, result=row, dfirst0=row, dcontext0=row)
    grad_shape = (4, BLOCK_ROWS, width)
    call.temp(grads=((8,) + grad_shape[1:], F32))
    call.blocks(keep=(grad_shape, BF), send=(grad_shape, BF))
    call.temp(**attn_saved(*sizes))
    call.temp(
        attended=((4,) + row[0], BF),
        act1=((4, rows, 64), BF),
        slope1=((4, rows, 64), F32),
        std1=((4,) + row[0], BF),
        scale1=((4, rows, 1), F32),
        slope=((2, rows, hidden), BF),
        chain=((3,) + row[0], BF),
        sums=((4, 2, width), F32),
        up=row,
        held=portions_shape(rows, width),
        live=((rows, 1), F32),
        bias=((rows, 256), F32),
        wide=((rows, hidden), BF),
        dsum=((rows, width), F32),
        low=row,
        dpre=((rows, 64), BF),
        dinner=row,
    )
    call.flops = 12 * rows * width * (4 * width + 2 * hidden)
    norms = tuple(norm_saved(rows, width))

    def body(r):
        first, second = r.section == 0, r.section == 1

        def fill(name, target, at, mine):
            return Fill(
                getattr(r, "own_" + name), getattr(r, "got_" + name), target, r.weight_sems.at[at], mine
            )

        qkv, out1 = fill("qkv", r.qkv, 0, second), fill("out", r.outs.at[1], 1, second)
        mats1, vecs1 = fill("mats", r.mats.at[1], 2, second), fill("vecs", r.vecs.at[1], 3, second)
        out0 = fill("out", r.outs.at[0], 4, first)
        mats0, vecs0 = fill("mats", r.mats.at[0], 5, first), fill("vecs", r.vecs.at[0], 6, first)
        win0, win1 = (Fill(r.own_win, r.got_win, r.win, r.win_sems, m, 4, 2) for m in (first, second))
        wout0, wout1 = (Fill(r.own_wout, r.got_wout, r.wout, r.wout_sems, m) for m in (first, second))

        def base_copy(slot):
            return pltpu.make_async_copy(r.base.at[slot], r.chain.at[0], r.base_sems.at[0])

        def slot_copies():
            copies = [pltpu.make_async_copy(r.cotangent.at[r.level], r.up, r.up_sems.at[0])]
            for at, name in enumerate(norms):
                copies.append(
                    pltpu.make_async_copy(
                        getattr(r, "far_" + name).at[r.step], getattr(r, name).at[0], r.norm_sems.at[at]
                    )
                )
            return copies

        def begin():
            for item in (mats0, vecs0):
                item.start()
            base_copy(0).start()
            for item in (win0, wout0):
                item.start()
            zero(r.grads, r.sums)
            for item in (mats0, vecs0, win0, wout0):
                item.wait()
            for item in (qkv, out1, mats1, vecs1, out0):
                item.start()

        def later(act):
            pl.when(r.step > 0)(act)

        r.at_first(begin)
        for item in slot_copies():
            item.start()
        live_column(r.valid, r.level, r.live)
        base_copy(r.step).wait()
        later(lambda: r.copy("result", r.step - 1).wait())

        def saved_of(stage):
            return tuple(getattr(r, n).at[stage] for n in ("act1", "slope1", "std1", "scale1"))

        def adapter_at(stage):
            return adapter_of(r.mats.at[stage // 2], r.vecs.at[stage // 2], stage % 2)

        def forward(at, carry):
            stage = at + 1
            inner = r.attended.at[stage]
            here = r.chain.at[at]

            @pl.when(at == 1)
            def _():
                win1.start()
                wout1.start()
                for item in (qkv, out1, mats1, vecs1):
                    r.at_first(item.wait)
                qkv_phase(here, r.qkv.at[0], r.packed)
                attention_forward(r.level, r.valid, r.bias, r.packed, r.context, r.held, r.linv)
                project(r.context, r.outs.at[1, 0], inner)

            @pl.when(at != 1)
            def _():
                @pl.when(at == 2)
                def _():
                    win1.wait()
                    wout1.wait()

                ffn_forward(here, r.win.at[0], r.wout.at[0], r.wide, r.slope.at[stage // 2], inner)

            def norm(target):
                adapter_norm(
                    here, inner, r.live, adapter_at(stage), saved_of(stage), target, r.sums.at[stage]
                )

            norm(r.chain.at[lax.rem(at + 1, 3)])
            return carry

        lax.fori_loop(0, 3, forward, 0)
        r.result[...] = r.chain[0]
        r.start("result")

        @pl.when(r.step + 1 < slots)
        def _():
            base_copy(r.step + 1).start()

        for item in slot_copies():
            item.wait()

        def backward(at, carry):
            stage = 3 - at
            inner = r.attended.at[stage]

            @pl.when(stage % 2 == 1)
            def _():
                r.dsum[...] = r.up[...].astype(F32)

            norm_adapter_back(
                r.dsum, saved_of(stage), inner, adapter_at(stage), r.low, r.dpre, r.dinner,
                r.grads.at[2 * stage], r.grads.at[2 * stage + 1],
            )

            @pl.when(stage % 2 == 1)
            def _():
                @pl.when(at == 2)
                def _():
                    wout0.wait()
                    win0.wait()

                ffn_backward(r.dinner, r.win.at[0], r.wout.at[0], r.slope.at[stage // 2], r.wide, r.dsum)

            @pl.when(stage % 2 == 0)
            def _():
                @pl.when(at == 3)
                def _():
                    r.at_first(out0.wait)
                    later(lambda: r.copy("dfirst0", r.step - 1).wait())

                @pl.when(at == 1)
                def _():
                    wout0.start()
                    win0.start()
                    later(lambda: r.copy("dcontext0", r.step - 1).wait())

                project_back(r.dinner, r.outs.at[stage // 2, 0], r.dcontext0)

                @pl.when(at == 1)
                def _():
                    attention_backward(
                        r.level, r.packed, r.context, r.held, r.linv, r.dcontext0, r.packed,
                        short_pairs=2,
                    )
                    input_backward(r.packed, r.qkv.at[0], r.dsum, r.up)

            return carry

        lax.fori_loop(0, 4, backward, 0)
        r.dfirst0[...] = r.dsum[...].astype(BF)
        r.start("dfirst0", "dcontext0")

        def finish():
            r.wait("result", "dfirst0", "dcontext0")
            for layer in range(2):
                attn, ffn = r.sums.at[2 * layer], r.sums.at[2 * layer + 1]
                target = r.grads.at[4 * layer + ATTN_UP]
                if layer == 0:
                    attn = r.stats
                target[STATS : STATS + 1, :] = attn[0:1, :]
                target[STATS + 1 : STATS + 3, :] = ffn[...]
                count = jnp.zeros((1, 1), F32)
                for slot in range(slots):
                    row = jnp.where(valid_row(r.valid, r.level_of(slot)) > 0, 1.0, 0.0)
                    count += jnp.sum(row, axis=1, keepdims=True)
                target[STATS + 3 : STATS + 4, :] = jnp.broadcast_to(count, (1, width))
            for block in range(4):
                r.keep[block] = r.grads[4 * r.section + block].astype(BF)
                r.send[block] = r.grads[4 - 4 * r.section + block].astype(BF)

        r.at_last(finish)

    return call.run(body, "middle_part")


def first_attn_backward(section, back, there, kept, own, got, sizes, slots):
    rows, width, hidden = sizes
    pairs = width // 128
    call = Call(section, slots)
    call.load(packed=kept.packed, dcontext=back.dcontext0, context=kept.context, linv=kept.linv)
    call.load(dfirst=back.dfirst0)
    call.raw(portions=kept.portions, own=own.qkv, got=got.qkv, here=back.result, there=there)
    call.out(input_grad=((slots, rows, width), BF), result=((2 * slots, rows, width), BF))
    shape, dtype = portions_shape(rows, width)
    call.temp(
        held=((slots,) + shape, dtype),
        qkv=(own.qkv.shape, BF),
        stage=((2 * slots, rows, width), BF),
        dentry=((slots, rows, width), BF),
    )
    call.sems(
        qkv_sems=3, pair_sems=(slots, pairs), in_sems=2 * slots, out_sems=2 * slots, grad_sems=slots
    )
    call.flops = 2 * rows * width * width * 12

    def body(r):
        fill = Fill(r.own, r.got, r.qkv, r.qkv_sems, r.section == 0, 3, 1)

        def pair_copy_of(slot, pair, length):
            return pair_copy(r.portions.at[slot], r.held.at[slot], r.pair_sems.at[slot], pair, length)

        loads = ("packed", "dcontext", "context", "linv")
        ins, outs = [], []
        for at in range(slots):
            mine, other = (jnp.where(r.section == 0, PLAN[a][at], PLAN[1 - a][at]) for a in range(2))
            for source, target in ((r.here, mine), (r.there, other)):
                n = len(ins)
                ins.append(pltpu.make_async_copy(source.at[at], r.stage.at[n], r.in_sems.at[n]))
                outs.append(
                    pltpu.make_async_copy(r.stage.at[n], r.result.at[target], r.out_sems.at[n])
                )

        def start_pairs(slot, some):
            def starts(length):
                for pair in some:
                    pair_copy_of(slot, pair, length).start()

            by_level(r.level_of(slot), starts)

        def begin():
            for name in loads:
                r.copy(name, 0).start()
            start_pairs(0, range(2))

        def go_on():
            start_pairs(0, range(2, pairs))
            fill.start()
            r.copy("dfirst", 0).start()
            for slot in range(1, slots):
                for name in loads:
                    r.copy(name, slot).start()
                start_pairs(slot, range(pairs))
                r.copy("dfirst", slot).start()
            for item in ins:
                item.start()

        def grad_copy(slot):
            target = jnp.where(r.level_of(slot) % slots == 0, 0, 1)
            return pltpu.make_async_copy(
                r.dentry.at[slot], r.input_grad.at[target], r.grad_sems.at[slot]
            )

        r.at_first(begin)
        r.wait(*loads)
        r.at_first(go_on)
        attention_backward(
            r.level, r.packed, r.context, r.held.at[r.step], r.linv, r.dcontext, r.packed,
            r.step, pair_copy_of,
        )
        r.wait("dfirst")
        r.at_first(fill.wait)
        input_backward(r.packed, r.qkv.at[0], r.dfirst, r.dentry.at[r.step])
        grad_copy(r.step).start()

        def pass_on():
            for come, go in zip(ins, outs):
                come.wait()
                go.start()

        def finish():
            for slot in range(slots):
                grad_copy(slot).wait()
            for item in outs:
                item.wait()

        r.at_first(pass_on)
        r.at_last(finish)

    return call.run(body, "attn_back")


def packed_small(mats, vecs):
    width = mats[0].shape[-1]

    def kernel(*refs):
        sources, (out_mats, out_vecs) = refs[:-2], refs[-2:]
        for at in range(4):
            out_mats[at] = sources[at][0]
        out_vecs[...] = jnp.zeros_like(out_vecs)
        for at, ref in enumerate(sources[4:]):
            out_vecs[at // 4, at % 4 : at % 4 + 1, 0 : ref.shape[1]] = ref[...]

    return pl.pallas_call(
        kernel,
        out_shape=(
            jax.ShapeDtypeStruct((4, 64, width), BF),
            jax.ShapeDtypeStruct((2, 4, width), F32),
        ),
        compiler_params=pltpu.CompilerParams(vmem_limit_bytes=62 << 20),
        name="pack",
    )(*mats, *vecs)


def unpacked(quarters, member):
    width = quarters[0].shape[-1]
    matrix = jax.ShapeDtypeStruct((1, MATRIX_ROWS, width), F32)
    vector = jax.ShapeDtypeStruct((1, width), F32)
    small = jax.ShapeDtypeStruct((1, 64), F32)
    group = (matrix, small, matrix, vector, vector, vector)

    def kernel(member, *refs):
        sources, outs = refs[:4], refs[4:]

        def block(at):
            picked = sources[0][...]
            for d in (1, 2, 3):
                picked = jnp.where((member[0] ^ at) == d, sources[d][...], picked)
            return picked.astype(F32)

        for down, up, (mat_down, down_bias, mat_up, up_bias, gain, bias) in (
            (ATTN_DOWN, ATTN_UP, outs[:6]),
            (FFN_DOWN, FFN_UP, outs[6:12]),
        ):
            down, up = block(down), block(up)
            mat_down[0] = down[:MATRIX_ROWS]
            mat_up[0] = up[:MATRIX_ROWS]
            for row, target in ((UP_BIAS, up_bias), (GAIN, gain), (BIAS, bias), (DOWN_BIAS, down_bias)):
                target[...] = down[row : row + 1, : target.shape[1]]
        sums = block(ATTN_UP)[STATS : STATS + STAT_ROWS]
        means = jnp.sum(sums, axis=1, keepdims=True) / (sums[3:4, 0:1] * width)
        lane = lax.broadcasted_iota(jnp.int32, (1, 3), 1)
        picked = jnp.where(lane == 0, means[0:1], jnp.where(lane == 1, means[1:2], means[2:3]))
        outs[12][...] = jnp.sqrt(picked)

    vmem = pl.BlockSpec(memory_space=pltpu.VMEM)
    outs = pl.pallas_call(
        kernel,
        in_specs=[pl.BlockSpec(memory_space=pltpu.SMEM)] + [vmem] * 4,
        out_shape=group * 2 + (jax.ShapeDtypeStruct((1, 3), F32),),
        compiler_params=pltpu.CompilerParams(vmem_limit_bytes=SMALL_LIMIT),
        name="unpack",
    )(member.astype(jnp.int32).reshape(1), *quarters)
    outs = list(outs)
    for at in (0, 6):
        outs[at] = jnp.swapaxes(outs[at], 1, 2)
    return tuple(outs)


def swap(value):
    return lax.ppermute(value, "section", [(0, 1), (1, 0)])


def after(value, *others):
    return lax.optimization_barrier((value,) + others)[0]


def exchanged(value, bits):
    count = lax.axis_size("dp")
    return lax.ppermute(value, "dp", [(at, at ^ bits) for at in range(count)])


def summed_quarters(parts, before_last):
    mine, count = lax.axis_index("dp"), lax.axis_size("dp")
    member = mine & 3

    def quarter(d):
        first, second = (lax.dynamic_index_in_dim(v, member ^ d, 0, keepdims=False) for v in parts)
        return first + second

    def together(own, a, b, c):
        own, a, b, c = (v.astype(F32) for v in (own, a, b, c))
        return ((own + a) + (b + c)).astype(BF)

    total = together(quarter(0), *(exchanged(quarter(d), d) for d in (1, 2, 3)))
    bit = 4
    while bit < count:
        total = total + exchanged(total, bit)
        bit *= 2
    total = after(total, before_last)
    return [total] + [exchanged(total, d) for d in (1, 2, 3)], member


def body(
    tokens, valid, cotangent, qkv, out, win, wout,
    attn_down, attn_down_bias, attn_up, attn_up_bias, gain1, bias1,
    ffn_down, ffn_down_bias, ffn_up, ffn_up_bias, gain2, bias2,
):
    section = lax.axis_index("section")
    micro_count, rows, width = tokens.shape
    sizes = (rows, width, win.shape[-1])
    slots = micro_count // 2
    mats, vecs = packed_small(
        (jnp.swapaxes(attn_down, 1, 2), attn_up, jnp.swapaxes(ffn_down, 1, 2), ffn_up),
        (attn_down_bias, attn_up_bias, gain1, bias1, ffn_down_bias, ffn_up_bias, gain2, bias2),
    )
    own = Layer(qkv, out, win, wout, mats, vecs)
    early = [swap(v) for v in (qkv, out, mats, vecs)]
    got_qkv, got_out, got_mats, got_vecs = early
    got_win, got_wout = (swap(after(v, *early)) for v in (win, wout))
    got = Layer(got_qkv, got_out, got_win, got_wout, got_mats, got_vecs)
    where = section.astype(jnp.int32).reshape(1)

    kept = first_attn_forward(where, tokens, valid, own, got, sizes, slots)
    back = middle_part(where, kept, cotangent, valid, own, got, sizes, slots)

    got_grads = swap(back.send)
    there = swap(after(back.result, got_grads))
    quarters, member = summed_quarters((back.keep, got_grads), there)
    last = first_attn_backward(where, back, there, kept, own, got, sizes, slots)
    small = unpacked([quarters[0]] + [after(v, last.input_grad) for v in quarters[1:]], member)
    return (last.result, last.input_grad) + small


def solution(mesh):
    rows = P(None, "dp", None)
    matrix, vector = P("section", None, None), P("section", None)
    weights = (matrix, vector, matrix, vector, vector, vector)
    return jax.shard_map(
        body,
        mesh=mesh,
        in_specs=(rows, P(None, "dp"), rows) + (matrix,) * 4 + weights * 2,
        out_specs=(rows, P("section", "dp", None)) + weights * 2 + (vector,),
        check_vma=False,
    )
```
